32 devices in a mesh: dp: 8 (over z, y), mp: 4 (over x, core).
Axes of the slice: x: 2, y: 2, z: 4, core: 2. Of those that a mesh axis runs over, the one named last changes fastest.
Arguments:
- patches: bfloat16 [384, 50176], P('mp', 'dp'), may hold values from -6 to 6
- keep_mask: int32 [256, 196], P('dp'), may hold values from 0 to 1, as said below
- ln1_gain: bfloat16 [384], P('mp'), may hold values from 0.25 to 1.75
- ln1_bias: bfloat16 [384], P('mp'), may hold values from -3 to 3
- w_qkv: bfloat16 [384, 1152], P('mp'), may hold values from -0.3125 to 0.3125
- q_bias: bfloat16 [384], P('mp'), may hold values from -3 to 3
- v_bias: bfloat16 [384], P('mp'), may hold values from -3 to 3
- mix_pre: float32 [8, 8], replicated, may hold values from -3 to 3
- mix_post: float32 [8, 8], replicated, may hold values from -3 to 3
- w_proj: bfloat16 [384, 384], P('mp'), may hold values from -1.5 to 1.5
- proj_bias: bfloat16 [384], P('mp'), may hold values from -3 to 3
- gamma1: bfloat16 [384], P('mp'), may hold values from 0.25 to 1.75
- ln2_gain: bfloat16 [384], P('mp'), may hold values from 0.25 to 1.75
- ln2_bias: bfloat16 [384], P('mp'), may hold values from -3 to 3
- w_fc1: bfloat16 [384, 1536], P('mp'), may hold values from -0.3125 to 0.3125
- fc1_bias: bfloat16 [1536], P('mp'), may hold values from -3 to 3
- w_fc2: bfloat16 [1536, 384], P('mp'), may hold values from -0.15625 to 0.15625
- fc2_bias: bfloat16 [384], P('mp'), may hold values from -3 to 3
- gamma2: bfloat16 [384], P('mp'), may hold values from 0.25 to 1.75
- cotangent: bfloat16 [384, 50176], P('mp', 'dp'), may hold values from -6 to 6
Outputs:
- output: bfloat16 [384, 50176], P('mp', 'dp')
- input_grad: bfloat16 [384, 50176], P('mp', 'dp')
- ln1_gain_grad: float32 [384], P('mp')
- ln1_bias_grad: float32 [384], P('mp')
- w_qkv_grad: float32 [384, 1152], P('mp')
- q_bias_grad: float32 [384], P('mp')
- v_bias_grad: float32 [384], P('mp')
- mix_pre_grad: float32 [8, 8], replicated
- mix_post_grad: float32 [8, 8], replicated
- w_proj_grad: float32 [384, 384], P('mp')
- proj_bias_grad: float32 [384], P('mp')
- gamma1_grad: float32 [384], P('mp')
- ln2_gain_grad: float32 [384], P('mp')
- ln2_bias_grad: float32 [384], P('mp')
- w_fc1_grad: float32 [384, 1536], P('mp')
- fc1_bias_grad: float32 [1536], P('mp')
- w_fc2_grad: float32 [1536, 384], P('mp')
- fc2_bias_grad: float32 [384], P('mp')
- gamma2_grad: float32 [384], P('mp')
The draws below stay inside these ranges and needn't reach their ends.
Inputs may be any that keep to these rules, and one draw needn't show every extreme that they name: `keep_mask`: entry 0 of every image is 1; the share of kept patches differs from image to image.
All inputs are finite; a program needn't handle non-finite values.
Results may differ from the reference program's by a relative error of at most 0.019.
Values may be sent and summed in bfloat16 or wider, within the bound.
A program may use at most 128 MiB of HBM per device.

```python
import math
import jax
import jax.numpy as jnp
from jax import lax

D = 384
HEADS = 8
FF = 1536
PATCHES = 196
IMAGES = 256


def draw_keep_mask(key, part):
    key = jax.random.fold_in(key, 11)
    rate_key, cell_key = jax.random.split(key)
    keep_rate = jax.random.randint(rate_key, (IMAGES, 1), 1, 9)
    cell_draw = jax.random.randint(cell_key, (IMAGES, PATCHES), 0, 8)
    leading = (jnp.arange(PATCHES) == 0)[None, :]
    return jnp.where((cell_draw < keep_rate) | leading, 1, 0).astype(jnp.int32)


def level_of(key, extent, shards, low, top_value):
    def one(axis_at, parts):
        draws = jax.random.uniform(jax.random.fold_in(jax.random.fold_in(key, 6), axis_at), (parts,), jnp.float32, low / len(shards), top_value / len(shards))
        return jnp.repeat(jnp.exp(draws), extent[axis_at] // parts).reshape((-1,) + (1,) * (len(extent) - axis_at - 1))

    level = one(*shards[0])
    for cut in shards[1:]:
        level = level * one(*cut)
    return level


def normal_values(key, shape, spread, bound, cuts=(), kind=jnp.bfloat16):
    entries = spread * jax.random.normal(key, shape, jnp.float32)
    if cuts:
        entries = entries * level_of(key, shape, cuts, -0.22, 0.18)
    return jnp.clip(entries, -bound, bound).astype(kind)


def setup_inputs(seed: int = 0) -> dict:
    key_of = jax.random.split(jax.random.key(seed), 21)
    patches = normal_values(key_of[0], (D, IMAGES * PATCHES), 1.0, 6.0, ((0, 4), (1, 8)))
    keep_mask = draw_keep_mask(jax.random.fold_in(key_of[20], 71), 0)
    ln1_gain = jnp.clip(1.0 + 0.15 * jax.random.normal(key_of[2], (D,), jnp.float32), 0.25, 1.75).astype(jnp.bfloat16)
    ln1_bias = normal_values(key_of[3], (D,), 0.5, 3.0, ((0, 4),))
    w_qkv = normal_values(key_of[4], (D, 3 * D), D ** -0.5, 0.3125, ((0, 4),))
    q_bias = normal_values(key_of[5], (D,), 0.5, 3.0, ((0, 4),))
    v_bias = normal_values(key_of[6], (D,), 0.5, 3.0, ((0, 4),))
    mix_pre = normal_values(key_of[7], (HEADS, HEADS), 0.5, 3.0, (), jnp.float32)
    mix_post = normal_values(key_of[8], (HEADS, HEADS), 0.5, 3.0, (), jnp.float32)
    w_proj = normal_values(key_of[9], (D, D), (max(D // 24, 8)) ** -0.5, 1.5, ((0, 4),))
    proj_bias = normal_values(key_of[10], (D,), 0.5, 3.0, ((0, 4),))
    gamma1 = jnp.clip(1.0 + 0.15 * jax.random.normal(key_of[11], (D,), jnp.float32), 0.25, 1.75).astype(jnp.bfloat16)
    ln2_gain = jnp.clip(1.0 + 0.15 * jax.random.normal(key_of[12], (D,), jnp.float32), 0.25, 1.75).astype(jnp.bfloat16)
    ln2_bias = normal_values(key_of[13], (D,), 0.5, 3.0, ((0, 4),))
    w_fc1 = normal_values(key_of[14], (D, FF), D ** -0.5, 0.3125, ((0, 4),))
    fc1_bias = normal_values(key_of[15], (FF,), 0.5, 3.0, ((0, 4),))
    w_fc2 = normal_values(key_of[16], (FF, D), FF ** -0.5, 0.15625, ((0, 4),))
    fc2_bias = normal_values(key_of[17], (D,), 0.5, 3.0, ((0, 4),))
    gamma2 = jnp.clip(1.0 + 0.15 * jax.random.normal(key_of[18], (D,), jnp.float32), 0.25, 1.75).astype(jnp.bfloat16)
    cotangent = normal_values(key_of[19], (D, IMAGES * PATCHES), 1.0, 6.0, ((0, 4), (1, 8)))
    return dict(patches=patches, keep_mask=keep_mask, ln1_gain=ln1_gain, ln1_bias=ln1_bias, w_qkv=w_qkv, q_bias=q_bias, v_bias=v_bias, mix_pre=mix_pre, mix_post=mix_post, w_proj=w_proj, proj_bias=proj_bias, gamma1=gamma1, ln2_gain=ln2_gain, ln2_bias=ln2_bias, w_fc1=w_fc1, fc1_bias=fc1_bias, w_fc2=w_fc2, fc2_bias=fc2_bias, gamma2=gamma2, cotangent=cotangent)


EPSILON = 1e-06
MASKED = -1000000000.0
HIGHEST = lax.Precision.HIGHEST

@jax.custom_vjp
def low(v):
    return lax.optimization_barrier(v.astype(jnp.bfloat16)).astype(jnp.float32)

@jax.custom_vjp
def low_back(v):
    return v

def low_keep(v):
    return (low(v), None)

def low_pass(kept, grad):
    return (grad,)

def back_keep(v):
    return (v, None)

def back_low(kept, grad):
    return (low(grad),)
low.defvjp(low_keep, low_pass)
low_back.defvjp(back_keep, back_low)

def normalize(values, gain, shift):
    centred = values - lax.optimization_barrier(jnp.mean(values, axis=-1, keepdims=True))
    return centred * lax.rsqrt(lax.optimization_barrier(jnp.mean(centred * centred, axis=-1, keepdims=True)) + EPSILON) * gain + shift

def layer(params, inputs, keep_block):
    ln1_gain, ln1_bias, w_qkv, q_bias, v_bias, mix_pre, mix_post, w_proj, proj_bias, gamma1, ln2_gain, ln2_bias, w_fc1, fc1_bias, w_fc2, fc2_bias, gamma2 = params
    images, length, channels = inputs.shape
    head_count = mix_pre.shape[0]
    head_size = channels // head_count
    flat_rows = inputs.reshape(images * length, channels)
    first_in = low(normalize(flat_rows, ln1_gain, ln1_bias))
    joined = jnp.dot(first_in, w_qkv, precision=HIGHEST)
    shaped = (images, length, head_count, head_size)
    queries = low_back(low(joined[:, :channels] + q_bias)).reshape(shaped)
    key_vectors = low_back(low(joined[:, channels:2 * channels])).reshape(shaped)
    values = low_back(low(joined[:, 2 * channels:] + v_bias)).reshape(shaped)
    scores = low_back(jnp.einsum('bihe,bjhe->bhij', queries, key_vectors, precision=HIGHEST) * head_size ** (-0.5))
    logits = jnp.where(keep_block[:, None, None, :] > 0, jnp.einsum('hg,bgij->bhij', mix_pre, scores, precision=HIGHEST), MASKED)
    exponent = jnp.exp(logits - lax.optimization_barrier(jnp.max(logits, axis=-1, keepdims=True)))
    softened = exponent / lax.optimization_barrier(jnp.sum(exponent, axis=-1, keepdims=True))
    mixed_probs = low(jnp.einsum('hg,bgij->bhij', mix_post, softened, precision=HIGHEST))
    attended = jnp.einsum('bhij,bjhe->bihe', mixed_probs, values, precision=HIGHEST)
    attended = low_back(low(attended.reshape(images * length, channels)))
    branch = low_back(jnp.dot(attended, w_proj, precision=HIGHEST) + proj_bias)
    middle = flat_rows + gamma1 * branch
    second = low(normalize(middle, ln2_gain, ln2_bias))
    hidden = low_back(jnp.dot(second, w_fc1, precision=HIGHEST) + fc1_bias)
    active = low_back(low(jax.nn.gelu(hidden, approximate=False)))
    mlp_out = low_back(jnp.dot(active, w_fc2, precision=HIGHEST) + fc2_bias)
    return (middle + gamma2 * mlp_out).reshape(images, length, channels)

def reference(patches, keep_mask, ln1_gain, ln1_bias, w_qkv, q_bias, v_bias, mix_pre, mix_post, w_proj, proj_bias, gamma1, ln2_gain, ln2_bias, w_fc1, fc1_bias, w_fc2, fc2_bias, gamma2, cotangent):
    params = tuple((weight.astype(jnp.float32) for weight in (ln1_gain, ln1_bias, w_qkv, q_bias, v_bias, mix_pre, mix_post, w_proj, proj_bias, gamma1, ln2_gain, ln2_bias, w_fc1, fc1_bias, w_fc2, fc2_bias, gamma2)))
    per_step = math.gcd(IMAGES, 16)
    step_count = IMAGES // per_step
    inputs = patches.astype(jnp.float32).T.reshape(step_count, per_step, PATCHES, D)
    keep_steps = keep_mask.reshape(step_count, per_step, PATCHES)
    grads_in = cotangent.astype(jnp.float32).T.reshape(step_count, per_step, PATCHES, D)

    def advance(totals, portion):
        inputs_now, keep_now, grad_now = portion
        outputs, pullback = jax.vjp(lambda weights, tensor: layer(weights, tensor, keep_now), params, inputs_now)
        weight_grads, input_grad = pullback(grad_now)
        totals = jax.tree.map(lambda left_side, right_side: left_side + right_side, totals, weight_grads)
        return (totals, (outputs.astype(jnp.bfloat16), input_grad.astype(jnp.bfloat16)))
    initial = jax.tree.map(jnp.zeros_like, params)
    totals, (outputs, input_grads) = lax.scan(advance, initial, (inputs, keep_steps, grads_in))
    return (outputs.reshape(IMAGES * PATCHES, D).T, input_grads.reshape(IMAGES * PATCHES, D).T, totals[0], totals[1], totals[2], totals[3], totals[4], totals[5], totals[6], totals[7], totals[8], totals[9], totals[10], totals[11], totals[12], totals[13], totals[14], totals[15], totals[16])
```

```python
import functools
import jax
import jax.numpy as jnp
from jax import lax
from jax.experimental import pallas as pl
from jax.experimental.pallas import tpu as pltpu
from jax.sharding import PartitionSpec as P

PATCHES = 196
HEADS = 8
EPSILON = 1e-06
MASKED = -1000000000.0
F32 = jnp.float32
BF16 = jnp.bfloat16
LANES = 256
KEYS = 208


def dot(a, b):
    return lax.dot_general(a, b, (((1,), (0,)), ((), ())), preferred_element_type=F32)


def dot_nt(a, b):
    return lax.dot_general(a, b, (((1,), (1,)), ((), ())), preferred_element_type=F32)


def twice(col):
    return jnp.concatenate([col, col], axis=1)


def fold(v):
    return v[:, :128] + v[:, 128:]


def lane_column(row):
    return jnp.transpose(jnp.broadcast_to(row, (128, row.shape[1])))


def gelu_parts(h):
    e = jnp.exp(-0.5 * h * h)
    cum = 0.5 * (1.0 + lax.erf(h * 0.7071067811865476))
    return cum, cum + h * (e * 0.3989422804014327)


def layout(C, FF):
    names = ["g1", "b1", "qb", "vb", "pb", "s1", "g2", "b2", "fb2", "s2", "fb1"]
    off, at = {}, 0
    for n in names:
        w = FF if n == "fb1" else C
        off[n] = (at, w)
        at += w
    return off, at


def core_kernel(n_img, C, FF, phases, *refs):
    (x_ref, c_ref, mask_ref, prow_ref, mrow_ref, wqkv_ref, wproj_ref, wfc1_ref, wfc2_ref,
     wqkvT_ref, wprojT_ref, wfc1T_ref, wfc2T_ref,
     out_ref, ig_ref, dqkv_ref, dproj_ref, dfc1_ref, dfc2_ref, dvec_ref, dmix_ref,
     first_s, qkv_s, p_s, a_s, da_s, gm_s, gt_s, vmixT_s, col_s, mcol_s, kmix_s, act_s, slope_s, gh_s, mid_s) = refs
    off, total = layout(C, FF)
    hd = C // HEADS
    inv_c = 1.0 / C

    def col(name, lo=0, hi=None):
        o, w = off[name]
        hi = w if hi is None else hi
        return twice(col_s[o + lo:o + hi, :])

    for i in range(0, total, 384):
        col_s[i:i + 384, :] = lane_column(prow_ref[:, i:i + 384])
    for h in range(2 * HEADS):
        mcol_s[h] = lane_column(mrow_ref[h:h + 1, :])
    p_s[...] = jnp.zeros_like(p_s)
    gt_s[...] = jnp.zeros_like(gt_s)
    for r in (dqkv_ref, dproj_ref, dfc1_ref, dfc2_ref, dvec_ref, dmix_ref):
        r[...] = jnp.zeros_like(r)

    lane = lax.broadcasted_iota(jnp.int32, (C, LANES), 1)

    def lanes_of(b):
        return pl.ds(pl.multiple_of(b * LANES, LANES), LANES)

    def norm(x):
        mean = jnp.sum(x, axis=0, keepdims=True) * inv_c
        d = x - mean
        inv = lax.rsqrt(jnp.sum(d * d, axis=0, keepdims=True) * inv_c + EPSILON)
        return d * inv, inv

    def norm_back(u, n, inv, g):
        s = u * g
        m1 = jnp.sum(s, axis=0, keepdims=True) * inv_c
        m2 = jnp.sum(s * n, axis=0, keepdims=True) * inv_c
        return inv * (s - m1 - n * m2)

    def add_vec(name, v, lo=0):
        o, _ = off[name]
        o += lo
        dvec_ref[o:o + v.shape[0], :] += fold(v)

    def phase_a(b, _):
        at = lanes_of(b)
        x = x_ref[:, at].astype(F32)
        n1, _inv = norm(x)
        first = (n1 * col("g1") + col("b1")).astype(BF16)
        first_s[:, at] = first
        q = (dot(wqkvT_ref[0:C, :], first) + col("qb")).astype(BF16)
        qkv_s[0:C, at] = q
        k = dot(wqkvT_ref[C:2 * C, :], first).astype(BF16)
        qkv_s[C:2 * C, at] = k
        v = (dot(wqkvT_ref[2 * C:3 * C, :], first) + col("vb")).astype(BF16)
        qkv_s[2 * C:3 * C, at] = v
        mcolm = lane_column(mask_ref[pl.ds(b, 1), :])[:KEYS]
        maskc = twice(mcolm)
        kr = jnp.transpose(k.astype(F32))[:KEYS]
        for h in range(HEADS):
            kmix = (kr * mrow_ref[h:h + 1, :]).astype(BF16)
            logit = dot(kmix, q) + maskc
            top = jnp.max(logit, axis=0, keepdims=True)
            e = jnp.exp(logit - top)
            inv = 1.0 / jnp.sum(e, axis=0, keepdims=True)
            p_s[b, h * LANES:h * LANES + KEYS, :] = (e * inv).astype(BF16)
            vmixT_s[:, h * LANES:(h + 1) * LANES] = (v.astype(F32) * twice(mcol_s[HEADS + h])).astype(BF16)
        a_s[:, at] = dot(vmixT_s[...], p_s[b]).astype(BF16)
        return 0

    def phase_b(b, _):
        at = lanes_of(b)
        x = x_ref[:, at].astype(F32)
        att = a_s[:, at]
        branch = dot(wprojT_ref[...], att) + col("pb")
        middle = x + col("s1") * branch
        n2, inv2 = norm(middle)
        second = (n2 * col("g2") + col("b2")).astype(BF16)
        step = 128
        for r in range(0, FF, step):
            hid = dot(wfc1T_ref[r:r + step, :], second) + col("fb1", r, r + step)
            cum, slope = gelu_parts(hid)
            act_s[r:r + step, :] = (hid * cum).astype(BF16)
            slope_s[r:r + step, :] = slope
        act = act_s[...]
        mlp = dot(wfc2T_ref[...], act) + col("fb2")
        cot = c_ref[:, at].astype(F32)
        out_ref[:, at] = (middle + col("s2") * mlp).astype(BF16)
        add_vec("s2", cot * mlp)
        g_mlp = (col("s2") * cot).astype(BF16)
        add_vec("fb2", g_mlp.astype(F32))
        for r in range(0, FF, step):
            g_act = dot(wfc2_ref[r:r + step, :], g_mlp)
            gh = (g_act * slope_s[r:r + step, :]).astype(BF16)
            gh_s[r:r + step, :] = gh
            add_vec("fb1", gh.astype(F32), r)
            dfc2_ref[r:r + step, :] += dot_nt(act_s[r:r + step, :], g_mlp)
        gh = gh_s[...]
        dfc1_ref[...] += dot_nt(second, gh)
        g_second = dot(wfc1_ref[...], gh)
        add_vec("g2", g_second * n2)
        add_vec("b2", g_second)
        g_mid = cot + norm_back(g_second, n2, inv2, col("g2"))
        gm_s[:, at] = g_mid
        add_vec("s1", g_mid * branch)
        g_br = (col("s1") * g_mid).astype(BF16)
        add_vec("pb", g_br.astype(F32))
        dproj_ref[...] += dot_nt(att, g_br)
        da_s[:, at] = dot(wproj_ref[...], g_br).astype(BF16)
        return 0

    def phase_c(b, _):
        at = lanes_of(b)
        da = da_s[:, at]
        q = qkv_s[0:C, at]
        kT = qkv_s[C:2 * C, at].astype(F32)
        vT = qkv_s[2 * C:3 * C, at].astype(F32)
        kr = jnp.transpose(kT)[:KEYS]
        vr = jnp.transpose(vT)[:KEYS]
        gv = jnp.zeros((KEYS, C), F32)
        gk = jnp.zeros((KEYS, C), F32)
        for h in range(HEADS):
            prow = mrow_ref[HEADS + h:HEADS + h + 1, :]
            mrow = mrow_ref[h:h + 1, :]
            vmix = (vr * prow).astype(BF16)
            gs = dot(vmix, da)
            pb16 = p_s[b, h * LANES:h * LANES + KEYS, :]
            p = pb16.astype(F32)
            d = jnp.sum(gs * p, axis=0, keepdims=True)
            gt = (p * (gs - d)).astype(BF16)
            gt_s[h * LANES:h * LANES + KEYS, :] = gt
            w = dot_nt(pb16, da)
            gv = gv + prow * w
            dmix_ref[HEADS + h:HEADS + h + 1, :] += jnp.sum(w * vr, axis=0, keepdims=True)
            xk = dot_nt(gt, q)
            gk = gk + mrow * xk
            dmix_ref[h:h + 1, :] += jnp.sum(xk * kr, axis=0, keepdims=True)
            vmixT_s[:, h * LANES:(h + 1) * LANES] = (kT * twice(mcol_s[h])).astype(BF16)
        gq = dot(vmixT_s[...], gt_s[...]).astype(BF16)
        pad = jnp.zeros((LANES - KEYS, C), F32)
        gkT = jnp.transpose(jnp.concatenate([gk, pad], axis=0)).astype(BF16)
        gvT = jnp.transpose(jnp.concatenate([gv, pad], axis=0)).astype(BF16)
        add_vec("qb", gq.astype(F32))
        add_vec("vb", gvT.astype(F32))
        gj = jnp.concatenate([gq, gkT, gvT], axis=0)
        first = first_s[:, at]
        dqkv_ref[...] += dot_nt(first, gj)
        g_first = dot(wqkv_ref[...], gj)
        n1, inv1 = norm(x_ref[:, at].astype(F32))
        add_vec("g1", g_first * n1)
        add_vec("b1", g_first)
        ig_ref[:, at] = (gm_s[:, at] + norm_back(g_first, n1, inv1, col("g1"))).astype(BF16)
        return 0

    if "a" in phases:
        lax.fori_loop(0, n_img, phase_a, 0)
    if "b" in phases:
        lax.fori_loop(0, n_img, phase_b, 0)
    if "c" in phases:
        lax.fori_loop(0, n_img, phase_c, 0)


def core_call(n_img, C, FF, args, phases="abc"):
    off, total = layout(C, FF)
    S = jax.ShapeDtypeStruct
    T = n_img * LANES
    outs = (S((C, T), BF16), S((C, T), BF16), S((C, 3 * C), F32), S((C, C), F32), S((C, FF), F32), S((FF, C), F32),
            S((total, 128), F32), S((2 * HEADS, C), F32))
    V = pltpu.VMEM
    scratch = [V((C, T), BF16), V((3 * C, T), BF16), V((n_img, HEADS * LANES, LANES), BF16), V((C, T), BF16),
               V((C, T), BF16), V((C, T), F32), V((HEADS * LANES, LANES), BF16), V((C, HEADS * LANES), BF16),
               V((total, 128), F32), V((2 * HEADS, C, 128), F32), V((HEADS * KEYS, C), BF16),
               V((FF, LANES), BF16), V((FF, LANES), F32), V((FF, LANES), BF16), V((C, LANES), F32)]
    vm = pl.BlockSpec(memory_space=pltpu.VMEM)
    return pl.pallas_call(
        functools.partial(core_kernel, n_img, C, FF, phases),
        out_shape=outs,
        in_specs=[vm] * len(args),
        out_specs=[vm] * len(outs),
        scratch_shapes=scratch,
        compiler_params=pltpu.CompilerParams(vmem_limit_bytes=63 * 2 ** 20),
        name="layer_core",
    )(*args)


PARAMS = ("ln1_gain", "ln1_bias", "q_bias", "v_bias", "proj_bias", "gamma1", "ln2_gain", "ln2_bias",
          "fc2_bias", "gamma2")


def local(patches, keep_mask, ln1_gain, ln1_bias, w_qkv, q_bias, v_bias, mix_pre, mix_post, w_proj, proj_bias,
          gamma1, ln2_gain, ln2_bias, w_fc1, fc1_bias, w_fc2, fc2_bias, gamma2, cotangent):
    n_mp = lax.axis_size("mp")
    CS = patches.shape[0]
    C = CS * n_mp
    FF = w_fc2.shape[0] * n_mp
    n_img = keep_mask.shape[0] // n_mp
    factor = (C // HEADS) ** (-0.5)

    def spread(a):
        a = lax.all_to_all(a, "mp", split_axis=1, concat_axis=0, tiled=True)
        a = a.reshape(C, n_img, PATCHES)
        return jnp.pad(a, ((0, 0), (0, 0), (0, LANES - PATCHES))).reshape(C, n_img * LANES)

    gather = lambda a: lax.all_gather(a, "mp", axis=0, tiled=True)
    x, cot = spread(patches), spread(cotangent)
    vecs = [ln1_gain, ln1_bias, q_bias, v_bias, proj_bias, gamma1, ln2_gain, ln2_bias, fc2_bias, gamma2]
    allv = lax.all_gather(jnp.concatenate(vecs + [fc1_bias]), "mp", axis=0)
    small = allv[:, :10 * CS].reshape(n_mp, 10, CS).transpose(1, 0, 2).reshape(1, 10 * C)
    prow = jnp.concatenate([small, allv[:, 10 * CS:].reshape(1, FF)], axis=1).astype(F32)
    ws = [gather(w_qkv), gather(w_proj), gather(w_fc1), gather(w_fc2)]
    wts = [w.T for w in ws]
    offset = lax.axis_index("mp") * n_img
    keep = lax.dynamic_slice_in_dim(keep_mask, offset, n_img, 0)
    mask = jnp.pad(jnp.where(keep > 0, 0.0, MASKED).astype(F32), ((0, 0), (0, LANES - PATCHES)),
                   constant_values=MASKED)
    hd = C // HEADS
    mrow = jnp.concatenate([jnp.repeat(mix_pre, hd, axis=1) * factor, jnp.repeat(mix_post.T, hd, axis=1)], 0)
    out, ig, dqkv, dproj, dfc1, dfc2, dvec, dmix = core_call(n_img, C, FF, [x, cot, mask, prow, mrow] + ws + wts)

    def collect(a):
        a = a.reshape(C, n_img, LANES)[:, :, :PATCHES].reshape(C, n_img * PATCHES)
        return lax.all_to_all(a, "mp", split_axis=0, concat_axis=1, tiled=True)

    out_shard, grad_shard = collect(out), collect(ig)
    dm = jnp.sum(dmix.reshape(2, HEADS, HEADS, hd), axis=3)
    pre_total, post_total = lax.psum((dm[0] * factor, dm[1].T), ("dp", "mp"))
    dv = jnp.sum(dvec, axis=1)
    dsmall = dv[:10 * C].reshape(10, n_mp, CS).transpose(1, 0, 2).reshape(n_mp, 10 * CS)
    pieces = [dqkv.reshape(n_mp, -1), dproj.reshape(n_mp, -1), dfc1.reshape(n_mp, -1), dfc2.reshape(n_mp, -1),
              dsmall, dv[10 * C:].reshape(n_mp, -1)]
    packed = jnp.concatenate([p.astype(BF16) for p in pieces], axis=1)
    own = lax.psum_scatter(packed, "mp", scatter_dimension=0, tiled=True)
    own = lax.psum(own, "dp")[0].astype(F32)
    res, at = [], 0
    for shape in ((CS, 3 * C), (CS, C), (CS, FF), (FF // n_mp, C), (10, CS), (FF // n_mp,)):
        size = 1
        for s in shape:
            size *= s
        res.append(own[at:at + size].reshape(shape))
        at += size
    gqkv, gproj, gfc1, gfc2, gs, gfb1 = res
    return (out_shard, grad_shard, gs[0], gs[1], gqkv, gs[2], gs[3], pre_total, post_total, gproj, gs[4], gs[5],
            gs[6], gs[7], gfc1, gfb1, gfc2, gs[8], gs[9])


def solution(mesh):
    m, mn = P("mp"), P("mp", None)
    big = P("mp", "dp")
    in_specs = (big, P("dp", None), m, m, mn, m, m, P(), P(), mn, m, m, m, m, mn, m, mn, m, m, big)
    out_specs = (big, big, m, m, mn, m, m, P(), P(), mn, m, m, m, m, mn, m, mn, m, m)
    return jax.shard_map(local, mesh=mesh, in_specs=in_specs, out_specs=out_specs, check_vma=False)
```

```python
import functools
import jax
import jax.numpy as jnp
from jax import lax
from jax.experimental import pallas as pl
from jax.experimental.pallas import tpu as pltpu
from jax.sharding import PartitionSpec as P

PATCHES = 196
HEADS = 8
EPSILON = 1e-06
MASKED = -1000000000.0
F32 = jnp.float32
BF16 = jnp.bfloat16
LANES = 256
KEYS = 208


def dot(a, b):
    return lax.dot_general(a, b, (((1,), (0,)), ((), ())), preferred_element_type=F32)


def dot_nt(a, b):
    return lax.dot_general(a, b, (((1,), (1,)), ((), ())), preferred_element_type=F32)


def twice(col):
    return jnp.concatenate([col, col], axis=1)


def fold(v):
    return v[:, :128] + v[:, 128:]


def lane_column(row):
    return jnp.transpose(jnp.broadcast_to(row, (128, row.shape[1])))


def gelu_parts(h):
    e = jnp.exp(-0.5 * h * h)
    cum = 0.5 * (1.0 + lax.erf(h * 0.7071067811865476))
    return cum, cum + h * (e * 0.3989422804014327)


MESH = pl.DeviceIdType.MESH
TILE = 128
VECS = ("g1", "b1", "qb", "vb", "pb", "s1", "g2", "b2", "fb2", "s2")


class Plan:
    def __init__(self, n_mp, patches, keep_mask, w_fc2):
        self.n_mp = n_mp
        self.nx = n_mp // 2
        self.CS, self.cols = patches
        self.C = self.CS * n_mp
        self.FFS = w_fc2[0]
        self.FF = self.FFS * n_mp
        self.n_img = keep_mask[0] // n_mp
        self.tok = self.n_img * PATCHES
        starts = [self.tok * m for m in range(n_mp)]
        self.bases = [s // TILE * TILE for s in starts]
        self.shifts = [s % TILE for s in starts]
        top = max(self.shifts)
        self.width = -(-(self.tok + top) // TILE) * TILE
        self.wide = self.width + TILE
        self.pairs = self.n_img // 2
        self.in_cuts = [0] + [-(-(2 * PATCHES * (k + 1) + top) // TILE) * TILE for k in range(self.pairs)]
        self.out_cuts = [0] + [2 * PATCHES * (k + 1) // TILE * TILE for k in range(self.pairs - 1)] + [self.width]
        self.vrows = len(VECS) + self.FFS // self.CS
        self.off = {}
        at = 0
        for name in VECS + ("fb1",):
            w = self.FF if name == "fb1" else self.C
            self.off[name] = (at, w)
            at += w
        self.total = at


def layer_kernel(pn, x_hbm, c_hbm, wqkv_hbm, wproj_hbm, wfc1_hbm, wfc2_hbm, mask_ref, pvec_ref, mrow_ref,
                 out_ref, ig_ref, dqkv_ref, dproj_ref, dfc1_ref, dfc2_ref, dvec_ref, dmix_ref,
                 xw_s, cw_s, pv_s, wqkv_s, wproj_s, wfc1_s, wfc2_s, wqkvT_s, wprojT_s, wfc1T_s, wfc2T_s,
                 ow_s, iw_s, orecv_s, irecv_s,
                 x_s, first_s, qkv_s, p_s, a_s, gm_s, gt_s, vmixT_s, col_s, mcol_s, act_s, slope_s, gh_s,
                 ssem, rsem, lsem):
    C, CS, FF, n_img, n_mp, nx = pn.C, pn.CS, pn.FF, pn.n_img, pn.n_mp, pn.nx
    inv_c = 1.0 / C
    me = lax.axis_index("mp")
    core = me % 2
    xi = me // 2
    sibling = me + 1 - 2 * core
    my_shift = (pn.tok * me) % TILE

    count = [0, 0]
    sent = []

    def remote(src, dst, dev):
        i = count[0]
        count[0] += 1
        copy = pltpu.make_async_remote_copy(src_ref=src, dst_ref=dst, send_sem=ssem.at[i], recv_sem=rsem.at[i],
                                            device_id={"mp": dev}, device_id_type=MESH)
        sent.append(copy)
        return copy

    def local_copy(src, dst):
        i = count[1]
        count[1] += 1
        return pltpu.make_async_copy(src, dst, lsem.at[i])

    def peer(d):
        return (me + d) % n_mp

    def aligned(v, n):
        return pl.multiple_of(v, n)

    def window(src, dst, k):
        lo, hi = pn.in_cuts[k], pn.in_cuts[k + 1]
        mine = dst.at[pl.ds(aligned(me * CS, CS), CS), pl.ds(lo, hi - lo)]

        def part(m):
            base = (pn.tok * m) // TILE * TILE
            return src.at[:, pl.ds(aligned(base + lo, TILE), hi - lo)]

        return [local_copy(part(me), mine)] + [remote(part(peer(d)), mine, peer(d)) for d in range(1, n_mp)]

    x_parts = [window(x_hbm, xw_s, k) for k in range(pn.pairs)]
    c_parts = [window(c_hbm, cw_s, k) for k in range(pn.pairs)]
    vec_parts = [local_copy(pvec_ref, pv_s.at[me])]
    vec_parts += [remote(pvec_ref, pv_s.at[me], peer(d)) for d in range(1, n_mp)]

    def weight(src, dst):
        rows = src.shape[0]

        def shard(m):
            return dst.at[pl.ds(aligned(m * rows, rows), rows), :]

        own = local_copy(src, shard(me))
        across = [remote(src, shard(me), ((xi + d) % nx) * 2 + core) for d in range(1, nx)]
        beside = remote(src, shard(me), sibling)
        relay = []
        for d in range(1, nx):
            s = shard(((xi + nx - d) % nx) * 2 + core)
            relay.append(remote(s, s, sibling))
        return own, across, beside, relay

    w_parts = [weight(s, d) for s, d in ((wqkv_hbm, wqkv_s), (wproj_hbm, wproj_s), (wfc1_hbm, wfc1_s),
                                         (wfc2_hbm, wfc2_s))]

    def result(src, dst, k):
        lo, hi = pn.out_cuts[k], pn.out_cuts[k + 1]
        there = dst.at[me, :, pl.ds(lo, hi - lo)]

        def part(m):
            return src.at[pl.ds(aligned(m * CS, CS), CS), pl.ds(lo, hi - lo)]

        return [local_copy(part(me), there)] + [remote(part(peer(d)), there, peer(d)) for d in range(1, n_mp)]

    o_parts = [result(ow_s, orecv_s, k) for k in range(pn.pairs)]
    i_parts = [result(iw_s, irecv_s, k) for k in range(pn.pairs)]

    def start(copies):
        for c in copies:
            c.start()

    def arrive(copies):
        copies[0].wait()
        for c in copies[1:]:
            c.wait_recv()

    def start_weight(w):
        own, across, beside, _ = w
        own.start()
        start(across)
        beside.start()

    def relay_weight(w):
        _, across, _, relay = w
        for a, r in zip(across, relay):
            a.wait_recv()
            r.start()

    def have_weight(w):
        own, _, beside, relay = w
        own.wait()
        beside.wait_recv()
        for r in relay:
            r.wait_recv()

    barrier = pltpu.get_barrier_semaphore()
    for d in range(1, n_mp):
        pl.semaphore_signal(barrier, inc=1, device_id={"mp": peer(d)}, device_id_type=MESH)
    pl.semaphore_wait(barrier, n_mp - 1)

    start(vec_parts)
    start_weight(w_parts[0])
    for k in range(pn.pairs):
        start(x_parts[k])

    for h in range(2 * HEADS):
        mcol_s[h] = lane_column(mrow_ref[h:h + 1, :])
    p_s[...] = jnp.zeros_like(p_s)
    gt_s[...] = jnp.zeros_like(gt_s)
    for r in (dqkv_ref, dproj_ref, dfc1_ref, dfc2_ref, dvec_ref, dmix_ref):
        r[...] = jnp.zeros_like(r)

    arrive(vec_parts)
    for m in range(n_mp):
        t = jnp.transpose(jnp.concatenate([pv_s[m], jnp.zeros((TILE - 16, TILE), F32)], axis=0))
        for i in range(pn.vrows):
            if i < len(VECS):
                at = pn.off[VECS[i]][0] + m * CS
            else:
                at = pn.off["fb1"][0] + m * pn.FFS + (i - len(VECS)) * CS
            col_s[at:at + CS, :] = jnp.broadcast_to(t[:CS, i:i + 1], (CS, TILE))

    def turn(src, dst):
        rows, cols = src.shape
        for r in range(0, rows, 384):
            for c in range(0, cols, 384):
                dst[c:c + 384, r:r + 384] = jnp.transpose(src[r:r + 384, c:c + 384])

    relay_weight(w_parts[0])
    for w in w_parts[1:]:
        start_weight(w)
    have_weight(w_parts[0])
    turn(wqkv_s, wqkvT_s)

    def col(name, lo=0, hi=None):
        o, w = pn.off[name]
        hi = w if hi is None else hi
        return twice(col_s[o + lo:o + hi, :])

    def lanes_of(b):
        return pl.ds(pl.multiple_of(b * LANES, LANES), LANES)

    lane = lax.broadcasted_iota(jnp.int32, (C, TILE), 1)

    def take(src, b):
        s = b * PATCHES + my_shift
        r = s % TILE
        t = s // TILE
        left = (TILE - r) % TILE
        last = (s + PATCHES - 1) // TILE
        parts = [pltpu.roll(src[:, pl.ds(aligned(i * TILE, TILE), TILE)].astype(F32), left, 1)
                 for i in (t, t + 1, last)]
        lo = jnp.where(lane < TILE - r, parts[0], parts[1])
        hi = jnp.where(lane < TILE - r, parts[1], parts[2])
        hi = jnp.where(lane < PATCHES - TILE, hi, 0.0)
        return jnp.concatenate([lo, hi], axis=1)

    def put(dst, b, v):
        s = b * PATCHES + my_shift
        r = s % TILE
        t = s // TILE
        at = [pl.ds(aligned((t + i) * TILE, TILE), TILE) for i in range(3)]
        lo = pltpu.roll(v[:, :TILE], r, 1)
        hi = pltpu.roll(v[:, TILE:], r, 1)
        old = dst[:, at[0]].astype(F32)
        dst[:, at[0]] = jnp.where(lane < r, old, lo).astype(BF16)
        dst[:, at[1]] = jnp.where(lane < r, lo, hi).astype(BF16)
        dst[:, at[2]] = hi.astype(BF16)

    def norm(x):
        mean = jnp.sum(x, axis=0, keepdims=True) * inv_c
        d = x - mean
        inv = lax.rsqrt(jnp.sum(d * d, axis=0, keepdims=True) * inv_c + EPSILON)
        return d * inv, inv

    def norm_back(u, n, inv, g):
        s = u * g
        m1 = jnp.sum(s, axis=0, keepdims=True) * inv_c
        m2 = jnp.sum(s * n, axis=0, keepdims=True) * inv_c
        return inv * (s - m1 - n * m2)

    def add_vec(name, v, lo=0):
        o = pn.off[name][0] + lo
        dvec_ref[o:o + v.shape[0], :] += fold(v)

    def when_each(b, at, do):
        for k in range(pn.pairs):
            pl.when(b == at(k))(functools.partial(do, k))

    def phase_a(b, _):
        when_each(b, lambda k: 2 * k, lambda k: arrive(x_parts[k]))
        when_each(b, lambda k: k, lambda k: start(c_parts[k]))
        at = lanes_of(b)
        x = take(xw_s, b)
        x_s[:, at] = x.astype(BF16)
        n1, _inv = norm(x)
        first = (n1 * col("g1") + col("b1")).astype(BF16)
        first_s[:, at] = first
        q = (dot(wqkvT_s[0:C, :], first) + col("qb")).astype(BF16)
        qkv_s[0:C, at] = q
        k = dot(wqkvT_s[C:2 * C, :], first).astype(BF16)
        qkv_s[C:2 * C, at] = k
        v = (dot(wqkvT_s[2 * C:3 * C, :], first) + col("vb")).astype(BF16)
        qkv_s[2 * C:3 * C, at] = v
        maskc = twice(lane_column(mask_ref[pl.ds(me * n_img + b, 1), :])[:KEYS])
        kr = jnp.transpose(k.astype(F32))[:KEYS]
        for h in range(HEADS):
            kmix = (kr * mrow_ref[h:h + 1, :]).astype(BF16)
            logit = dot(kmix, q) + maskc
            top = jnp.max(logit, axis=0, keepdims=True)
            e = jnp.exp(logit - top)
            inv = 1.0 / jnp.sum(e, axis=0, keepdims=True)
            p_s[b, h * LANES:h * LANES + KEYS, :] = (e * inv).astype(BF16)
            vmixT_s[:, h * LANES:(h + 1) * LANES] = (v.astype(F32) * twice(mcol_s[HEADS + h])).astype(BF16)
        a_s[:, at] = dot(vmixT_s[...], p_s[b]).astype(BF16)
        return 0

    lax.fori_loop(0, n_img, phase_a, 0)

    for w in w_parts[1:]:
        relay_weight(w)
    for w, s, d in zip(w_parts[1:], (wproj_s, wfc1_s, wfc2_s), (wprojT_s, wfc1T_s, wfc2T_s)):
        have_weight(w)
        turn(s, d)

    def phase_b(b, _):
        when_each(b, lambda k: 2 * k, lambda k: arrive(c_parts[k]))
        at = lanes_of(b)
        x = x_s[:, at].astype(F32)
        att = a_s[:, at]
        branch = dot(wprojT_s[...], att) + col("pb")
        middle = x + col("s1") * branch
        n2, inv2 = norm(middle)
        second = (n2 * col("g2") + col("b2")).astype(BF16)
        step = 128
        for r in range(0, FF, step):
            hid = dot(wfc1T_s[r:r + step, :], second) + col("fb1", r, r + step)
            cum, slope = gelu_parts(hid)
            act_s[r:r + step, :] = (hid * cum).astype(BF16)
            slope_s[r:r + step, :] = slope
        act = act_s[...]
        mlp = dot(wfc2T_s[...], act) + col("fb2")
        cot = take(cw_s, b)
        put(ow_s, b, middle + col("s2") * mlp)
        when_each(b, lambda k: 2 * k + 1, lambda k: start(o_parts[k]))
        add_vec("s2", cot * mlp)
        g_mlp = (col("s2") * cot).astype(BF16)
        add_vec("fb2", g_mlp.astype(F32))
        for r in range(0, FF, step):
            g_act = dot(wfc2_s[r:r + step, :], g_mlp)
            gh = (g_act * slope_s[r:r + step, :]).astype(BF16)
            gh_s[r:r + step, :] = gh
            add_vec("fb1", gh.astype(F32), r)
            dfc2_ref[r:r + step, :] += dot_nt(act_s[r:r + step, :], g_mlp)
        gh = gh_s[...]
        dfc1_ref[...] += dot_nt(second, gh)
        g_second = dot(wfc1_s[...], gh)
        add_vec("g2", g_second * n2)
        add_vec("b2", g_second)
        g_mid = cot + norm_back(g_second, n2, inv2, col("g2"))
        gm_s[:, at] = g_mid
        add_vec("s1", g_mid * branch)
        g_br = (col("s1") * g_mid).astype(BF16)
        add_vec("pb", g_br.astype(F32))
        dproj_ref[...] += dot_nt(att, g_br)
        a_s[:, at] = dot(wproj_s[...], g_br).astype(BF16)
        return 0

    lax.fori_loop(0, n_img, phase_b, 0)

    def phase_c(b, _):
        at = lanes_of(b)
        da = a_s[:, at]
        q = qkv_s[0:C, at]
        kT = qkv_s[C:2 * C, at].astype(F32)
        vT = qkv_s[2 * C:3 * C, at].astype(F32)
        kr = jnp.transpose(kT)[:KEYS]
        vr = jnp.transpose(vT)[:KEYS]
        gv = jnp.zeros((KEYS, C), F32)
        gk = jnp.zeros((KEYS, C), F32)
        for h in range(HEADS):
            prow = mrow_ref[HEADS + h:HEADS + h + 1, :]
            mrow = mrow_ref[h:h + 1, :]
            vmix = (vr * prow).astype(BF16)
            gs = dot(vmix, da)
            pb16 = p_s[b, h * LANES:h * LANES + KEYS, :]
            p = pb16.astype(F32)
            d = jnp.sum(gs * p, axis=0, keepdims=True)
            gt = (p * (gs - d)).astype(BF16)
            gt_s[h * LANES:h * LANES + KEYS, :] = gt
            w = dot_nt(pb16, da)
            gv = gv + prow * w
            dmix_ref[HEADS + h:HEADS + h + 1, :] += jnp.sum(w * vr, axis=0, keepdims=True)
            xk = dot_nt(gt, q)
            gk = gk + mrow * xk
            dmix_ref[h:h + 1, :] += jnp.sum(xk * kr, axis=0, keepdims=True)
            vmixT_s[:, h * LANES:(h + 1) * LANES] = (kT * twice(mcol_s[h])).astype(BF16)
        gq = dot(vmixT_s[...], gt_s[...]).astype(BF16)
        pad = jnp.zeros((LANES - KEYS, C), F32)
        gkT = jnp.transpose(jnp.concatenate([gk, pad], axis=0)).astype(BF16)
        gvT = jnp.transpose(jnp.concatenate([gv, pad], axis=0)).astype(BF16)
        add_vec("qb", gq.astype(F32))
        add_vec("vb", gvT.astype(F32))
        gj = jnp.concatenate([gq, gkT, gvT], axis=0)
        first = first_s[:, at]
        dqkv_ref[...] += dot_nt(first, gj)
        g_first = dot(wqkv_s[...], gj)
        n1, inv1 = norm(x_s[:, at].astype(F32))
        add_vec("g1", g_first * n1)
        add_vec("b1", g_first)
        put(iw_s, b, gm_s[:, at] + norm_back(g_first, n1, inv1, col("g1")))
        when_each(b, lambda k: 2 * k + 1, lambda k: start(i_parts[k]))
        return 0

    lax.fori_loop(0, n_img, phase_c, 0)

    lane_out = lax.broadcasted_iota(jnp.int32, (CS, TILE), 1)

    def join(recv, dst):
        for j in range(pn.cols // TILE):
            parts = [(m, j - pn.bases[m] // TILE) for m in range(n_mp)
                     if pn.bases[m] <= j * TILE and j * TILE < pn.bases[m] + pn.shifts[m] + pn.tok]
            v = None
            for m, l in parts:
                w = recv[m, :, l * TILE:(l + 1) * TILE]
                v = w if v is None else jnp.where(lane_out < pn.shifts[m], v.astype(F32), w.astype(F32)).astype(BF16)
            dst[:, j * TILE:(j + 1) * TILE] = v

    for k in range(pn.pairs):
        arrive(o_parts[k])
    join(orecv_s, out_ref)
    for k in range(pn.pairs):
        arrive(i_parts[k])
    join(irecv_s, ig_ref)
    for c in sent:
        c.wait_send()


def layer_call(pn, x, cot, ws, mask, pvec, mrow):
    C, CS, FF, n_img, n_mp = pn.C, pn.CS, pn.FF, pn.n_img, pn.n_mp
    S = jax.ShapeDtypeStruct
    T = n_img * LANES
    outs = (S((CS, pn.cols), BF16), S((CS, pn.cols), BF16), S((C, 3 * C), F32), S((C, C), F32), S((C, FF), F32),
            S((FF, C), F32), S((pn.total, TILE), F32), S((2 * HEADS, C), F32))
    V = pltpu.VMEM
    remotes = (4 * pn.pairs + 1) * (n_mp - 1) + 4 * (2 * (pn.nx - 1) + 1)
    locals_ = 4 * pn.pairs + 1 + 4
    scratch = [V((C, pn.wide), BF16), V((C, pn.wide), BF16), V((n_mp, 16, TILE), F32),
               V((C, 3 * C), BF16), V((C, C), BF16), V((C, FF), BF16), V((FF, C), BF16),
               V((3 * C, C), BF16), V((C, C), BF16), V((FF, C), BF16), V((C, FF), BF16),
               V((C, pn.wide), BF16), V((C, pn.wide), BF16),
               V((n_mp, CS, pn.width), BF16), V((n_mp, CS, pn.width), BF16),
               V((C, T), BF16), V((C, T), BF16), V((3 * C, T), BF16), V((n_img, HEADS * LANES, LANES), BF16),
               V((C, T), BF16), V((C, T), F32), V((HEADS * LANES, LANES), BF16), V((C, HEADS * LANES), BF16),
               V((pn.total, TILE), F32), V((2 * HEADS, C, TILE), F32),
               V((FF, LANES), BF16), V((FF, LANES), F32), V((FF, LANES), BF16),
               pltpu.SemaphoreType.DMA((remotes,)), pltpu.SemaphoreType.DMA((remotes,)),
               pltpu.SemaphoreType.DMA((locals_,))]
    vm = pl.BlockSpec(memory_space=pltpu.VMEM)
    hbm = pl.BlockSpec(memory_space=pl.ANY)
    return pl.pallas_call(
        functools.partial(layer_kernel, pn),
        out_shape=outs,
        in_specs=[hbm] * 6 + [vm] * 3,
        out_specs=[vm] * len(outs),
        scratch_shapes=scratch,
        compiler_params=pltpu.CompilerParams(vmem_limit_bytes=63 * 2 ** 20, collective_id=0, has_side_effects=True),
        name="layer",
    )(x, cot, *ws, mask, pvec, mrow)


def local(patches, keep_mask, ln1_gain, ln1_bias, w_qkv, q_bias, v_bias, mix_pre, mix_post, w_proj, proj_bias,
          gamma1, ln2_gain, ln2_bias, w_fc1, fc1_bias, w_fc2, fc2_bias, gamma2, cotangent):
    n_mp = lax.axis_size("mp")
    pn = Plan(n_mp, patches.shape, keep_mask.shape, w_fc2.shape)
    C, CS, FF, FFS = pn.C, pn.CS, pn.FF, pn.FFS
    hd = C // HEADS
    factor = hd ** (-0.5)
    vecs = jnp.stack([ln1_gain, ln1_bias, q_bias, v_bias, proj_bias, gamma1, ln2_gain, ln2_bias, fc2_bias, gamma2])
    vecs = jnp.concatenate([vecs, fc1_bias.reshape(-1, CS)], axis=0).astype(F32)
    pvec = jnp.pad(vecs, ((0, 16 - pn.vrows), (0, TILE - CS)))
    mask = jnp.pad(jnp.where(keep_mask > 0, 0.0, MASKED).astype(F32), ((0, 0), (0, LANES - PATCHES)),
                   constant_values=MASKED)
    mrow = jnp.concatenate([jnp.repeat(mix_pre, hd, axis=1) * factor, jnp.repeat(mix_post.T, hd, axis=1)], 0)
    out, ig, dqkv, dproj, dfc1, dfc2, dvec, dmix = layer_call(
        pn, patches, cotangent, (w_qkv, w_proj, w_fc1, w_fc2), mask, pvec, mrow)
    dm = jnp.sum(dmix.reshape(2, HEADS, HEADS, hd), axis=3)
    pre_total, post_total = lax.psum((dm[0] * factor, dm[1].T), ("dp", "mp"))
    dv = jnp.sum(dvec, axis=1)
    dsmall = dv[:10 * C].reshape(10, n_mp, CS).transpose(1, 0, 2).reshape(n_mp, 10 * CS)
    pieces = [dqkv.reshape(n_mp, -1), dproj.reshape(n_mp, -1), dfc1.reshape(n_mp, -1), dfc2.reshape(n_mp, -1),
              dsmall, dv[10 * C:].reshape(n_mp, -1)]
    packed = jnp.concatenate([p.astype(BF16) for p in pieces], axis=1)
    own = lax.psum_scatter(packed, "mp", scatter_dimension=0, tiled=True)
    own = lax.psum(own, "dp")[0].astype(F32)
    res, at = [], 0
    for shape in ((CS, 3 * C), (CS, C), (CS, FF), (FFS, C), (10, CS), (FFS,)):
        size = 1
        for s in shape:
            size *= s
        res.append(own[at:at + size].reshape(shape))
        at += size
    gqkv, gproj, gfc1, gfc2, gs, gfb1 = res
    return (out, ig, gs[0], gs[1], gqkv, gs[2], gs[3], pre_total, post_total, gproj, gs[4], gs[5],
            gs[6], gs[7], gfc1, gfb1, gfc2, gs[8], gs[9])


def solution(mesh):
    m, mn = P("mp"), P("mp", None)
    big = P("mp", "dp")
    in_specs = (big, P("dp", None), m, m, mn, m, m, P(), P(), mn, m, m, m, m, mn, m, mn, m, m, big)
    out_specs = (big, big, m, m, mn, m, m, P(), P(), mn, m, m, m, m, mn, m, mn, m, m)
    return jax.shard_map(local, mesh=mesh, in_specs=in_specs, out_specs=out_specs, check_vma=False)
```

```python
import functools
import jax
import jax.numpy as jnp
from jax import lax
from jax.experimental import pallas as pl
from jax.experimental.pallas import tpu as pltpu
from jax.sharding import PartitionSpec as P

PATCHES = 196
HEADS = 8
EPSILON = 1e-06
MASKED = -1000000000.0
F32 = jnp.float32
BF16 = jnp.bfloat16
VMEM_BYTES = 63 * 2 ** 20
LANES = 256
KEYS = 208


def dot(a, b):
    return lax.dot_general(a, b, (((1,), (0,)), ((), ())), preferred_element_type=F32)


def dot_nt(a, b):
    return lax.dot_general(a, b, (((1,), (1,)), ((), ())), preferred_element_type=F32)


def twice(col):
    return jnp.concatenate([col, col], axis=1)


def fold(v):
    return v[:, :128] + v[:, 128:]


def lane_column(row):
    return jnp.transpose(jnp.broadcast_to(row, (128, row.shape[1])))


def gelu_parts(h):
    e = jnp.exp(-0.5 * h * h)
    cum = 0.5 * (1.0 + lax.erf(h * 0.7071067811865476))
    return cum, cum + h * (e * 0.3989422804014327)


MESH = pl.DeviceIdType.MESH
TILE = 128
VECS = ("g1", "b1", "qb", "vb", "pb", "s1", "g2", "b2", "fb2", "s2")


class Plan:
    def __init__(self, n_dp, n_mp, patches, keep_mask, w_fc2):
        self.n_dp = n_dp
        self.n_mp = n_mp
        self.nx = n_mp // 2
        self.CS, self.cols = patches
        self.C = self.CS * n_mp
        self.FFS = w_fc2[0]
        self.FF = self.FFS * n_mp
        self.n_img = keep_mask[0] // n_mp
        self.tok = self.n_img * PATCHES
        starts = [self.tok * m for m in range(n_mp)]
        self.bases = [s // TILE * TILE for s in starts]
        self.shifts = [s % TILE for s in starts]
        top = max(self.shifts)
        self.width = -(-(self.tok + top) // TILE) * TILE
        self.wide = self.width + TILE
        self.pairs = self.n_img // 2
        self.in_cuts = [0] + [-(-(2 * PATCHES * (k + 1) + top) // TILE) * TILE for k in range(self.pairs)]
        self.out_cuts = [0] + [2 * PATCHES * (k + 1) // TILE * TILE for k in range(self.pairs - 1)] + [self.width]
        self.vrows = len(VECS) + self.FFS // self.CS
        self.off = {}
        at = 0
        for name in VECS + ("fb1",):
            w = self.FF if name == "fb1" else self.C
            self.off[name] = (at, w)
            at += w
        self.total = at
        fc2 = self.pieces(self.FFS)
        fc1 = self.pieces(self.CS * (self.FF // self.C + 1))
        qkv = self.pieces(self.CS * (3 * self.C // TILE))
        self.groups = ((fc2, self.C), (fc1, self.C), (qkv, TILE))

    def pieces(self, rows):
        return -(-rows // (16 * self.n_dp)) * 16 * self.n_dp

    def group_scratch(self, rows, lanes):
        V = pltpu.VMEM
        nx = self.nx
        return [V((nx * rows if lanes == TILE else 16, lanes), BF16), V((nx, rows, lanes), BF16), V((max(nx - 1, 1), rows, lanes), BF16),
                V((max(nx - 1, 1), rows, lanes), BF16), V((rows, lanes), BF16),
                V((self.n_dp, rows // self.n_dp, lanes), BF16), V((rows, lanes), BF16)]


class Group:
    def __init__(self, pn, refs, share, fill):
        self.pn, self.share, self.fill = pn, share, fill
        self.s1, self.r1, self.s2, self.r2, self.s3, self.r3, self.r4 = refs
        self.prow = self.s3.shape[0] // pn.n_dp

    def build(self, remote, xi, core, sibling, dp):
        pn = self.pn
        self.xi, self.core, self.dp = xi, core, dp
        self.c1 = [remote(self.first(x), self.r1.at[x], {"mp": sibling}) for x in range(pn.nx)]
        self.c2 = [remote(self.s2.at[d - 1], self.r2.at[d - 1], {"mp": ((xi + d) % pn.nx) * 2 + core})
                   for d in range(1, pn.nx)]
        self.c3, self.c4 = [], []
        own = self.r4.at[self.rows(dp)]
        for e in range(1, pn.n_dp):
            to = (dp + e) % pn.n_dp
            self.c3.append(remote(self.s3.at[self.rows(to)], self.r3.at[e], {"dp": to}))
            self.c4.append(remote(own, own, {"dp": to}))

    def first(self, x):
        rows = self.s3.shape[0]
        return self.s1.at[pl.ds(x * rows, rows), :]

    def rows(self, q):
        return pl.ds(pl.multiple_of(q * self.prow, 16), self.prow)

    def over_cores(self):
        for x in range(self.pn.nx):
            self.fill(self.first(x), None, 2 * x + 1 - self.core, lambda at, v: v)
            self.c1[x].start()

    def over_x(self):
        for c in self.c1:
            c.wait_recv()
        for d in range(1, self.pn.nx):
            x = (self.xi + d) % self.pn.nx
            self.fill(self.s2, d - 1, 2 * x + self.core, lambda at, v: v + self.r1[x, at, :].astype(F32))
            self.c2[d - 1].start()

    def over_dp(self):
        for c in self.c2:
            c.wait_recv()

        def add(at, v):
            v = v + self.r1[self.xi, at, :].astype(F32)
            for d in range(1, self.pn.nx):
                v = v + self.r2[d - 1, at, :].astype(F32)
            return v

        self.fill(self.s3, None, 2 * self.xi + self.core, add)
        for c in self.c3:
            c.start()

    def to_all(self):
        v = self.s3[self.rows(self.dp), :].astype(F32)
        for e in range(1, self.pn.n_dp):
            self.c3[e - 1].wait_recv()
            v = v + self.r3[e].astype(F32)
        self.r4[self.rows(self.dp), :] = v.astype(BF16)
        for c in self.c4:
            c.start()

    def finish(self):
        for c in self.c4:
            c.wait_recv()


def layer_kernel(pn, x_hbm, c_hbm, wqkv_hbm, wproj_hbm, wfc1_hbm, wfc2_hbm, keep_ref, pvec_ref, pre_ref, post_ref,
                 out_ref, ig_ref, gqkv_ref, gproj_ref, gfc1_ref, gfc2_ref, gvec_ref, gmix_ref,
                 xw_s, cw_s, pv_s, wqkv_s, wproj_s, wfc1_s, wfc2_s, wqkvT_s, wprojT_s, wfc1T_s, wfc2T_s,
                 orecv_s, irecv_s,
                 x_s, first_s, qkv_s, p_s, a_s, gm_s, gt_s, vmixT_s, col_s, slope_s, gh_s, mrow_s, mask_s,
                 dqkv_ref, dproj_ref, dfc1_ref, dfc2_ref, dvec_ref, dmix_ref,
                 pack_s, hop1_s, pack2_s, hop2_s, *rest):
    group_refs = [list(rest[7 * i:7 * i + 7]) for i in range(3)]
    group_refs[0][0], group_refs[1][0] = wfc1T_s, wfc2_s
    ssem, rsem, lsem = rest[21:]
    ow_s, iw_s, act_s = xw_s, cw_s, gt_s
    C, CS, FF, n_img, n_mp, nx = pn.C, pn.CS, pn.FF, pn.n_img, pn.n_mp, pn.nx
    inv_c = 1.0 / C
    n_dp = pn.n_dp
    dp = lax.axis_index("dp")
    me = lax.axis_index("mp")
    core = me % 2
    xi = me // 2
    sibling = me + 1 - 2 * core
    my_shift = (pn.tok * me) % TILE

    count = [0, 0]
    sent = []

    def remote(src, dst, dev):
        i = count[0]
        count[0] += 1
        copy = pltpu.make_async_remote_copy(src_ref=src, dst_ref=dst, send_sem=ssem.at[i], recv_sem=rsem.at[i],
                                            device_id=dev, device_id_type=MESH)
        sent.append(copy)
        return copy

    def local_copy(src, dst):
        i = count[1]
        count[1] += 1
        return pltpu.make_async_copy(src, dst, lsem.at[i])

    def peer(d):
        return (me + d) % n_mp

    def aligned(v, n):
        return pl.multiple_of(v, n)

    def window(src, dst, k):
        lo, hi = pn.in_cuts[k], pn.in_cuts[k + 1]
        mine = dst.at[pl.ds(aligned(me * CS, CS), CS), pl.ds(lo, hi - lo)]

        def part(m):
            base = (pn.tok * m) // TILE * TILE
            return src.at[:, pl.ds(aligned(base + lo, TILE), hi - lo)]

        return [local_copy(part(me), mine)] + [remote(part(peer(d)), mine, {"mp": peer(d)}) for d in range(1, n_mp)]

    x_parts = [window(x_hbm, xw_s, k) for k in range(pn.pairs)]
    c_parts = [window(c_hbm, cw_s, k) for k in range(pn.pairs)]
    vec_parts = [local_copy(pvec_ref, pv_s.at[me])]
    vec_parts += [remote(pvec_ref, pv_s.at[me], {"mp": peer(d)}) for d in range(1, n_mp)]

    def weight(src, dst):
        rows = src.shape[0]

        def shard(m):
            return dst.at[pl.ds(aligned(m * rows, rows), rows), :]

        own = local_copy(src, shard(me))
        across = [remote(src, shard(me), {"mp": ((xi + d) % nx) * 2 + core}) for d in range(1, nx)]
        beside = remote(src, shard(me), {"mp": sibling})
        relay = []
        for d in range(1, nx):
            s = shard(((xi + nx - d) % nx) * 2 + core)
            relay.append(remote(s, s, {"mp": sibling}))
        return own, across, beside, relay

    w_parts = [weight(s, d) for s, d in ((wqkv_hbm, wqkv_s), (wproj_hbm, wproj_s), (wfc1_hbm, wfc1_s),
                                         (wfc2_hbm, wfc2_s))]

    def result(src, dst, k):
        lo, hi = pn.out_cuts[k], pn.out_cuts[k + 1]
        there = dst.at[me, :, pl.ds(lo, hi - lo)]

        def part(m):
            return src.at[pl.ds(aligned(m * CS, CS), CS), pl.ds(lo, hi - lo)]

        return [local_copy(part(me), there)] + [remote(part(peer(d)), there, {"mp": peer(d)}) for d in range(1, n_mp)]

    o_parts = [result(ow_s, orecv_s, k) for k in range(pn.pairs)]
    i_parts = [result(iw_s, irecv_s, k) for k in range(pn.pairs)]

    def fill_fc2(dst, slot, j, add):
        put_rows(dst, slot, 0, add, dfc2_ref[pl.ds(aligned(j * pn.FFS, pn.FFS), pn.FFS), :])

    def fill_fc1(dst, slot, j, add):
        at = pl.ds(aligned(j * CS, CS), CS)
        for i in range(FF // C):
            put_rows(dst, slot, i * CS, add, dfc1_ref[at, i * C:(i + 1) * C])
        put_rows(dst, slot, FF // C * CS, add, dproj_ref[at, :])

    def fill_qkv(dst, slot, j, add):
        at = pl.ds(aligned(j * CS, CS), CS)
        for i in range(3 * C // TILE):
            put_rows(dst, slot, i * CS, add, dqkv_ref[at, i * TILE:(i + 1) * TILE])

    def put_rows(dst, slot, lo, add, v):
        at = slice(lo, lo + v.shape[0])
        v = add(at, v).astype(BF16)
        if slot is None:
            dst[at, :] = v
        else:
            dst[slot, at, :] = v

    groups = [Group(pn, r, None, f) for r, f in zip(group_refs, (fill_fc2, fill_fc1, fill_qkv))]
    for g in groups:
        g.build(remote, xi, core, sibling, dp)
    g_fc2, g_fc1, g_qkv = groups
    hop1 = [remote(pack_s.at[peer(d)], hop1_s.at[me], {"mp": peer(d)}) for d in range(1, n_mp)]
    hop2 = [remote(pack2_s, hop2_s.at[dp], {"dp": (dp + e) % n_dp}) for e in range(1, n_dp)]

    def start(copies):
        for c in copies:
            c.start()

    def arrive(copies):
        copies[0].wait()
        for c in copies[1:]:
            c.wait_recv()

    def start_weight(w):
        own, across, beside, _ = w
        own.start()
        start(across)
        beside.start()

    def relay_weight(w):
        _, across, _, relay = w
        for a, r in zip(across, relay):
            a.wait_recv()
            r.start()

    def have_weight(w):
        own, _, beside, relay = w
        own.wait()
        beside.wait_recv()
        for r in relay:
            r.wait_recv()

    barrier = pltpu.get_barrier_semaphore()
    for d in range(1, n_mp):
        pl.semaphore_signal(barrier, inc=1, device_id={"mp": peer(d)}, device_id_type=MESH)
    for e in range(1, n_dp):
        pl.semaphore_signal(barrier, inc=1, device_id={"dp": (dp + e) % n_dp}, device_id_type=MESH)
    pl.semaphore_wait(barrier, n_mp - 1 + n_dp - 1)

    start(vec_parts)
    start_weight(w_parts[0])
    for k in range(pn.pairs):
        start(x_parts[k])

    hd = C // HEADS
    factor = hd ** (-0.5)
    head_of = lax.broadcasted_iota(jnp.int32, (1, C), 1) // hd
    for h in range(HEADS):
        pre = post = jnp.zeros((1, C), F32)
        for g in range(HEADS):
            pre = jnp.where(head_of == g, pre_ref[h, g] * factor, pre)
            post = jnp.where(head_of == g, post_ref[g, h], post)
        mrow_s[h:h + 1, :] = pre
        mrow_s[HEADS + h:HEADS + h + 1, :] = post
    mask_s[...] = jnp.full_like(mask_s, MASKED)
    for i in range(n_img):
        keep = keep_ref[pl.ds(me * n_img + i, 1), :]
        mask_s[i:i + 1, 0:PATCHES] = jnp.where(keep > 0, 0.0, MASKED)
    p_s[...] = jnp.zeros_like(p_s)
    for r in (dqkv_ref, dproj_ref, dfc1_ref, dfc2_ref, dvec_ref, dmix_ref):
        r[...] = jnp.zeros_like(r)

    arrive(vec_parts)
    for m in range(n_mp):
        t = jnp.transpose(jnp.concatenate([pv_s[m], jnp.zeros((TILE - 16, TILE), F32)], axis=0))
        for i in range(pn.vrows):
            if i < len(VECS):
                at = pn.off[VECS[i]][0] + m * CS
            else:
                at = pn.off["fb1"][0] + m * pn.FFS + (i - len(VECS)) * CS
            col_s[at:at + CS, :] = jnp.broadcast_to(t[:CS, i:i + 1], (CS, TILE))

    def turn(src, dst):
        rows, cols = src.shape
        for r in range(0, rows, 384):
            for c in range(0, cols, 384):
                dst[c:c + 384, r:r + 384] = jnp.transpose(src[r:r + 384, c:c + 384])

    relay_weight(w_parts[0])
    for w in w_parts[1:]:
        start_weight(w)
    have_weight(w_parts[0])
    turn(wqkv_s, wqkvT_s)

    def col(name, lo=0, hi=None):
        o, w = pn.off[name]
        hi = w if hi is None else hi
        return twice(col_s[o + lo:o + hi, :])

    def lanes_of(b):
        return pl.ds(pl.multiple_of(b * LANES, LANES), LANES)

    lane = lax.broadcasted_iota(jnp.int32, (C, TILE), 1)

    def take(src, b):
        s = b * PATCHES + my_shift
        r = s % TILE
        t = s // TILE
        left = (TILE - r) % TILE
        last = (s + PATCHES - 1) // TILE
        parts = [pltpu.roll(src[:, pl.ds(aligned(i * TILE, TILE), TILE)].astype(F32), left, 1)
                 for i in (t, t + 1, last)]
        lo = jnp.where(lane < TILE - r, parts[0], parts[1])
        hi = jnp.where(lane < TILE - r, parts[1], parts[2])
        hi = jnp.where(lane < PATCHES - TILE, hi, 0.0)
        return jnp.concatenate([lo, hi], axis=1)

    def put(dst, b, v):
        s = b * PATCHES + my_shift
        r = s % TILE
        t = s // TILE
        at = [pl.ds(aligned((t + i) * TILE, TILE), TILE) for i in range(3)]
        lo = pltpu.roll(v[:, :TILE], r, 1)
        hi = pltpu.roll(v[:, TILE:], r, 1)
        old = dst[:, at[0]].astype(F32)
        dst[:, at[0]] = jnp.where(lane < r, old, lo).astype(BF16)
        dst[:, at[1]] = jnp.where(lane < r, lo, hi).astype(BF16)
        dst[:, at[2]] = hi.astype(BF16)

    def norm(x):
        mean = jnp.sum(x, axis=0, keepdims=True) * inv_c
        d = x - mean
        inv = lax.rsqrt(jnp.sum(d * d, axis=0, keepdims=True) * inv_c + EPSILON)
        return d * inv, inv

    def norm_back(u, n, inv, g):
        s = u * g
        m1 = jnp.sum(s, axis=0, keepdims=True) * inv_c
        m2 = jnp.sum(s * n, axis=0, keepdims=True) * inv_c
        return inv * (s - m1 - n * m2)

    def add_vec(name, v, lo=0):
        o = pn.off[name][0] + lo
        dvec_ref[o:o + v.shape[0], :] += fold(v)

    def when_each(b, at, do):
        for k in range(pn.pairs):
            pl.when(b == at(k))(functools.partial(do, k))

    def phase_a(b, _):
        when_each(b, lambda k: 2 * k, lambda k: arrive(x_parts[k]))
        when_each(b, lambda k: k, lambda k: start(c_parts[k]))
        at = lanes_of(b)
        x = take(xw_s, b)
        x_s[:, at] = x.astype(BF16)
        n1, _inv = norm(x)
        first = (n1 * col("g1") + col("b1")).astype(BF16)
        first_s[:, at] = first
        q = (dot(wqkvT_s[0:C, :], first) + col("qb")).astype(BF16)
        qkv_s[0:C, at] = q
        k = dot(wqkvT_s[C:2 * C, :], first).astype(BF16)
        qkv_s[C:2 * C, at] = k
        v = (dot(wqkvT_s[2 * C:3 * C, :], first) + col("vb")).astype(BF16)
        qkv_s[2 * C:3 * C, at] = v
        maskc = twice(lane_column(mask_s[pl.ds(b, 1), :])[:KEYS])
        kr = jnp.transpose(k.astype(F32))[:KEYS]
        for h in range(HEADS):
            kmix = (kr * mrow_s[h:h + 1, :]).astype(BF16)
            logit = dot(kmix, q) + maskc
            top = jnp.max(logit, axis=0, keepdims=True)
            e = jnp.exp(logit - top)
            inv = 1.0 / jnp.sum(e, axis=0, keepdims=True)
            p_s[b, h * LANES:h * LANES + KEYS, :] = (e * inv).astype(BF16)
            vf = v.astype(F32)
            for g in range(HEADS):
                at_g = slice(g * hd, (g + 1) * hd)
                vmixT_s[at_g, h * LANES:(h + 1) * LANES] = (vf[at_g] * post_ref[g, h]).astype(BF16)
        a_s[:, at] = dot(vmixT_s[...], p_s[b]).astype(BF16)
        return 0

    lax.fori_loop(0, n_img, phase_a, 0)

    for w in w_parts[1:]:
        relay_weight(w)
    for w, s, d in zip(w_parts[1:], (wproj_s, wfc1_s, wfc2_s), (wprojT_s, wfc1T_s, wfc2T_s)):
        have_weight(w)
        turn(s, d)

    def phase_b(b, _):
        when_each(b, lambda k: 2 * k, lambda k: arrive(c_parts[k]))
        at = lanes_of(b)
        x = x_s[:, at].astype(F32)
        att = a_s[:, at]
        branch = dot(wprojT_s[...], att) + col("pb")
        middle = x + col("s1") * branch
        n2, inv2 = norm(middle)
        second = (n2 * col("g2") + col("b2")).astype(BF16)
        step = 128
        for r in range(0, FF, step):
            hid = dot(wfc1T_s[r:r + step, :], second) + col("fb1", r, r + step)
            cum, slope = gelu_parts(hid)
            act_s[r:r + step, :] = (hid * cum).astype(BF16)
            slope_s[r:r + step, :] = slope
        act = act_s[0:FF, :]
        mlp = dot(wfc2T_s[...], act) + col("fb2")
        cot = take(cw_s, b)
        put(ow_s, b, middle + col("s2") * mlp)
        when_each(b, lambda k: 2 * k + 1, lambda k: start(o_parts[k]))
        add_vec("s2", cot * mlp)
        g_mlp = (col("s2") * cot).astype(BF16)
        add_vec("fb2", g_mlp.astype(F32))
        for r in range(0, FF, step):
            g_act = dot(wfc2_s[r:r + step, :], g_mlp)
            gh = (g_act * slope_s[r:r + step, :]).astype(BF16)
            gh_s[r:r + step, :] = gh
            add_vec("fb1", gh.astype(F32), r)
            dfc2_ref[r:r + step, :] += dot_nt(act_s[r:r + step, :], g_mlp)
        gh = gh_s[...]
        dfc1_ref[...] += dot_nt(second, gh)
        g_second = dot(wfc1_s[...], gh)
        add_vec("g2", g_second * n2)
        add_vec("b2", g_second)
        g_mid = cot + norm_back(g_second, n2, inv2, col("g2"))
        gm_s[:, at] = g_mid
        add_vec("s1", g_mid * branch)
        g_br = (col("s1") * g_mid).astype(BF16)
        add_vec("pb", g_br.astype(F32))
        dproj_ref[...] += dot_nt(att, g_br)
        a_s[:, at] = dot(wproj_s[...], g_br).astype(BF16)
        return 0

    lax.fori_loop(0, n_img, phase_b, 0)

    def phase_c(b, _):
        at = lanes_of(b)
        da = a_s[:, at]
        q = qkv_s[0:C, at]
        kT = qkv_s[C:2 * C, at].astype(F32)
        vT = qkv_s[2 * C:3 * C, at].astype(F32)
        kr = jnp.transpose(kT)[:KEYS]
        vr = jnp.transpose(vT)[:KEYS]
        gv = jnp.zeros((KEYS, C), F32)
        gk = jnp.zeros((KEYS, C), F32)
        for h in range(HEADS):
            prow = mrow_s[HEADS + h:HEADS + h + 1, :]
            mrow = mrow_s[h:h + 1, :]
            vmix = (vr * prow).astype(BF16)
            gs = dot(vmix, da)
            pb16 = p_s[b, h * LANES:h * LANES + KEYS, :]
            p = pb16.astype(F32)
            d = jnp.sum(gs * p, axis=0, keepdims=True)
            gt = (p * (gs - d)).astype(BF16)
            gt_s[h * LANES:h * LANES + KEYS, :] = gt
            w = dot_nt(pb16, da)
            gv = gv + prow * w
            dmix_ref[HEADS + h:HEADS + h + 1, :] += jnp.sum(w * vr, axis=0, keepdims=True)
            xk = dot_nt(gt, q)
            gk = gk + mrow * xk
            dmix_ref[h:h + 1, :] += jnp.sum(xk * kr, axis=0, keepdims=True)
            for g in range(HEADS):
                at_g = slice(g * hd, (g + 1) * hd)
                vmixT_s[at_g, h * LANES:(h + 1) * LANES] = (kT[at_g] * (pre_ref[h, g] * factor)).astype(BF16)
        gq = dot(vmixT_s[...], gt_s[...]).astype(BF16)
        pad = jnp.zeros((LANES - KEYS, C), F32)
        gkT = jnp.transpose(jnp.concatenate([gk, pad], axis=0)).astype(BF16)
        gvT = jnp.transpose(jnp.concatenate([gv, pad], axis=0)).astype(BF16)
        add_vec("qb", gq.astype(F32))
        add_vec("vb", gvT.astype(F32))
        gj = jnp.concatenate([gq, gkT, gvT], axis=0)
        qkv_s[:, at] = gj
        dqkv_ref[...] += dot_nt(first_s[:, at], gj)
        for step, do in ((1, g_fc2.over_x), (2, g_fc1.over_x), (4, g_fc2.over_dp), (5, g_fc1.over_dp),
                         (6, g_fc2.to_all)):
            pl.when(b == step * n_img // 8)(do)
        return 0

    for w in w_parts[1:]:
        for c in w[3]:
            c.wait_send()
    g_fc2.over_cores()
    g_fc1.over_cores()
    gt_s[...] = jnp.zeros_like(gt_s)
    lax.fori_loop(0, n_img, phase_c, 0)
    g_qkv.over_cores()

    def phase_d(b, _):
        at = lanes_of(b)
        g_first = dot(wqkv_s[...], qkv_s[:, at])
        n1, inv1 = norm(x_s[:, at].astype(F32))
        add_vec("g1", g_first * n1)
        add_vec("b1", g_first)
        put(iw_s, b, gm_s[:, at] + norm_back(g_first, n1, inv1, col("g1")))
        when_each(b, lambda k: 2 * k + 1, lambda k: start(i_parts[k]))
        for step, do in ((1, g_qkv.over_x), (3, g_fc1.to_all), (6, g_qkv.over_dp)):
            pl.when(b == step * n_img // 8)(do)
        return 0

    lax.fori_loop(0, n_img, phase_d, 0)

    sums = []
    for m in range(n_mp):
        for i in range(pn.vrows):
            if i < len(VECS):
                o = pn.off[VECS[i]][0] + m * CS
            else:
                o = pn.off["fb1"][0] + m * pn.FFS + (i - len(VECS)) * CS
            block = jnp.concatenate([dvec_ref[o:o + CS, :], jnp.zeros((TILE - CS, TILE), F32)], axis=0)
            pack_s[m, i:i + 1, :] = jnp.sum(jnp.transpose(block), axis=0, keepdims=True)
        pack_s[m, pn.vrows:16, :] = jnp.zeros((16 - pn.vrows, TILE), F32)
    lane_of = lax.broadcasted_iota(jnp.int32, (2 * HEADS, TILE), 1)
    heads = lax.broadcasted_iota(jnp.int32, (2 * HEADS, C), 1) // hd
    dmix = dmix_ref[...]
    mix = jnp.zeros((2 * HEADS, TILE), F32)
    for g in range(HEADS):
        mix = jnp.where(lane_of == g, jnp.sum(jnp.where(heads == g, dmix, 0.0), axis=1, keepdims=True), mix)
    for m in range(n_mp):
        pack_s[m, 16:32, :] = mix
    start(hop1)
    hop1_s[me] = pack_s[me]
    for c in hop1:
        c.wait_recv()
    both = hop1_s[0]
    for m in range(1, n_mp):
        both = both + hop1_s[m]
    pack2_s[...] = both
    start(hop2)
    hop2_s[dp] = both
    g_qkv.to_all()
    for c in hop2:
        c.wait_recv()
    both = hop2_s[0]
    for e in range(1, n_dp):
        both = both + hop2_s[e]
    gvec_ref[...] = both[0:16]
    gmix_ref[...] = both[16:32]

    lane_out = lax.broadcasted_iota(jnp.int32, (CS, TILE), 1)

    def join(recv, dst):
        for j in range(pn.cols // TILE):
            parts = [(m, j - pn.bases[m] // TILE) for m in range(n_mp)
                     if pn.bases[m] <= j * TILE and j * TILE < pn.bases[m] + pn.shifts[m] + pn.tok]
            v = None
            for m, l in parts:
                w = recv[m, :, l * TILE:(l + 1) * TILE]
                v = w if v is None else jnp.where(lane_out < pn.shifts[m], v.astype(F32), w.astype(F32)).astype(BF16)
            dst[:, j * TILE:(j + 1) * TILE] = v

    for k in range(pn.pairs):
        arrive(o_parts[k])
    join(orecv_s, out_ref)
    for k in range(pn.pairs):
        arrive(i_parts[k])
    join(irecv_s, ig_ref)
    g_fc2.finish()
    gfc2_ref[...] = g_fc2.r4[0:pn.FFS, :].astype(F32)
    g_fc1.finish()
    for i in range(FF // C):
        gfc1_ref[:, i * C:(i + 1) * C] = g_fc1.r4[i * CS:(i + 1) * CS, :].astype(F32)
    gproj_ref[...] = g_fc1.r4[FF // C * CS:(FF // C + 1) * CS, :].astype(F32)
    g_qkv.finish()
    for i in range(3 * C // TILE):
        gqkv_ref[:, i * TILE:(i + 1) * TILE] = g_qkv.r4[i * CS:(i + 1) * CS, :].astype(F32)
    relays = [id(c) for w in w_parts[1:] for c in w[3]]
    for c in sent:
        if id(c) not in relays:
            c.wait_send()


def layer_call(pn, x, cot, ws, keep, pvec, pre, post):
    C, CS, FF, n_img, n_mp, n_dp = pn.C, pn.CS, pn.FF, pn.n_img, pn.n_mp, pn.n_dp
    S = jax.ShapeDtypeStruct
    T = n_img * LANES
    outs = (S((CS, pn.cols), BF16), S((CS, pn.cols), BF16), S((CS, 3 * C), F32), S((CS, C), F32), S((CS, FF), F32),
            S((pn.FFS, C), F32), S((16, TILE), F32), S((2 * HEADS, TILE), F32))
    V = pltpu.VMEM
    remotes = (4 * pn.pairs + 2) * (n_mp - 1) + 4 * (2 * (pn.nx - 1) + 1)
    remotes += 3 * (2 * pn.nx - 1 + 2 * (n_dp - 1)) + n_dp - 1
    locals_ = 4 * pn.pairs + 1 + 4
    scratch = [V((C, pn.wide), BF16), V((C, pn.wide), BF16), V((n_mp, 16, TILE), F32),
               V((C, 3 * C), BF16), V((C, C), BF16), V((C, FF), BF16), V((FF, C), BF16),
               V((3 * C, C), BF16), V((C, C), BF16), V((FF, C), BF16), V((C, FF), BF16),
               V((n_mp, CS, pn.width), BF16), V((n_mp, CS, pn.width), BF16),
               V((C, T), BF16), V((C, T), BF16), V((3 * C, T), BF16), V((n_img, HEADS * LANES, LANES), BF16),
               V((C, T), BF16), V((C, T), F32), V((HEADS * LANES, LANES), BF16), V((C, HEADS * LANES), BF16),
               V((pn.total, TILE), F32), V((FF, LANES), F32), V((FF, LANES), BF16),
               V((2 * HEADS, C), F32), V((max(n_img, 8), LANES), F32),
               V((C, 3 * C), F32), V((C, C), F32), V((C, FF), F32), V((FF, C), F32), V((pn.total, TILE), F32),
               V((2 * HEADS, C), F32),
               V((n_mp, 32, TILE), F32), V((n_mp, 32, TILE), F32), V((32, TILE), F32), V((n_dp, 32, TILE), F32)]
    for rows, lanes in pn.groups:
        scratch += pn.group_scratch(rows, lanes)
    scratch += [pltpu.SemaphoreType.DMA((remotes,)), pltpu.SemaphoreType.DMA((remotes,)),
                pltpu.SemaphoreType.DMA((locals_,))]
    vm = pl.BlockSpec(memory_space=pltpu.VMEM)
    sm = pl.BlockSpec(memory_space=pltpu.SMEM)
    hbm = pl.BlockSpec(memory_space=pl.ANY)
    return pl.pallas_call(
        functools.partial(layer_kernel, pn),
        out_shape=outs,
        in_specs=[hbm] * 6 + [vm] * 2 + [sm] * 2,
        out_specs=[vm] * len(outs),
        scratch_shapes=scratch,
        compiler_params=pltpu.CompilerParams(vmem_limit_bytes=VMEM_BYTES, collective_id=0, has_side_effects=True),
        name="layer",
    )(x, cot, *ws, keep, pvec, pre, post)


def local(patches, keep_mask, ln1_gain, ln1_bias, w_qkv, q_bias, v_bias, mix_pre, mix_post, w_proj, proj_bias,
          gamma1, ln2_gain, ln2_bias, w_fc1, fc1_bias, w_fc2, fc2_bias, gamma2, cotangent):
    n_mp, n_dp = lax.axis_size("mp"), lax.axis_size("dp")
    pn = Plan(n_dp, n_mp, patches.shape, keep_mask.shape, w_fc2.shape)
    C, CS = pn.C, pn.CS
    factor = (C // HEADS) ** (-0.5)
    vecs = jnp.stack([ln1_gain, ln1_bias, q_bias, v_bias, proj_bias, gamma1, ln2_gain, ln2_bias, fc2_bias, gamma2])
    vecs = jnp.concatenate([vecs, fc1_bias.reshape(-1, CS)], axis=0).astype(F32)
    pvec = jnp.pad(vecs, ((0, 16 - pn.vrows), (0, TILE - CS)))
    out, ig, gqkv, gproj, gfc1, gfc2, gvec, gmix = layer_call(
        pn, patches, cotangent, (w_qkv, w_proj, w_fc1, w_fc2), keep_mask, pvec, mix_pre, mix_post)
    gs = gvec[:, :CS]
    gfb1 = gs[len(VECS):pn.vrows].reshape(-1)
    pre_total = gmix[:HEADS, :HEADS] * factor
    post_total = gmix[HEADS:, :HEADS].T
    return (out, ig, gs[0], gs[1], gqkv, gs[2], gs[3], pre_total, post_total, gproj, gs[4], gs[5],
            gs[6], gs[7], gfc1, gfb1, gfc2, gs[8], gs[9])


def solution(mesh):
    m, mn = P("mp"), P("mp", None)
    big = P("mp", "dp")
    in_specs = (big, P("dp", None), m, m, mn, m, m, P(), P(), mn, m, m, m, m, mn, m, mn, m, m, big)
    out_specs = (big, big, m, m, mn, m, m, P(), P(), mn, m, m, m, m, mn, m, mn, m, m)
    return jax.shard_map(local, mesh=mesh, in_specs=in_specs, out_specs=out_specs, check_vma=False)
```

```python
import functools
import jax
import jax.numpy as jnp
from jax import lax
from jax.experimental import pallas as pl
from jax.experimental.pallas import tpu as pltpu
from jax.sharding import PartitionSpec as P

PATCHES = 196
HEADS = 8
EPSILON = 1e-06
MASKED = -1000000000.0
F32 = jnp.float32
BF16 = jnp.bfloat16
VMEM_BYTES = 63 * 2 ** 20
LANES = 256
KEYS = 208


def dot(a, b):
    return lax.dot_general(a, b, (((1,), (0,)), ((), ())), preferred_element_type=F32)


def dot_nt(a, b):
    return lax.dot_general(a, b, (((1,), (1,)), ((), ())), preferred_element_type=F32)


def twice(col):
    return jnp.concatenate([col, col], axis=1)


def fold(v):
    return v[:, :128] + v[:, 128:]


def lane_column(row):
    return jnp.transpose(jnp.broadcast_to(row, (128, row.shape[1])))


def gelu_parts(h):
    e = jnp.exp(-0.5 * h * h)
    cum = 0.5 * (1.0 + lax.erf(h * 0.7071067811865476))
    return cum, cum + h * (e * 0.3989422804014327)


MESH = pl.DeviceIdType.MESH
TILE = 128
VECS = ("g1", "b1", "qb", "vb", "pb", "s1", "g2", "b2", "fb2", "s2")


class Plan:
    def __init__(self, n_dp, n_mp, patches, keep_mask, w_fc2):
        self.n_dp = n_dp
        self.n_mp = n_mp
        self.nx = n_mp // 2
        self.CS, self.cols = patches
        self.C = self.CS * n_mp
        self.FFS = w_fc2[0]
        self.FF = self.FFS * n_mp
        self.n_img = keep_mask[0] // n_mp
        self.tok = self.n_img * PATCHES
        starts = [self.tok * m for m in range(n_mp)]
        self.bases = [s // TILE * TILE for s in starts]
        self.shifts = [s % TILE for s in starts]
        top = max(self.shifts)
        self.width = -(-(self.tok + top) // TILE) * TILE
        self.wide = self.width + TILE
        self.pairs = self.n_img // 2
        self.in_cuts = [0] + [-(-(2 * PATCHES * (k + 1) + top) // TILE) * TILE for k in range(self.pairs)]
        self.out_cuts = [0] + [2 * PATCHES * (k + 1) // TILE * TILE for k in range(self.pairs - 1)] + [self.width]
        self.vrows = len(VECS) + self.FFS // self.CS
        self.off = {}
        at = 0
        for name in VECS + ("fb1",):
            w = self.FF if name == "fb1" else self.C
            self.off[name] = (at, w)
            at += w
        self.total = at
        fc2 = self.pieces(self.FFS)
        fc1 = self.pieces(self.CS * (self.FF // self.C + 1))
        qkv = self.pieces(self.CS * (3 * self.C // TILE))
        self.groups = ((fc2, self.C), (fc1, self.C), (qkv, TILE))

        self.lane_parts = n_dp // 2
        self.spread = (self.FFS % (16 * n_dp) == 0 and self.CS % 32 == 0 and n_dp % 2 == 0
                       and self.FF % (TILE * self.lane_parts) == 0)

    def pieces(self, rows):
        return -(-rows // (16 * self.n_dp)) * 16 * self.n_dp

    def group_scratch(self, rows, lanes):
        V = pltpu.VMEM
        nx = self.nx
        return [V((nx * rows if lanes == TILE else 16, lanes), BF16), V((nx, rows, lanes), BF16), V((max(nx - 1, 1), rows, lanes), BF16),
                V((max(nx - 1, 1), rows, lanes), BF16), V((rows, lanes), BF16),
                V((self.n_dp, rows // self.n_dp, lanes), BF16)]


class Group:
    def __init__(self, pn, refs, share, fill):
        self.pn, self.share, self.fill = pn, share, fill
        self.s1, self.r1, self.s2, self.r2, self.s3, self.r3, self.r4 = refs
        self.prow = self.s3.shape[0] // pn.n_dp

    def build(self, remote, xi, core, sibling, dp):
        pn = self.pn
        self.xi, self.core, self.dp = xi, core, dp
        self.c1 = [remote(self.first(x), self.r1.at[x], {"mp": sibling}) for x in range(pn.nx)]
        self.c2 = [remote(self.s2.at[d - 1], self.r2.at[d - 1], {"mp": ((xi + d) % pn.nx) * 2 + core})
                   for d in range(1, pn.nx)]
        self.c3, self.c4 = [], []
        own = self.r4.at[self.rows(dp)]
        for e in range(1, pn.n_dp):
            to = (dp + e) % pn.n_dp
            self.c3.append(remote(self.s3.at[self.rows(to)], self.r3.at[e], {"dp": to}))
            self.c4.append(remote(own, own, {"dp": to}))

    def first(self, x):
        rows = self.s3.shape[0]
        return self.s1.at[pl.ds(x * rows, rows), :]

    def rows(self, q):
        return pl.ds(pl.multiple_of(q * self.prow, 16), self.prow)

    def over_cores(self):
        for x in range(self.pn.nx):
            self.fill(self.first(x), None, 2 * x + 1 - self.core, lambda at, v: v)
            self.c1[x].start()

    def over_x(self):
        for c in self.c1:
            c.wait_recv()
        for d in range(1, self.pn.nx):
            x = (self.xi + d) % self.pn.nx
            self.fill(self.s2, d - 1, 2 * x + self.core, lambda at, v: v + self.r1[x, at, :].astype(F32))
            self.c2[d - 1].start()

    def over_dp(self):
        for c in self.c2:
            c.wait_recv()

        def add(at, v):
            v = v + self.r1[self.xi, at, :].astype(F32)
            for d in range(1, self.pn.nx):
                v = v + self.r2[d - 1, at, :].astype(F32)
            return v

        self.fill(self.s3, None, 2 * self.xi + self.core, add)
        for c in self.c3:
            c.start()

    def to_all(self):
        v = self.s3[self.rows(self.dp), :].astype(F32)
        for e in range(1, self.pn.n_dp):
            self.c3[e - 1].wait_recv()
            v = v + self.r3[e].astype(F32)
        self.r4[self.rows(self.dp), :] = v.astype(BF16)
        for c in self.c4:
            c.start()

    def finish(self):
        for c in self.c4:
            c.wait_recv()


def layer_kernel(pn, x_hbm, c_hbm, wqkv_hbm, wproj_hbm, wfc1_hbm, wfc2_hbm, keep_ref, pre_ref, post_ref, *rest):
    vec_refs, rest = rest[:len(VECS) + 1], rest[len(VECS) + 1:]
    layer_body(pn, x_hbm, c_hbm, wqkv_hbm, wproj_hbm, wfc1_hbm, wfc2_hbm, keep_ref, pre_ref, post_ref, vec_refs,
               *rest)


def layer_body(pn, x_hbm, c_hbm, wqkv_hbm, wproj_hbm, wfc1_hbm, wfc2_hbm, keep_ref, pre_ref, post_ref, vec_refs,
                 orecv_s, irecv_s, small_ref, r4_fc2, r4_fc1, r4_qkv,
                 xw_s, cw_s, pv_s, wqkv_s, wproj_s, wfc1_s, wfc2_s, wqkvT_s, wprojT_s, wfc1T_s, wfc2T_s,
                 x_s, first_s, qkv_s, p_s, a_s, gm_s, gt_s, vmixT_s, col_s, slope_s, gh_s, mrow_s, mask_s,
                 dqkv_ref, dproj_ref, dfc1_ref, dfc2_ref, dvec_ref, dmix_ref,
                 pack_s, hop1_s, pack2_s, hop2_s, pvec_ref, *rest):
    group_refs = [list(rest[6 * i:6 * i + 6]) + [r] for i, r in enumerate((r4_fc2, r4_fc1, r4_qkv))]
    group_refs[0][0], group_refs[1][0] = wfc1T_s, wfc2_s
    ssem, rsem, lsem = rest[18:]
    ow_s, iw_s, act_s = xw_s, cw_s, gt_s
    C, CS, FF, n_img, n_mp, nx = pn.C, pn.CS, pn.FF, pn.n_img, pn.n_mp, pn.nx
    inv_c = 1.0 / C
    n_dp = pn.n_dp
    dp = lax.axis_index("dp")
    me = lax.axis_index("mp")
    core = me % 2
    xi = me // 2
    sibling = me + 1 - 2 * core
    my_shift = (pn.tok * me) % TILE

    count = [0, 0]
    sent = []

    def remote(src, dst, dev):
        i = count[0]
        count[0] += 1
        copy = pltpu.make_async_remote_copy(src_ref=src, dst_ref=dst, send_sem=ssem.at[i], recv_sem=rsem.at[i],
                                            device_id=dev, device_id_type=MESH)
        sent.append(copy)
        return copy

    def local_copy(src, dst):
        i = count[1]
        count[1] += 1
        return pltpu.make_async_copy(src, dst, lsem.at[i])

    def peer(d):
        return (me + d) % n_mp

    def aligned(v, n):
        return pl.multiple_of(v, n)

    def window(src, dst, k):
        lo, hi = pn.in_cuts[k], pn.in_cuts[k + 1]
        mine = dst.at[pl.ds(aligned(me * CS, CS), CS), pl.ds(lo, hi - lo)]

        def part(m):
            base = (pn.tok * m) // TILE * TILE
            return src.at[:, pl.ds(aligned(base + lo, TILE), hi - lo)]

        return [local_copy(part(me), mine)] + [remote(part(peer(d)), mine, {"mp": peer(d)}) for d in range(1, n_mp)]

    x_parts = [window(x_hbm, xw_s, k) for k in range(pn.pairs)]
    c_parts = [window(c_hbm, cw_s, k) for k in range(pn.pairs)]
    vec_parts = [local_copy(pvec_ref, pv_s.at[me])]
    vec_parts += [remote(pvec_ref, pv_s.at[me], {"mp": peer(d)}) for d in range(1, n_mp)]

    def weight(src, dst):
        rows = src.shape[0]

        def shard(m):
            return dst.at[pl.ds(aligned(m * rows, rows), rows), :]

        own = local_copy(src, shard(me))
        across = [remote(src, shard(me), {"mp": ((xi + d) % nx) * 2 + core}) for d in range(1, nx)]
        beside = remote(src, shard(me), {"mp": sibling})
        relay = []
        for d in range(1, nx):
            s = shard(((xi + nx - d) % nx) * 2 + core)
            relay.append(remote(s, s, {"mp": sibling}))
        return own, across, beside, relay

    def spread_weight(src, dst, block):
        rows = src.shape[0]

        def shard(m):
            return dst.at[pl.ds(aligned(m * rows, rows), rows), :]

        own = local_copy(src, shard(me))
        beside = remote(src, shard(me), {"mp": sibling})
        across = [remote(block(src, 0, dp), block(dst, me * rows, dp), {"mp": ((xi + d) % nx) * 2 + core})
                  for d in range(1, nx)]
        along, relay = [], []
        for d in range(1, nx):
            m = ((xi + nx - d) % nx) * 2 + core
            mine = block(dst, m * rows, dp)
            along += [remote(mine, mine, {"dp": (dp + e) % n_dp}) for e in range(1, n_dp)]
            relay.append(remote(shard(m), shard(m), {"mp": sibling}))
        return own, across, beside, relay, along

    def fc1_block(ref, row, q):
        rows, lanes = CS // 2, FF // pn.lane_parts
        return ref.at[pl.ds(aligned(row + q // pn.lane_parts * rows, 16), rows),
                      pl.ds(aligned(q % pn.lane_parts * lanes, TILE), lanes)]

    def fc2_block(ref, row, q):
        rows = pn.FFS // n_dp
        return ref.at[pl.ds(aligned(row + q * rows, 16), rows), :]

    w_parts = [weight(s, d) for s, d in ((wqkv_hbm, wqkv_s), (wproj_hbm, wproj_s))]
    for s, d, block in ((wfc1_hbm, wfc1_s, fc1_block), (wfc2_hbm, wfc2_s, fc2_block)):
        w_parts.append(spread_weight(s, d, block) if pn.spread else weight(s, d))

    def result(src, dst, k):
        lo, hi = pn.out_cuts[k], pn.out_cuts[k + 1]
        there = dst.at[me, :, pl.ds(lo, hi - lo)]

        def part(m):
            return src.at[pl.ds(aligned(m * CS, CS), CS), pl.ds(lo, hi - lo)]

        return [local_copy(part(me), there)] + [remote(part(peer(d)), there, {"mp": peer(d)}) for d in range(1, n_mp)]

    o_parts = [result(ow_s, orecv_s, k) for k in range(pn.pairs)]
    i_parts = [result(iw_s, irecv_s, k) for k in range(pn.pairs)]

    def fill_fc2(dst, slot, j, add):
        put_rows(dst, slot, 0, add, dfc2_ref[pl.ds(aligned(j * pn.FFS, pn.FFS), pn.FFS), :])

    def fill_fc1(dst, slot, j, add):
        at = pl.ds(aligned(j * CS, CS), CS)
        for i in range(FF // C):
            put_rows(dst, slot, i * CS, add, dfc1_ref[at, i * C:(i + 1) * C])
        put_rows(dst, slot, FF // C * CS, add, dproj_ref[at, :])

    def fill_qkv(dst, slot, j, add):
        at = pl.ds(aligned(j * CS, CS), CS)
        for i in range(3 * C // TILE):
            put_rows(dst, slot, i * CS, add, dqkv_ref[at, i * TILE:(i + 1) * TILE])

    def put_rows(dst, slot, lo, add, v):
        at = slice(lo, lo + v.shape[0])
        v = add(at, v).astype(BF16)
        if slot is None:
            dst[at, :] = v
        else:
            dst[slot, at, :] = v

    groups = [Group(pn, r, None, f) for r, f in zip(group_refs, (fill_fc2, fill_fc1, fill_qkv))]
    for g in groups:
        g.build(remote, xi, core, sibling, dp)
    g_fc2, g_fc1, g_qkv = groups
    hop1 = [remote(pack_s.at[peer(d)], hop1_s.at[me], {"mp": peer(d)}) for d in range(1, n_mp)]
    hop2 = [remote(pack2_s, hop2_s.at[dp], {"dp": (dp + e) % n_dp}) for e in range(1, n_dp)]

    def start(copies):
        for c in copies:
            c.start()

    def arrive(copies):
        copies[0].wait()
        for c in copies[1:]:
            c.wait_recv()

    def start_weight(w):
        start(w[1])
        w[0].start()
        w[2].start()

    def spread_along(w):
        if len(w) > 4:
            for a in w[1]:
                a.wait_recv()
            start(w[4])

    def relay_weight(w):
        for a in w[4] if len(w) > 4 else w[1]:
            a.wait_recv()
        start(w[3])

    def have_weight(w):
        own, _, beside, relay = w[:4]
        own.wait()
        beside.wait_recv()
        for r in relay:
            r.wait_recv()

    pvec_ref[...] = jnp.zeros_like(pvec_ref)
    for i, r in enumerate(vec_refs[:-1]):
        pvec_ref[i:i + 1, 0:CS] = r[...].astype(F32)
    for i in range(pn.FFS // CS):
        pvec_ref[len(VECS) + i:len(VECS) + i + 1, 0:CS] = vec_refs[-1][:, i * CS:(i + 1) * CS].astype(F32)

    barrier = pltpu.get_barrier_semaphore()
    for d in range(1, n_mp):
        pl.semaphore_signal(barrier, inc=1, device_id={"mp": peer(d)}, device_id_type=MESH)
    for e in range(1, n_dp):
        pl.semaphore_signal(barrier, inc=1, device_id={"dp": (dp + e) % n_dp}, device_id_type=MESH)
    pl.semaphore_wait(barrier, n_mp - 1 + n_dp - 1)

    start(vec_parts)
    start_weight(w_parts[0])
    start(x_parts[0])
    for w in w_parts[1:]:
        start_weight(w)
    for k in range(1, pn.pairs):
        start(x_parts[k])

    hd = C // HEADS
    factor = hd ** (-0.5)
    head_of = lax.broadcasted_iota(jnp.int32, (1, C), 1) // hd
    for h in range(HEADS):
        pre = post = jnp.zeros((1, C), F32)
        for g in range(HEADS):
            pre = jnp.where(head_of == g, pre_ref[h, g] * factor, pre)
            post = jnp.where(head_of == g, post_ref[g, h], post)
        mrow_s[h:h + 1, :] = pre
        mrow_s[HEADS + h:HEADS + h + 1, :] = post
    mask_s[...] = jnp.full_like(mask_s, MASKED)
    for i in range(n_img):
        keep = keep_ref[pl.ds(me * n_img + i, 1), :]
        mask_s[i:i + 1, 0:PATCHES] = jnp.where(keep > 0, 0.0, MASKED)
    p_s[...] = jnp.zeros_like(p_s)
    for r in (dqkv_ref, dproj_ref, dfc1_ref, dfc2_ref, dvec_ref, dmix_ref):
        r[...] = jnp.zeros_like(r)

    arrive(vec_parts)
    for m in range(n_mp):
        t = jnp.transpose(jnp.concatenate([pv_s[m], jnp.zeros((TILE - 16, TILE), F32)], axis=0))
        for i in range(pn.vrows):
            if i < len(VECS):
                at = pn.off[VECS[i]][0] + m * CS
            else:
                at = pn.off["fb1"][0] + m * pn.FFS + (i - len(VECS)) * CS
            col_s[at:at + CS, :] = jnp.broadcast_to(t[:CS, i:i + 1], (CS, TILE))

    def turn(src, dst):
        rows, cols = src.shape
        for r in range(0, rows, 384):
            for c in range(0, cols, 384):
                dst[c:c + 384, r:r + 384] = jnp.transpose(src[r:r + 384, c:c + 384])

    relay_weight(w_parts[0])
    for w in w_parts[2:]:
        spread_along(w)
    have_weight(w_parts[0])
    turn(wqkv_s, wqkvT_s)

    def col(name, lo=0, hi=None):
        o, w = pn.off[name]
        hi = w if hi is None else hi
        return twice(col_s[o + lo:o + hi, :])

    def lanes_of(b):
        return pl.ds(pl.multiple_of(b * LANES, LANES), LANES)

    lane = lax.broadcasted_iota(jnp.int32, (C, TILE), 1)

    def take(src, b):
        s = b * PATCHES + my_shift
        r = s % TILE
        t = s // TILE
        left = (TILE - r) % TILE
        last = (s + PATCHES - 1) // TILE
        parts = [pltpu.roll(src[:, pl.ds(aligned(i * TILE, TILE), TILE)].astype(F32), left, 1)
                 for i in (t, t + 1, last)]
        lo = jnp.where(lane < TILE - r, parts[0], parts[1])
        hi = jnp.where(lane < TILE - r, parts[1], parts[2])
        hi = jnp.where(lane < PATCHES - TILE, hi, 0.0)
        return jnp.concatenate([lo, hi], axis=1)

    def put(dst, b, v):
        s = b * PATCHES + my_shift
        r = s % TILE
        t = s // TILE
        at = [pl.ds(aligned((t + i) * TILE, TILE), TILE) for i in range(3)]
        lo = pltpu.roll(v[:, :TILE], r, 1)
        hi = pltpu.roll(v[:, TILE:], r, 1)
        old = dst[:, at[0]].astype(F32)
        dst[:, at[0]] = jnp.where(lane < r, old, lo).astype(BF16)
        dst[:, at[1]] = jnp.where(lane < r, lo, hi).astype(BF16)
        dst[:, at[2]] = hi.astype(BF16)

    def norm(x):
        mean = jnp.sum(x, axis=0, keepdims=True) * inv_c
        d = x - mean
        inv = lax.rsqrt(jnp.sum(d * d, axis=0, keepdims=True) * inv_c + EPSILON)
        return d * inv, inv

    def norm_back(u, n, inv, g):
        s = u * g
        m1 = jnp.sum(s, axis=0, keepdims=True) * inv_c
        m2 = jnp.sum(s * n, axis=0, keepdims=True) * inv_c
        return inv * (s - m1 - n * m2)

    def add_vec(name, v, lo=0):
        o = pn.off[name][0] + lo
        dvec_ref[o:o + v.shape[0], :] += fold(v)

    def when_each(b, at, do):
        for k in range(pn.pairs):
            pl.when(b == at(k))(functools.partial(do, k))

    def relay_weights():
        for w in w_parts[1:]:
            relay_weight(w)

    def phase_a(b, _):
        when_each(b, lambda k: 2 * k, lambda k: arrive(x_parts[k]))
        when_each(b, lambda k: k + n_img // 4, lambda k: start(c_parts[k]))
        pl.when(b == n_img - 1)(relay_weights)
        at = lanes_of(b)
        x = take(xw_s, b)
        x_s[:, at] = x.astype(BF16)
        n1, _inv = norm(x)
        first = (n1 * col("g1") + col("b1")).astype(BF16)
        first_s[:, at] = first
        q = (dot(wqkvT_s[0:C, :], first) + col("qb")).astype(BF16)
        qkv_s[0:C, at] = q
        k = dot(wqkvT_s[C:2 * C, :], first).astype(BF16)
        qkv_s[C:2 * C, at] = k
        v = (dot(wqkvT_s[2 * C:3 * C, :], first) + col("vb")).astype(BF16)
        qkv_s[2 * C:3 * C, at] = v
        maskc = twice(lane_column(mask_s[pl.ds(b, 1), :])[:KEYS])
        kr = jnp.transpose(k.astype(F32))[:KEYS]
        for h in range(HEADS):
            kmix = (kr * mrow_s[h:h + 1, :]).astype(BF16)
            logit = dot(kmix, q) + maskc
            top = jnp.max(logit, axis=0, keepdims=True)
            e = jnp.exp(logit - top)
            inv = 1.0 / jnp.sum(e, axis=0, keepdims=True)
            p_s[b, h * LANES:h * LANES + KEYS, :] = (e * inv).astype(BF16)
            vf = v.astype(F32)
            for g in range(HEADS):
                at_g = slice(g * hd, (g + 1) * hd)
                vmixT_s[at_g, h * LANES:(h + 1) * LANES] = (vf[at_g] * post_ref[g, h]).astype(BF16)
        a_s[:, at] = dot(vmixT_s[...], p_s[b]).astype(BF16)
        return 0

    lax.fori_loop(0, n_img, phase_a, 0)

    for w, s, d in zip(w_parts[1:], (wproj_s, wfc1_s, wfc2_s), (wprojT_s, wfc1T_s, wfc2T_s)):
        have_weight(w)
        turn(s, d)

    def phase_b(b, _):
        when_each(b, lambda k: 2 * k, lambda k: arrive(c_parts[k]))
        at = lanes_of(b)
        x = x_s[:, at].astype(F32)
        att = a_s[:, at]
        branch = dot(wprojT_s[...], att) + col("pb")
        middle = x + col("s1") * branch
        n2, inv2 = norm(middle)
        second = (n2 * col("g2") + col("b2")).astype(BF16)
        step = 128
        for r in range(0, FF, step):
            hid = dot(wfc1T_s[r:r + step, :], second) + col("fb1", r, r + step)
            cum, slope = gelu_parts(hid)
            act_s[r:r + step, :] = (hid * cum).astype(BF16)
            slope_s[r:r + step, :] = slope
        act = act_s[0:FF, :]
        mlp = dot(wfc2T_s[...], act) + col("fb2")
        cot = take(cw_s, b)
        put(ow_s, b, middle + col("s2") * mlp)
        when_each(b, lambda k: 2 * k + 1, lambda k: start(o_parts[k]))
        add_vec("s2", cot * mlp)
        g_mlp = (col("s2") * cot).astype(BF16)
        add_vec("fb2", g_mlp.astype(F32))
        for r in range(0, FF, step):
            g_act = dot(wfc2_s[r:r + step, :], g_mlp)
            gh = (g_act * slope_s[r:r + step, :]).astype(BF16)
            gh_s[r:r + step, :] = gh
            add_vec("fb1", gh.astype(F32), r)
            dfc2_ref[r:r + step, :] += dot_nt(act_s[r:r + step, :], g_mlp)
        gh = gh_s[...]
        dfc1_ref[...] += dot_nt(second, gh)
        g_second = dot(wfc1_s[...], gh)
        add_vec("g2", g_second * n2)
        add_vec("b2", g_second)
        g_mid = cot + norm_back(g_second, n2, inv2, col("g2"))
        gm_s[:, at] = g_mid
        add_vec("s1", g_mid * branch)
        g_br = (col("s1") * g_mid).astype(BF16)
        add_vec("pb", g_br.astype(F32))
        dproj_ref[...] += dot_nt(att, g_br)
        a_s[:, at] = dot(wproj_s[...], g_br).astype(BF16)
        return 0

    lax.fori_loop(0, n_img, phase_b, 0)

    def phase_c(b, _):
        at = lanes_of(b)
        da = a_s[:, at]
        q = qkv_s[0:C, at]
        kT = qkv_s[C:2 * C, at].astype(F32)
        vT = qkv_s[2 * C:3 * C, at].astype(F32)
        kr = jnp.transpose(kT)[:KEYS]
        vr = jnp.transpose(vT)[:KEYS]
        gv = jnp.zeros((KEYS, C), F32)
        gk = jnp.zeros((KEYS, C), F32)
        for h in range(HEADS):
            prow = mrow_s[HEADS + h:HEADS + h + 1, :]
            mrow = mrow_s[h:h + 1, :]
            vmix = (vr * prow).astype(BF16)
            gs = dot(vmix, da)
            pb16 = p_s[b, h * LANES:h * LANES + KEYS, :]
            p = pb16.astype(F32)
            d = jnp.sum(gs * p, axis=0, keepdims=True)
            gt = (p * (gs - d)).astype(BF16)
            gt_s[h * LANES:h * LANES + KEYS, :] = gt
            w = dot_nt(pb16, da)
            gv = gv + prow * w
            dmix_ref[HEADS + h:HEADS + h + 1, :] += jnp.sum(w * vr, axis=0, keepdims=True)
            xk = dot_nt(gt, q)
            gk = gk + mrow * xk
            dmix_ref[h:h + 1, :] += jnp.sum(xk * kr, axis=0, keepdims=True)
            for g in range(HEADS):
                at_g = slice(g * hd, (g + 1) * hd)
                vmixT_s[at_g, h * LANES:(h + 1) * LANES] = (kT[at_g] * (pre_ref[h, g] * factor)).astype(BF16)
        gq = dot(vmixT_s[...], gt_s[...]).astype(BF16)
        pad = jnp.zeros((LANES - KEYS, C), F32)
        gkT = jnp.transpose(jnp.concatenate([gk, pad], axis=0)).astype(BF16)
        gvT = jnp.transpose(jnp.concatenate([gv, pad], axis=0)).astype(BF16)
        add_vec("qb", gq.astype(F32))
        add_vec("vb", gvT.astype(F32))
        gj = jnp.concatenate([gq, gkT, gvT], axis=0)
        qkv_s[:, at] = gj
        dqkv_ref[...] += dot_nt(first_s[:, at], gj)
        for step, do in ((1, g_fc2.over_x), (2, g_fc1.over_x), (4, g_fc2.over_dp), (5, g_fc1.over_dp),
                         (6, g_fc2.to_all)):
            pl.when(b == step * n_img // 8)(do)
        return 0

    lent = [c for w in w_parts[1:] for c in w[3] + (w[4] if len(w) > 4 else [])]
    for c in lent:
        c.wait_send()
    g_fc2.over_cores()
    g_fc1.over_cores()
    gt_s[...] = jnp.zeros_like(gt_s)
    lax.fori_loop(0, n_img, phase_c, 0)
    g_qkv.over_cores()

    def phase_d(b, _):
        at = lanes_of(b)
        g_first = dot(wqkv_s[...], qkv_s[:, at])
        n1, inv1 = norm(x_s[:, at].astype(F32))
        add_vec("g1", g_first * n1)
        add_vec("b1", g_first)
        put(iw_s, b, gm_s[:, at] + norm_back(g_first, n1, inv1, col("g1")))
        when_each(b, lambda k: 2 * k + 1, lambda k: start(i_parts[k]))
        for step, do in ((1, g_qkv.over_x), (3, g_fc1.to_all), (6, g_qkv.over_dp)):
            pl.when(b == step * n_img // 8)(do)
        return 0

    lax.fori_loop(0, n_img, phase_d, 0)

    sums = []
    for m in range(n_mp):
        for i in range(pn.vrows):
            if i < len(VECS):
                o = pn.off[VECS[i]][0] + m * CS
            else:
                o = pn.off["fb1"][0] + m * pn.FFS + (i - len(VECS)) * CS
            block = jnp.concatenate([dvec_ref[o:o + CS, :], jnp.zeros((TILE - CS, TILE), F32)], axis=0)
            pack_s[m, i:i + 1, :] = jnp.sum(jnp.transpose(block), axis=0, keepdims=True)
        pack_s[m, pn.vrows:16, :] = jnp.zeros((16 - pn.vrows, TILE), F32)
    lane_of = lax.broadcasted_iota(jnp.int32, (2 * HEADS, TILE), 1)
    heads = lax.broadcasted_iota(jnp.int32, (2 * HEADS, C), 1) // hd
    dmix = dmix_ref[...]
    mix = jnp.zeros((2 * HEADS, TILE), F32)
    for g in range(HEADS):
        mix = jnp.where(lane_of == g, jnp.sum(jnp.where(heads == g, dmix, 0.0), axis=1, keepdims=True), mix)
    for m in range(n_mp):
        pack_s[m, 16:32, :] = mix
    start(hop1)
    hop1_s[me] = pack_s[me]
    for c in hop1:
        c.wait_recv()
    both = hop1_s[0]
    for m in range(1, n_mp):
        both = both + hop1_s[m]
    pack2_s[...] = both
    start(hop2)
    hop2_s[dp] = both
    g_qkv.to_all()
    for c in hop2:
        c.wait_recv()
    both = hop2_s[0]
    for e in range(1, n_dp):
        both = both + hop2_s[e]
    small_ref[...] = both

    for k in range(pn.pairs):
        arrive(o_parts[k])
        arrive(i_parts[k])
    for g in groups:
        g.finish()
    lent = [id(c) for c in lent]
    for c in sent:
        if id(c) not in lent:
            c.wait_send()


def layer_call(pn, x, cot, ws, keep, pre, post, vecs):
    C, CS, FF, n_img, n_mp, n_dp = pn.C, pn.CS, pn.FF, pn.n_img, pn.n_mp, pn.n_dp
    S = jax.ShapeDtypeStruct
    T = n_img * LANES
    outs = (S((n_mp, CS, pn.width), BF16), S((n_mp, CS, pn.width), BF16), S((32, TILE), F32))
    outs += tuple(S(g, BF16) for g in pn.groups)
    V = pltpu.VMEM
    remotes = (4 * pn.pairs + 2) * (n_mp - 1) + 4 * (2 * (pn.nx - 1) + 1)
    remotes += 3 * (2 * pn.nx - 1 + 2 * (n_dp - 1)) + n_dp - 1
    if pn.spread:
        remotes += 2 * (pn.nx - 1) * (n_dp - 1)
    locals_ = 4 * pn.pairs + 1 + 4
    scratch = [V((C, pn.wide), BF16), V((C, pn.wide), BF16), V((n_mp, 16, TILE), F32),
               V((C, 3 * C), BF16), V((C, C), BF16), V((C, FF), BF16), V((FF, C), BF16),
               V((3 * C, C), BF16), V((C, C), BF16), V((FF, C), BF16), V((C, FF), BF16),
               V((C, T), BF16), V((C, T), BF16), V((3 * C, T), BF16), V((n_img, HEADS * LANES, LANES), BF16),
               V((C, T), BF16), V((C, T), F32), V((HEADS * LANES, LANES), BF16), V((C, HEADS * LANES), BF16),
               V((pn.total, TILE), F32), V((FF, LANES), F32), V((FF, LANES), BF16),
               V((2 * HEADS, C), F32), V((max(n_img, 8), LANES), F32),
               V((C, 3 * C), F32), V((C, C), F32), V((C, FF), F32), V((FF, C), F32), V((pn.total, TILE), F32),
               V((2 * HEADS, C), F32),
               V((n_mp, 32, TILE), F32), V((n_mp, 32, TILE), F32), V((32, TILE), F32), V((n_dp, 32, TILE), F32),
               V((16, TILE), F32)]
    for rows, lanes in pn.groups:
        scratch += pn.group_scratch(rows, lanes)
    scratch += [pltpu.SemaphoreType.DMA((remotes,)), pltpu.SemaphoreType.DMA((remotes,)),
                pltpu.SemaphoreType.DMA((locals_,))]
    vm = pl.BlockSpec(memory_space=pltpu.VMEM)
    sm = pl.BlockSpec(memory_space=pltpu.SMEM)
    hbm = pl.BlockSpec(memory_space=pl.ANY)
    return pl.pallas_call(
        functools.partial(layer_kernel, pn),
        out_shape=outs,
        in_specs=[hbm] * 6 + [vm] + [sm] * 2 + [vm] * len(vecs),
        out_specs=[vm] * len(outs),
        scratch_shapes=scratch,
        compiler_params=pltpu.CompilerParams(vmem_limit_bytes=VMEM_BYTES, collective_id=0, has_side_effects=True),
        name="layer",
    )(x, cot, *ws, keep, pre, post, *vecs)


def finish_kernel(pn, orecv, irecv, small, r_fc2, r_fc1, r_qkv, out_ref, ig_ref, gqkv_ref, gproj_ref, gfc1_ref,
                  gfc2_ref, pre_ref, post_ref, fb1_ref, *vec_refs):
    C, CS, FF = pn.C, pn.CS, pn.FF
    lane_out = lax.broadcasted_iota(jnp.int32, (CS, TILE), 1)

    def join(recv, dst):
        for j in range(pn.cols // TILE):
            parts = [(m, j - pn.bases[m] // TILE) for m in range(pn.n_mp)
                     if pn.bases[m] <= j * TILE and j * TILE < pn.bases[m] + pn.shifts[m] + pn.tok]
            v = None
            for m, l in parts:
                w = recv[m, :, l * TILE:(l + 1) * TILE]
                v = w if v is None else jnp.where(lane_out < pn.shifts[m], v.astype(F32), w.astype(F32)).astype(BF16)
            dst[:, j * TILE:(j + 1) * TILE] = v

    join(orecv, out_ref)
    join(irecv, ig_ref)
    gfc2_ref[...] = r_fc2[0:pn.FFS, :].astype(F32)
    for i in range(FF // C):
        gfc1_ref[:, i * C:(i + 1) * C] = r_fc1[i * CS:(i + 1) * CS, :].astype(F32)
    gproj_ref[...] = r_fc1[FF // C * CS:(FF // C + 1) * CS, :].astype(F32)
    for i in range(3 * C // TILE):
        gqkv_ref[:, i * TILE:(i + 1) * TILE] = r_qkv[i * CS:(i + 1) * CS, :].astype(F32)
    pre_ref[...] = small[16:16 + HEADS, 0:HEADS] * (C // HEADS) ** (-0.5)
    pad = jnp.zeros((TILE - HEADS, TILE), F32)
    post_ref[...] = jnp.transpose(jnp.concatenate([small[16 + HEADS:16 + 2 * HEADS, :], pad], axis=0))[0:HEADS, 0:HEADS]
    for i, r in enumerate(vec_refs):
        r[...] = small[i:i + 1, 0:CS]
    for i in range(pn.FFS // CS):
        fb1_ref[:, i * CS:(i + 1) * CS] = small[len(VECS) + i:len(VECS) + i + 1, 0:CS]


def finish_call(pn, parts):
    S = jax.ShapeDtypeStruct
    C, CS = pn.C, pn.CS
    outs = (S((CS, pn.cols), BF16), S((CS, pn.cols), BF16), S((CS, 3 * C), F32), S((CS, C), F32), S((CS, pn.FF), F32),
            S((pn.FFS, C), F32), S((HEADS, HEADS), F32), S((HEADS, HEADS), F32), S((1, pn.FFS), F32))
    outs += (S((1, CS), F32),) * len(VECS)
    vm = pl.BlockSpec(memory_space=pltpu.VMEM)
    return pl.pallas_call(
        functools.partial(finish_kernel, pn),
        out_shape=outs,
        in_specs=[vm] * len(parts),
        out_specs=[vm] * len(outs),
        compiler_params=pltpu.CompilerParams(vmem_limit_bytes=32 * 2 ** 20),
        name="finish",
    )(*parts)


def local(patches, keep_mask, ln1_gain, ln1_bias, w_qkv, q_bias, v_bias, mix_pre, mix_post, w_proj, proj_bias,
          gamma1, ln2_gain, ln2_bias, w_fc1, fc1_bias, w_fc2, fc2_bias, gamma2, cotangent):
    n_mp, n_dp = lax.axis_size("mp"), lax.axis_size("dp")
    pn = Plan(n_dp, n_mp, patches.shape, keep_mask.shape, w_fc2.shape)
    vecs = (ln1_gain, ln1_bias, q_bias, v_bias, proj_bias, gamma1, ln2_gain, ln2_bias, fc2_bias, gamma2, fc1_bias)
    parts = layer_call(pn, patches, cotangent, (w_qkv, w_proj, w_fc1, w_fc2), keep_mask, mix_pre, mix_post,
                       [v.reshape(1, -1) for v in vecs])
    out, ig, gqkv, gproj, gfc1, gfc2, pre_total, post_total, gfb1, *gs = finish_call(pn, parts)
    gfb1 = gfb1.reshape(-1)
    gs = [g.reshape(-1) for g in gs]
    return (out, ig, gs[0], gs[1], gqkv, gs[2], gs[3], pre_total, post_total, gproj, gs[4], gs[5],
            gs[6], gs[7], gfc1, gfb1, gfc2, gs[8], gs[9])


def solution(mesh):
    m, mn = P("mp"), P("mp", None)
    big = P("mp", "dp")
    in_specs = (big, P("dp", None), m, m, mn, m, m, P(), P(), mn, m, m, m, m, mn, m, mn, m, m, big)
    out_specs = (big, big, m, m, mn, m, m, P(), P(), mn, m, m, m, m, mn, m, mn, m, m)
    return jax.shard_map(local, mesh=mesh, in_specs=in_specs, out_specs=out_specs, check_vma=False)
```

```python
import functools
import jax
import jax.numpy as jnp
from jax import lax
from jax.experimental import pallas as pl
from jax.experimental.pallas import tpu as pltpu
from jax.sharding import PartitionSpec as P

PATCHES = 196
HEADS = 8
EPSILON = 1e-06
MASKED = -1000000000.0
F32 = jnp.float32
BF16 = jnp.bfloat16
VMEM_BYTES = 63 * 2 ** 20
LANES = 256
KEYS = 208


def dot(a, b):
    return lax.dot_general(a, b, (((1,), (0,)), ((), ())), preferred_element_type=F32)


def dot_nt(a, b):
    return lax.dot_general(a, b, (((1,), (1,)), ((), ())), preferred_element_type=F32)


def dot_tn(a, b):
    return lax.dot_general(a, b, (((0,), (0,)), ((), ())), preferred_element_type=F32)


def twice(col):
    return jnp.concatenate([col, col], axis=1)


def fold(v):
    r = v[:, :128]
    for i in range(128, v.shape[1], 128):
        r = r + v[:, i:i + 128]
    return r


def lane_column(row):
    return jnp.transpose(jnp.broadcast_to(row, (128, row.shape[1])))


def gelu_parts(h):
    e = jnp.exp(-0.5 * h * h)
    cum = 0.5 * (1.0 + lax.erf(h * 0.7071067811865476))
    return cum, cum + h * (e * 0.3989422804014327)


MESH = pl.DeviceIdType.MESH
TILE = 128
VECS = ("g1", "b1", "qb", "vb", "pb", "s1", "g2", "b2", "fb2", "s2")


class Plan:
    def __init__(self, n_dp, n_mp, patches, keep_mask, w_fc2):
        self.n_dp = n_dp
        self.n_mp = n_mp
        self.nx = n_mp // 2
        self.CS, self.cols = patches
        self.C = self.CS * n_mp
        self.FFS = w_fc2[0]
        self.FF = self.FFS * n_mp
        self.n_img = keep_mask[0] // n_mp
        self.tok = self.n_img * PATCHES
        starts = [self.tok * m for m in range(n_mp)]
        self.bases = [s // TILE * TILE for s in starts]
        self.shifts = [s % TILE for s in starts]
        top = max(self.shifts)
        self.width = -(-(self.tok + top) // TILE) * TILE
        self.wide = self.width + TILE
        self.pairs = self.n_img // 2
        self.in_cuts = [0] + [-(-(2 * PATCHES * (k + 1) + top) // TILE) * TILE for k in range(self.pairs)]
        self.out_cuts = [0] + [2 * PATCHES * (k + 1) // TILE * TILE for k in range(self.pairs - 1)] + [self.width]
        self.vrows = len(VECS) + self.FFS // self.CS
        self.off = {}
        at = 0
        for name in VECS + ("fb1",):
            w = self.FF if name == "fb1" else self.C
            self.off[name] = (at, w)
            at += w
        self.total = at
        self.n_y, self.n_z = 2, n_dp // 2
        half = self.CS // 2
        self.groups = ((self.pieces(self.FFS // 2), self.C), (self.pieces(half * (self.FF // self.C + 1)), self.C),
                       (self.pieces(half * (3 * self.C // TILE)), TILE))
        self.lane_parts = n_dp // 2
        self.spread = (self.FFS % (16 * n_dp) == 0 and self.CS % 32 == 0 and n_dp % 2 == 0
                       and self.FF % (TILE * self.lane_parts) == 0)

    def pieces(self, rows):
        return -(-rows // (16 * self.n_z)) * 16 * self.n_z

    def group_scratch(self, half, lanes):
        V = pltpu.VMEM
        nx, more = self.nx, max(self.nx - 1, 1)
        return [V((2 * nx * half if lanes == TILE else 16, lanes), BF16), V((nx, 2 * half, lanes), BF16),
                V((nx, half, lanes), BF16), V((nx, half, lanes), BF16), V((more, half, lanes), BF16),
                V((more, half, lanes), BF16), V((half, lanes), BF16), V((self.n_z, half // self.n_z, lanes), BF16),
                V((half, lanes), BF16)]


class Group:
    def __init__(self, pn, refs, blocks):
        self.pn, self.blocks = pn, blocks
        self.s1, self.r1, self.s2, self.r2, self.s3, self.r3, self.s4, self.r4, self.s5, self.out = refs
        self.half = self.s4.shape[0]
        self.piece = self.half // pn.n_z

    def build(self, remote, local_copy, xi, core, sibling, dp):
        pn, half = self.pn, self.half
        self.xi, self.core = xi, core
        self.y, self.z = dp % 2, dp // 2
        other = dp + 1 - 2 * self.y
        self.c1 = [remote(self.s1.at[pl.ds(2 * half * x, 2 * half), :], self.r1.at[x], {"mp": sibling})
                   for x in range(pn.nx)]
        self.c2 = [remote(self.s2.at[x], self.r2.at[x], {"dp": other}) for x in range(pn.nx)]
        self.c3 = [remote(self.s3.at[d - 1], self.r3.at[d - 1], {"mp": ((xi + d) % pn.nx) * 2 + core})
                   for d in range(1, pn.nx)]
        self.c4, self.c5 = [], []
        own = self.s5.at[self.rows(self.z)]
        for e in range(1, pn.n_z):
            to = (self.z + e) % pn.n_z
            self.c4.append(remote(self.s4.at[self.rows(to)], self.r4.at[e], {"dp": 2 * to + self.y}))
            self.c5.append(remote(own, own, {"dp": 2 * to + self.y}))
        there = self.out.at[pl.ds(pl.multiple_of(self.y * half, 16), half), :]
        self.c6 = [local_copy(self.s5, there), remote(self.s5, there, {"dp": other})]

    def rows(self, q):
        return pl.ds(pl.multiple_of(q * self.piece, 16), self.piece)

    def fill(self, dst, j, y, add):
        lo = 0
        for v in self.blocks(j, y):
            at = slice(lo, lo + v.shape[0])
            dst[at, :] = add(at, v).astype(BF16)
            lo = at.stop

    def over_cores(self):
        half = self.half
        for x in range(self.pn.nx):
            for y in range(2):
                self.fill(self.s1.at[pl.ds((2 * x + y) * half, half), :], 2 * x + 1 - self.core, y, lambda at, v: v)
            self.c1[x].start()

    def from_core(self, x, y, at):
        upper = slice(at.start + self.half, at.stop + self.half)
        return jnp.where(y == 0, self.r1[x, at, :].astype(F32), self.r1[x, upper, :].astype(F32))

    def over_y(self):
        y = 1 - self.y
        for x in range(self.pn.nx):
            self.c1[x].wait_recv()
            self.fill(self.s2.at[x], 2 * x + self.core, y, lambda at, v: v + self.from_core(x, y, at))
            self.c2[x].start()

    def over_x(self):
        for c in self.c2:
            c.wait_recv()
        for d in range(1, self.pn.nx):
            x = (self.xi + d) % self.pn.nx
            self.fill(self.s3.at[d - 1], 2 * x + self.core, self.y,
                      lambda at, v: v + self.from_core(x, self.y, at) + self.r2[x, at, :].astype(F32))
            self.c3[d - 1].start()

    def over_z(self):
        for c in self.c3:
            c.wait_recv()

        def add(at, v):
            v = v + self.from_core(self.xi, self.y, at) + self.r2[self.xi, at, :].astype(F32)
            for d in range(1, self.pn.nx):
                v = v + self.r3[d - 1, at, :].astype(F32)
            return v

        self.fill(self.s4, 2 * self.xi + self.core, self.y, add)
        for c in self.c4:
            c.start()

    def back_z(self):
        v = self.s4[self.rows(self.z), :].astype(F32)
        for e in range(1, self.pn.n_z):
            self.c4[e - 1].wait_recv()
            v = v + self.r4[e].astype(F32)
        self.s5[self.rows(self.z), :] = v.astype(BF16)
        for c in self.c5:
            c.start()

    def back_y(self):
        for c in self.c5:
            c.wait_recv()
        for c in self.c6:
            c.start()

    def finish(self):
        self.c6[0].wait()
        self.c6[1].wait_recv()


def layer_kernel(pn, x_hbm, c_hbm, wqkv_hbm, wproj_hbm, wfc1_hbm, wfc2_hbm, keep_ref, pre_ref, post_ref, *rest):
    vec_refs, rest = rest[:len(VECS) + 1], rest[len(VECS) + 1:]
    layer_body(pn, x_hbm, c_hbm, wqkv_hbm, wproj_hbm, wfc1_hbm, wfc2_hbm, keep_ref, pre_ref, post_ref, vec_refs,
               *rest)


def layer_body(pn, x_hbm, c_hbm, wqkv_hbm, wproj_hbm, wfc1_hbm, wfc2_hbm, keep_ref, pre_ref, post_ref, vec_refs,
                 orecv_s, irecv_s, small_ref, r4_fc2, r4_fc1, r4_qkv,
                 xw_s, cw_s, pv_s, wqkv_s, wproj_s, wfc1_s, wfc2_s, wqkvT_s, wprojT_s, wfc1T_s, wfc2T_s,
                 x_s, first_s, qkv_s, p_s, a_s, gm_s, col_s, act_s, slope_s, gh_s, two_s, mrow_s, mask_s,
                 dqkv_ref, dproj_ref, dfc1_ref, dfc2_ref, dvec_ref, dmix_ref,
                 pack_s, hop1_s, pack2_s, hop2_s, pvec_ref, *rest):
    group_refs = [list(rest[9 * i:9 * i + 9]) + [r] for i, r in enumerate((r4_fc2, r4_fc1, r4_qkv))]
    group_refs[0][0], group_refs[1][0] = wfc1T_s, wfc2_s
    ssem, rsem, lsem = rest[27:]
    ow_s, iw_s = xw_s, cw_s
    C, CS, FF, n_img, n_mp, nx = pn.C, pn.CS, pn.FF, pn.n_img, pn.n_mp, pn.nx
    inv_c = 1.0 / C
    n_dp = pn.n_dp
    dp = lax.axis_index("dp")
    me = lax.axis_index("mp")
    core = me % 2
    xi = me // 2
    sibling = me + 1 - 2 * core
    my_shift = (pn.tok * me) % TILE

    count = [0, 0]
    sent = []

    def remote(src, dst, dev):
        i = count[0]
        count[0] += 1
        copy = pltpu.make_async_remote_copy(src_ref=src, dst_ref=dst, send_sem=ssem.at[i], recv_sem=rsem.at[i],
                                            device_id=dev, device_id_type=MESH)
        sent.append(copy)
        return copy

    def local_copy(src, dst):
        i = count[1]
        count[1] += 1
        return pltpu.make_async_copy(src, dst, lsem.at[i])

    def peer(d):
        return (me + d) % n_mp

    def aligned(v, n):
        return pl.multiple_of(v, n)

    def window(src, dst, k):
        lo, hi = pn.in_cuts[k], pn.in_cuts[k + 1]
        mine = dst.at[pl.ds(aligned(me * CS, CS), CS), pl.ds(lo, hi - lo)]

        def part(m):
            base = (pn.tok * m) // TILE * TILE
            return src.at[:, pl.ds(aligned(base + lo, TILE), hi - lo)]

        return [local_copy(part(me), mine)] + [remote(part(peer(d)), mine, {"mp": peer(d)}) for d in range(1, n_mp)]

    x_parts = [window(x_hbm, xw_s, k) for k in range(pn.pairs)]
    c_parts = [window(c_hbm, cw_s, k) for k in range(pn.pairs)]
    vec_parts = [local_copy(pvec_ref, pv_s.at[me])]
    vec_parts += [remote(pvec_ref, pv_s.at[me], {"mp": peer(d)}) for d in range(1, n_mp)]

    def weight(src, dst):
        rows = src.shape[0]

        def shard(m):
            return dst.at[pl.ds(aligned(m * rows, rows), rows), :]

        own = local_copy(src, shard(me))
        across = [remote(src, shard(me), {"mp": ((xi + d) % nx) * 2 + core}) for d in range(1, nx)]
        beside = remote(src, shard(me), {"mp": sibling})
        relay = []
        for d in range(1, nx):
            s = shard(((xi + nx - d) % nx) * 2 + core)
            relay.append(remote(s, s, {"mp": sibling}))
        return own, across, beside, relay

    def spread_weight(src, dst, block):
        rows = src.shape[0]

        def shard(m):
            return dst.at[pl.ds(aligned(m * rows, rows), rows), :]

        own = local_copy(src, shard(me))
        beside = remote(src, shard(me), {"mp": sibling})
        across = [remote(block(src, 0, dp), block(dst, me * rows, dp), {"mp": ((xi + d) % nx) * 2 + core})
                  for d in range(1, nx)]
        along, relay = [], []
        for d in range(1, nx):
            m = ((xi + nx - d) % nx) * 2 + core
            mine = block(dst, m * rows, dp)
            along += [remote(mine, mine, {"dp": (dp + e) % n_dp}) for e in range(1, n_dp)]
            relay.append(remote(shard(m), shard(m), {"mp": sibling}))
        return own, across, beside, relay, along

    def fc1_block(ref, row, q):
        rows, lanes = CS // 2, FF // pn.lane_parts
        return ref.at[pl.ds(aligned(row + q // pn.lane_parts * rows, 16), rows),
                      pl.ds(aligned(q % pn.lane_parts * lanes, TILE), lanes)]

    def fc2_block(ref, row, q):
        rows = pn.FFS // n_dp
        return ref.at[pl.ds(aligned(row + q * rows, 16), rows), :]

    w_parts = [weight(s, d) for s, d in ((wqkv_hbm, wqkv_s), (wproj_hbm, wproj_s))]
    for s, d, block in ((wfc1_hbm, wfc1_s, fc1_block), (wfc2_hbm, wfc2_s, fc2_block)):
        w_parts.append(spread_weight(s, d, block) if pn.spread else weight(s, d))

    def result(src, dst, k):
        lo, hi = pn.out_cuts[k], pn.out_cuts[k + 1]
        there = dst.at[me, :, pl.ds(lo, hi - lo)]

        def part(m):
            return src.at[pl.ds(aligned(m * CS, CS), CS), pl.ds(lo, hi - lo)]

        return [local_copy(part(me), there)] + [remote(part(peer(d)), there, {"mp": peer(d)}) for d in range(1, n_mp)]

    o_parts = [result(ow_s, orecv_s, k) for k in range(pn.pairs)]
    i_parts = [result(iw_s, irecv_s, k) for k in range(pn.pairs)]

    def rows_of(j, y, rows):
        return pl.ds(aligned(j * rows + y * (rows // 2), 8), rows // 2)

    def fc2_blocks(j, y):
        return [dfc2_ref[rows_of(j, y, pn.FFS), :]]

    def fc1_blocks(j, y):
        at = rows_of(j, y, CS)
        return [dfc1_ref[at, i * C:(i + 1) * C] for i in range(FF // C)] + [dproj_ref[at, :]]

    def qkv_blocks(j, y):
        at = rows_of(j, y, CS)
        return [dqkv_ref[at, i * TILE:(i + 1) * TILE] for i in range(3 * C // TILE)]

    groups = [Group(pn, r, f) for r, f in zip(group_refs, (fc2_blocks, fc1_blocks, qkv_blocks))]
    for g in groups:
        g.build(remote, local_copy, xi, core, sibling, dp)
    g_fc2, g_fc1, g_qkv = groups
    hop1 = [remote(pack_s.at[peer(d)], hop1_s.at[me], {"mp": peer(d)}) for d in range(1, n_mp)]
    hop2 = [remote(pack2_s, hop2_s.at[dp], {"dp": (dp + e) % n_dp}) for e in range(1, n_dp)]

    def start(copies):
        for c in copies:
            c.start()

    def arrive(copies):
        copies[0].wait()
        for c in copies[1:]:
            c.wait_recv()

    def start_weight(w):
        start(w[1])
        w[0].start()
        w[2].start()

    def spread_along(w):
        if len(w) > 4:
            for a in w[1]:
                a.wait_recv()
            start(w[4])

    def relay_weight(w):
        for a in w[4] if len(w) > 4 else w[1]:
            a.wait_recv()
        start(w[3])

    def have_weight(w):
        own, _, beside, relay = w[:4]
        own.wait()
        beside.wait_recv()
        for r in relay:
            r.wait_recv()

    pvec_ref[...] = jnp.zeros_like(pvec_ref)
    for i, r in enumerate(vec_refs[:-1]):
        pvec_ref[i:i + 1, 0:CS] = r[...].astype(F32)
    for i in range(pn.FFS // CS):
        pvec_ref[len(VECS) + i:len(VECS) + i + 1, 0:CS] = vec_refs[-1][:, i * CS:(i + 1) * CS].astype(F32)

    barrier = pltpu.get_barrier_semaphore()
    for d in range(1, n_mp):
        pl.semaphore_signal(barrier, inc=1, device_id={"mp": peer(d)}, device_id_type=MESH)
    for e in range(1, n_dp):
        pl.semaphore_signal(barrier, inc=1, device_id={"dp": (dp + e) % n_dp}, device_id_type=MESH)
    pl.semaphore_wait(barrier, n_mp - 1 + n_dp - 1)

    start(vec_parts)
    start_weight(w_parts[0])
    start(x_parts[0])
    for w in w_parts[1:]:
        start_weight(w)
    for k in range(1, pn.pairs):
        start(x_parts[k])

    hd = C // HEADS
    factor = hd ** (-0.5)
    head_of = lax.broadcasted_iota(jnp.int32, (1, C), 1) // hd
    for h in range(HEADS):
        pre = post = jnp.zeros((1, C), F32)
        for g in range(HEADS):
            pre = jnp.where(head_of == g, pre_ref[h, g] * factor, pre)
            post = jnp.where(head_of == g, post_ref[g, h], post)
        mrow_s[h:h + 1, :] = pre
        mrow_s[HEADS + h:HEADS + h + 1, :] = post
    mask_s[...] = jnp.full_like(mask_s, MASKED)
    for i in range(n_img):
        keep = keep_ref[pl.ds(me * n_img + i, 1), :]
        mask_s[i:i + 1, 0:PATCHES] = jnp.where(keep > 0, 0.0, MASKED)
    for r in (dqkv_ref, dproj_ref, dfc1_ref, dfc2_ref, dvec_ref, dmix_ref):
        r[...] = jnp.zeros_like(r)

    arrive(vec_parts)
    for m in range(n_mp):
        t = jnp.transpose(jnp.concatenate([pv_s[m], jnp.zeros((TILE - 16, TILE), F32)], axis=0))
        for i in range(pn.vrows):
            if i < len(VECS):
                at = pn.off[VECS[i]][0] + m * CS
            else:
                at = pn.off["fb1"][0] + m * pn.FFS + (i - len(VECS)) * CS
            col_s[at:at + CS, :] = jnp.broadcast_to(t[:CS, i:i + 1], (CS, TILE)).astype(BF16)

    def turn(src, dst):
        rows, cols = src.shape
        for r in range(0, rows, 384):
            for c in range(0, cols, 384):
                dst[c:c + 384, r:r + 384] = jnp.transpose(src[r:r + 384, c:c + 384])

    relay_weight(w_parts[0])
    for w in w_parts[2:]:
        spread_along(w)
    have_weight(w_parts[0])
    turn(wqkv_s, wqkvT_s)

    def col(name, lo=0, hi=None, width=2 * LANES):
        o, w = pn.off[name]
        hi = w if hi is None else hi
        v = twice(col_s[o + lo:o + hi, :].astype(F32))
        return v if width == LANES else twice(v)

    def lanes_of(b):
        return pl.ds(pl.multiple_of(b * LANES, LANES), LANES)

    def lanes_of_pair(k):
        return pl.ds(pl.multiple_of(k * 2 * LANES, 2 * LANES), 2 * LANES)

    def both(f, k):
        return jnp.concatenate([f(2 * k), f(2 * k + 1)], axis=1)

    lane = lax.broadcasted_iota(jnp.int32, (C, TILE), 1)

    def take(src, b):
        s = b * PATCHES + my_shift
        r = s % TILE
        t = s // TILE
        left = (TILE - r) % TILE
        last = (s + PATCHES - 1) // TILE
        parts = [pltpu.roll(src[:, pl.ds(aligned(i * TILE, TILE), TILE)].astype(F32), left, 1)
                 for i in (t, t + 1, last)]
        lo = jnp.where(lane < TILE - r, parts[0], parts[1])
        hi = jnp.where(lane < TILE - r, parts[1], parts[2])
        hi = jnp.where(lane < PATCHES - TILE, hi, 0.0)
        return jnp.concatenate([lo, hi], axis=1)

    def put(dst, b, v):
        s = b * PATCHES + my_shift
        r = s % TILE
        t = s // TILE
        at = [pl.ds(aligned((t + i) * TILE, TILE), TILE) for i in range(3)]
        lo = pltpu.roll(v[:, :TILE], r, 1)
        hi = pltpu.roll(v[:, TILE:], r, 1)
        old = dst[:, at[0]].astype(F32)
        dst[:, at[0]] = jnp.where(lane < r, old, lo).astype(BF16)
        dst[:, at[1]] = jnp.where(lane < r, lo, hi).astype(BF16)
        dst[:, at[2]] = hi.astype(BF16)

    def norm(x):
        mean = jnp.sum(x, axis=0, keepdims=True) * inv_c
        d = x - mean
        inv = lax.rsqrt(jnp.sum(d * d, axis=0, keepdims=True) * inv_c + EPSILON)
        return d * inv, inv

    def norm_back(u, n, inv, g):
        s = u * g
        m1 = jnp.sum(s, axis=0, keepdims=True) * inv_c
        m2 = jnp.sum(s * n, axis=0, keepdims=True) * inv_c
        return inv * (s - m1 - n * m2)

    def add_vec(name, v, lo=0):
        o = pn.off[name][0] + lo
        dvec_ref[o:o + v.shape[0], :] += fold(v)

    def when_each(k, do):
        for j in range(pn.pairs):
            pl.when(k == j)(functools.partial(do, j))

    def steps(k, plan):
        for at, do in plan:
            pl.when(k == at * pn.pairs // 4)(do)

    def relay_weights():
        for w in w_parts[1:]:
            relay_weight(w)

    mixed = gh_s.at[0:HEADS * KEYS, 0:C]

    def phase_a(k, _):
        when_each(k, lambda j: arrive(x_parts[j]))
        when_each(k, lambda j: start(c_parts[j]))
        pl.when(k == pn.pairs - 1)(relay_weights)
        for b in (2 * k, 2 * k + 1):
            at = lanes_of(b)
            x = take(xw_s, b)
            x_s[:, at] = x.astype(BF16)
            n1, _inv = norm(x)
            first = (n1 * col("g1", width=LANES) + col("b1", width=LANES)).astype(BF16)
            first_s[:, at] = first
            q = (dot(wqkvT_s[0:C, :], first) + col("qb", width=LANES)).astype(BF16)
            qkv_s[0:C, at] = q
            kT = dot(wqkvT_s[C:2 * C, :], first).astype(BF16)
            qkv_s[C:2 * C, at] = kT
            vT = (dot(wqkvT_s[2 * C:3 * C, :], first) + col("vb", width=LANES)).astype(BF16)
            qkv_s[2 * C:3 * C, at] = vT
            maskc = twice(lane_column(mask_s[pl.ds(b, 1), :])[:KEYS])
            kr = jnp.transpose(kT.astype(F32))[:KEYS]
            vr = jnp.transpose(vT.astype(F32))[:KEYS]
            for h in range(HEADS):
                rows = slice(h * KEYS, (h + 1) * KEYS)
                kmix = (kr * mrow_s[h:h + 1, :]).astype(BF16)
                logit = dot(kmix, q) + maskc
                top = jnp.max(logit, axis=0, keepdims=True)
                e = jnp.exp(logit - top)
                inv = 1.0 / jnp.sum(e, axis=0, keepdims=True)
                p_s[b, rows, :] = (e * inv).astype(BF16)
                mixed[rows, :] = (vr * mrow_s[HEADS + h:HEADS + h + 1, :]).astype(BF16)
            a_s[:, at] = dot_tn(mixed[...], p_s[b]).astype(BF16)
        return 0

    lax.fori_loop(0, pn.pairs, phase_a, 0)

    for w, s, d in zip(w_parts[1:], (wproj_s, wfc1_s, wfc2_s), (wprojT_s, wfc1T_s, wfc2T_s)):
        have_weight(w)
        turn(s, d)

    def phase_b(k, _):
        when_each(k, lambda j: arrive(c_parts[j]))
        at = lanes_of_pair(k)
        x = x_s[:, at].astype(F32)
        att = a_s[:, at]
        branch = dot(wprojT_s[...], att) + col("pb")
        middle = x + col("s1") * branch
        n2, inv2 = norm(middle)
        second = (n2 * col("g2") + col("b2")).astype(BF16)
        step = 256
        for r in range(0, FF, step):
            hid = dot(wfc1T_s[r:r + step, :], second) + col("fb1", r, r + step)
            cum, slope = gelu_parts(hid)
            act_s[r:r + step, :] = (hid * cum).astype(BF16)
            slope_s[r:r + step, :] = slope
        mlp = dot(wfc2T_s[...], act_s[0:FF, :]) + col("fb2")
        cot = both(lambda b: take(cw_s, b), k)
        result = middle + col("s2") * mlp
        put(ow_s, 2 * k, result[:, :LANES])
        put(ow_s, 2 * k + 1, result[:, LANES:])
        when_each(k, lambda j: start(o_parts[j]))
        add_vec("s2", cot * mlp)
        g_mlp = (col("s2") * cot).astype(BF16)
        add_vec("fb2", g_mlp.astype(F32))
        for r in range(0, FF, step):
            g_act = dot(wfc2_s[r:r + step, :], g_mlp)
            gh = (g_act * slope_s[r:r + step, :]).astype(BF16)
            gh_s[r:r + step, :] = gh
            add_vec("fb1", gh.astype(F32), r)
            dfc2_ref[r:r + step, :] += dot_nt(act_s[r:r + step, :], g_mlp)
        gh = gh_s[0:FF, :]
        dfc1_ref[...] += dot_nt(second, gh)
        g_second = dot(wfc1_s[...], gh)
        add_vec("g2", g_second * n2)
        add_vec("b2", g_second)
        g_mid = cot + norm_back(g_second, n2, inv2, col("g2"))
        gm_s[:, at] = g_mid
        add_vec("s1", g_mid * branch)
        g_br = (col("s1") * g_mid).astype(BF16)
        add_vec("pb", g_br.astype(F32))
        dproj_ref[...] += dot_nt(att, g_br)
        a_s[:, at] = dot(wproj_s[...], g_br).astype(BF16)
        return 0

    lax.fori_loop(0, pn.pairs, phase_b, 0)

    gt_s = act_s.at[0:HEADS * KEYS, 0:LANES]
    one_s = slope_s.at[0:HEADS * KEYS, 0:C]
    block = 16

    def unmix(wide, rows, side, out):
        parts = []
        for j in range(0, KEYS, block):
            total = jnp.zeros((block, C), F32)
            vj = side[j:j + block]
            for h in range(HEADS):
                wj = wide[h * KEYS + j:h * KEYS + j + block, :]
                total = total + mrow_s[rows + h:rows + h + 1, :] * wj
                t = wj * vj
                dmix_ref[rows + h] += t[:8] + t[8:]
            parts.append(total)
        parts.append(jnp.zeros((LANES - KEYS, C), F32))
        return jnp.transpose(jnp.concatenate(parts, axis=0)).astype(BF16)

    def phase_c(k, _):
        for b in (2 * k, 2 * k + 1):
            at = lanes_of(b)
            da = a_s[:, at]
            q = qkv_s[0:C, at]
            kr = jnp.transpose(qkv_s[C:2 * C, at].astype(F32))[:KEYS]
            vr = jnp.transpose(qkv_s[2 * C:3 * C, at].astype(F32))[:KEYS]
            for h in range(HEADS):
                rows = slice(h * KEYS, (h + 1) * KEYS)
                vmix = (vr * mrow_s[HEADS + h:HEADS + h + 1, :]).astype(BF16)
                gs = dot(vmix, da)
                p = p_s[b, rows, :].astype(F32)
                d = jnp.sum(gs * p, axis=0, keepdims=True)
                gt_s[rows, :] = (p * (gs - d)).astype(BF16)
                mixed[rows, :] = (kr * mrow_s[h:h + 1, :]).astype(BF16)
            gq = dot_tn(mixed[...], gt_s[...]).astype(BF16)
            one_s[...] = dot_nt(p_s[b], da)
            two_s[...] = dot_nt(gt_s[...], q)
            gv = unmix(one_s, HEADS, vr, None)
            gk = unmix(two_s, 0, kr, None)
            add_vec("qb", gq.astype(F32))
            add_vec("vb", gv.astype(F32))
            qkv_s[0:C, at] = gq
            qkv_s[C:2 * C, at] = gk
            qkv_s[2 * C:3 * C, at] = gv
        at = lanes_of_pair(k)
        dqkv_ref[...] += dot_nt(first_s[:, at], qkv_s[:, at])
        steps(k, ((0, g_fc2.over_x), (0, g_fc1.over_y), (1, g_fc2.over_z), (1, g_fc1.over_x), (2, g_fc2.back_z),
                  (2, g_fc1.over_z), (3, g_fc2.back_y), (3, g_fc1.back_z)))
        return 0

    lent = [c for w in w_parts[1:] for c in w[3] + (w[4] if len(w) > 4 else [])]
    for c in lent:
        c.wait_send()
    g_fc2.over_cores()
    g_fc1.over_cores()
    g_fc2.over_y()
    lax.fori_loop(0, pn.pairs, phase_c, 0)
    g_qkv.over_cores()

    def phase_d(k, _):
        at = lanes_of_pair(k)
        g_first = dot(wqkv_s[...], qkv_s[:, at])
        n1, inv1 = norm(x_s[:, at].astype(F32))
        add_vec("g1", g_first * n1)
        add_vec("b1", g_first)
        grad = gm_s[:, at] + norm_back(g_first, n1, inv1, col("g1"))
        put(iw_s, 2 * k, grad[:, :LANES])
        put(iw_s, 2 * k + 1, grad[:, LANES:])
        when_each(k, lambda j: start(i_parts[j]))
        steps(k, ((0, g_qkv.over_y), (1, g_fc1.back_y), (2, g_qkv.over_x)))
        return 0

    lax.fori_loop(0, pn.pairs, phase_d, 0)

    for m in range(n_mp):
        for i in range(pn.vrows):
            if i < len(VECS):
                o = pn.off[VECS[i]][0] + m * CS
            else:
                o = pn.off["fb1"][0] + m * pn.FFS + (i - len(VECS)) * CS
            block = jnp.concatenate([dvec_ref[o:o + CS, :], jnp.zeros((TILE - CS, TILE), F32)], axis=0)
            pack_s[m, i:i + 1, :] = jnp.sum(jnp.transpose(block), axis=0, keepdims=True)
        pack_s[m, pn.vrows:16, :] = jnp.zeros((16 - pn.vrows, TILE), F32)
    lane_of = lax.broadcasted_iota(jnp.int32, (2 * HEADS, TILE), 1)
    heads = lax.broadcasted_iota(jnp.int32, (2 * HEADS, C), 1) // hd
    dmix = jnp.sum(dmix_ref[...], axis=1)
    mix = jnp.zeros((2 * HEADS, TILE), F32)
    for g in range(HEADS):
        mix = jnp.where(lane_of == g, jnp.sum(jnp.where(heads == g, dmix, 0.0), axis=1, keepdims=True), mix)
    for m in range(n_mp):
        pack_s[m, 16:32, :] = mix
    start(hop1)
    g_qkv.over_z()
    hop1_s[me] = pack_s[me]
    for c in hop1:
        c.wait_recv()
    both_hops = hop1_s[0]
    for m in range(1, n_mp):
        both_hops = both_hops + hop1_s[m]
    pack2_s[...] = both_hops
    start(hop2)
    hop2_s[dp] = both_hops
    g_qkv.back_z()
    for c in hop2:
        c.wait_recv()
    both_hops = hop2_s[0]
    for e in range(1, n_dp):
        both_hops = both_hops + hop2_s[e]
    small_ref[...] = both_hops
    g_qkv.back_y()

    for k in range(pn.pairs):
        arrive(o_parts[k])
        arrive(i_parts[k])
    for g in groups:
        g.finish()
    lent = [id(c) for c in lent]
    for c in sent:
        if id(c) not in lent:
            c.wait_send()


def layer_call(pn, x, cot, ws, keep, pre, post, vecs):
    C, CS, FF, n_img, n_mp, n_dp = pn.C, pn.CS, pn.FF, pn.n_img, pn.n_mp, pn.n_dp
    S = jax.ShapeDtypeStruct
    T = n_img * LANES
    outs = (S((n_mp, CS, pn.width), BF16), S((n_mp, CS, pn.width), BF16), S((32, TILE), F32))
    outs += tuple(S((2 * half, lanes), BF16) for half, lanes in pn.groups)
    V = pltpu.VMEM
    remotes = (4 * pn.pairs + 2) * (n_mp - 1) + 4 * (2 * (pn.nx - 1) + 1)
    remotes += 3 * (3 * pn.nx - 1 + 2 * (pn.n_z - 1) + 1) + n_dp - 1
    if pn.spread:
        remotes += 2 * (pn.nx - 1) * (n_dp - 1)
    locals_ = 4 * pn.pairs + 1 + 4 + 3
    tall = max(FF, HEADS * KEYS)
    scratch = [V((C, pn.wide), BF16), V((C, pn.wide), BF16), V((n_mp, 16, TILE), F32),
               V((C, 3 * C), BF16), V((C, C), BF16), V((C, FF), BF16), V((FF, C), BF16),
               V((3 * C, C), BF16), V((C, C), BF16), V((FF, C), BF16), V((C, FF), BF16),
               V((C, T), BF16), V((C, T), BF16), V((3 * C, T), BF16), V((n_img, HEADS * KEYS, LANES), BF16),
               V((C, T), BF16), V((C, T), F32), V((pn.total, TILE), BF16), V((tall, 2 * LANES), BF16),
               V((tall, 2 * LANES), F32), V((tall, 2 * LANES), BF16), V((HEADS * KEYS, C), F32),
               V((2 * HEADS, C), F32), V((max(n_img, 8), LANES), F32),
               V((C, 3 * C), F32), V((C, C), F32), V((C, FF), F32), V((FF, C), F32), V((pn.total, TILE), F32),
               V((2 * HEADS, 8, C), F32),
               V((n_mp, 32, TILE), F32), V((n_mp, 32, TILE), F32), V((32, TILE), F32), V((n_dp, 32, TILE), F32),
               V((16, TILE), F32)]
    for rows, lanes in pn.groups:
        scratch += pn.group_scratch(rows, lanes)
    scratch += [pltpu.SemaphoreType.DMA((remotes,)), pltpu.SemaphoreType.DMA((remotes,)),
                pltpu.SemaphoreType.DMA((locals_,))]
    vm = pl.BlockSpec(memory_space=pltpu.VMEM)
    sm = pl.BlockSpec(memory_space=pltpu.SMEM)
    hbm = pl.BlockSpec(memory_space=pl.ANY)
    return pl.pallas_call(
        functools.partial(layer_kernel, pn),
        out_shape=outs,
        in_specs=[hbm] * 6 + [vm] + [sm] * 2 + [vm] * len(vecs),
        out_specs=[hbm, hbm, vm, hbm, hbm, hbm],
        scratch_shapes=scratch,
        compiler_params=pltpu.CompilerParams(vmem_limit_bytes=VMEM_BYTES, collective_id=0, has_side_effects=True),
        name="layer",
    )(x, cot, *ws, keep, pre, post, *vecs)


def finish_kernel(pn, orecv, irecv, small, r_fc2, r_fc1, r_qkv, out_hbm, ig_hbm, gqkv_hbm, gproj_hbm, gfc1_hbm,
                  gfc2_hbm, pre_ref, post_ref, fb1_ref, *rest):
    C, CS, FF = pn.C, pn.CS, pn.FF
    vec_refs, rest = rest[:len(VECS)], rest[len(VECS):]
    o_s, i_s, fc2_s, fc1_s, qkv_s, out_s, ig_s, gqkv_s, gproj_s, gfc1_s, gfc2_s, sem = rest
    ins = [pltpu.make_async_copy(a, b, sem.at[i]) for i, (a, b) in enumerate(
        ((orecv, o_s), (irecv, i_s), (r_fc2, fc2_s), (r_fc1, fc1_s), (r_qkv, qkv_s)))]
    outs = [pltpu.make_async_copy(a, b, sem.at[5 + i]) for i, (a, b) in enumerate(
        ((out_s, out_hbm), (ig_s, ig_hbm), (gfc2_s, gfc2_hbm), (gfc1_s, gfc1_hbm), (gproj_s, gproj_hbm),
         (gqkv_s, gqkv_hbm)))]
    for c in ins:
        c.start()
    lane_out = lax.broadcasted_iota(jnp.int32, (CS, TILE), 1)

    def join(recv, dst):
        for j in range(pn.cols // TILE):
            parts = [(m, j - pn.bases[m] // TILE) for m in range(pn.n_mp)
                     if pn.bases[m] <= j * TILE and j * TILE < pn.bases[m] + pn.shifts[m] + pn.tok]
            v = None
            for m, l in parts:
                w = recv[m, :, l * TILE:(l + 1) * TILE]
                v = w if v is None else jnp.where(lane_out < pn.shifts[m], v.astype(F32), w.astype(F32)).astype(BF16)
            dst[:, j * TILE:(j + 1) * TILE] = v

    def unpack(src, dst, at, lanes, rows):
        for y in range(2):
            lo = y * (src.shape[0] // 2) + at * (rows // 2)
            dst[y * (rows // 2):(y + 1) * (rows // 2), lanes] = src[lo:lo + rows // 2, :].astype(F32)

    pre_ref[...] = small[16:16 + HEADS, 0:HEADS] * (C // HEADS) ** (-0.5)
    pad = jnp.zeros((TILE - HEADS, TILE), F32)
    post_ref[...] = jnp.transpose(jnp.concatenate([small[16 + HEADS:16 + 2 * HEADS, :], pad], axis=0))[0:HEADS, 0:HEADS]
    for i, r in enumerate(vec_refs):
        r[...] = small[i:i + 1, 0:CS]
    for i in range(pn.FFS // CS):
        fb1_ref[:, i * CS:(i + 1) * CS] = small[len(VECS) + i:len(VECS) + i + 1, 0:CS]
    ins[0].wait()
    join(o_s, out_s)
    outs[0].start()
    ins[1].wait()
    join(i_s, ig_s)
    outs[1].start()
    ins[2].wait()
    unpack(fc2_s, gfc2_s, 0, slice(0, C), pn.FFS)
    outs[2].start()
    ins[3].wait()
    for i in range(FF // C):
        unpack(fc1_s, gfc1_s, i, slice(i * C, (i + 1) * C), CS)
    outs[3].start()
    unpack(fc1_s, gproj_s, FF // C, slice(0, C), CS)
    outs[4].start()
    ins[4].wait()
    for i in range(3 * C // TILE):
        unpack(qkv_s, gqkv_s, i, slice(i * TILE, (i + 1) * TILE), CS)
    outs[5].start()
    for c in outs:
        c.wait()


def finish_call(pn, parts):
    S = jax.ShapeDtypeStruct
    V = pltpu.VMEM
    C, CS = pn.C, pn.CS
    big = ((CS, pn.cols), (CS, pn.cols), (CS, 3 * C), (CS, C), (CS, pn.FF), (pn.FFS, C))
    outs = tuple(S(b, BF16 if i < 2 else F32) for i, b in enumerate(big))
    outs += (S((HEADS, HEADS), F32), S((HEADS, HEADS), F32), S((1, pn.FFS), F32))
    outs += (S((1, CS), F32),) * len(VECS)
    vm = pl.BlockSpec(memory_space=pltpu.VMEM)
    hbm = pl.BlockSpec(memory_space=pl.ANY)
    scratch = [V(p.shape, BF16) for i, p in enumerate(parts) if i != 2]
    scratch += [V(b, BF16 if i < 2 else F32) for i, b in enumerate(big)]
    return pl.pallas_call(
        functools.partial(finish_kernel, pn),
        out_shape=outs,
        in_specs=[hbm, hbm, vm, hbm, hbm, hbm],
        out_specs=[hbm] * len(big) + [vm] * (len(outs) - len(big)),
        scratch_shapes=scratch + [pltpu.SemaphoreType.DMA((11,))],
        compiler_params=pltpu.CompilerParams(vmem_limit_bytes=VMEM_BYTES),
        name="finish",
    )(*parts)


def local(patches, keep_mask, ln1_gain, ln1_bias, w_qkv, q_bias, v_bias, mix_pre, mix_post, w_proj, proj_bias,
          gamma1, ln2_gain, ln2_bias, w_fc1, fc1_bias, w_fc2, fc2_bias, gamma2, cotangent):
    n_mp, n_dp = lax.axis_size("mp"), lax.axis_size("dp")
    pn = Plan(n_dp, n_mp, patches.shape, keep_mask.shape, w_fc2.shape)
    vecs = (ln1_gain, ln1_bias, q_bias, v_bias, proj_bias, gamma1, ln2_gain, ln2_bias, fc2_bias, gamma2, fc1_bias)
    parts = layer_call(pn, patches, cotangent, (w_qkv, w_proj, w_fc1, w_fc2), keep_mask, mix_pre, mix_post,
                       [v.reshape(1, -1) for v in vecs])
    out, ig, gqkv, gproj, gfc1, gfc2, pre_total, post_total, gfb1, *gs = finish_call(pn, parts)
    gfb1 = gfb1.reshape(-1)
    gs = [g.reshape(-1) for g in gs]
    return (out, ig, gs[0], gs[1], gqkv, gs[2], gs[3], pre_total, post_total, gproj, gs[4], gs[5],
            gs[6], gs[7], gfc1, gfb1, gfc2, gs[8], gs[9])


def solution(mesh):
    m, mn = P("mp"), P("mp", None)
    big = P("mp", "dp")
    in_specs = (big, P("dp", None), m, m, mn, m, m, P(), P(), mn, m, m, m, m, mn, m, mn, m, m, big)
    out_specs = (big, big, m, m, mn, m, m, P(), P(), mn, m, m, m, m, mn, m, mn, m, m)
    return jax.shard_map(local, mesh=mesh, in_specs=in_specs, out_specs=out_specs, check_vma=False)
```

```python
import functools
import jax
import jax.numpy as jnp
from jax import lax
from jax.experimental import pallas as pl
from jax.experimental.pallas import tpu as pltpu
from jax.sharding import PartitionSpec as P

PATCHES = 196
HEADS = 8
EPSILON = 1e-06
MASKED = -1000000000.0
F32 = jnp.float32
BF16 = jnp.bfloat16
VMEM_BYTES = 63 * 2 ** 20
LANES = 256
KEYS = 208


def dot(a, b):
    return lax.dot_general(a, b, (((1,), (0,)), ((), ())), preferred_element_type=F32)


def dot_nt(a, b):
    return lax.dot_general(a, b, (((1,), (1,)), ((), ())), preferred_element_type=F32)


def dot_tn(a, b):
    return lax.dot_general(a, b, (((0,), (0,)), ((), ())), preferred_element_type=F32)


def twice(col):
    return jnp.concatenate([col, col], axis=1)


def fold(v):
    r = v[:, :128]
    for i in range(128, v.shape[1], 128):
        r = r + v[:, i:i + 128]
    return r


def lane_column(row):
    return jnp.transpose(jnp.broadcast_to(row, (128, row.shape[1])))


def gelu_parts(h):
    e = jnp.exp(-0.5 * h * h)
    cum = 0.5 * (1.0 + lax.erf(h * 0.7071067811865476))
    return cum, cum + h * (e * 0.3989422804014327)


MESH = pl.DeviceIdType.MESH
TILE = 128
VECS = ("g1", "b1", "qb", "vb", "pb", "s1", "g2", "b2", "fb2", "s2")


class Plan:
    def __init__(self, n_dp, n_mp, patches, keep_mask, w_fc2):
        self.n_dp = n_dp
        self.n_mp = n_mp
        self.nx = n_mp // 2
        self.CS, self.cols = patches
        self.C = self.CS * n_mp
        self.FFS = w_fc2[0]
        self.FF = self.FFS * n_mp
        self.n_img = keep_mask[0] // n_mp
        self.tok = self.n_img * PATCHES
        starts = [self.tok * m for m in range(n_mp)]
        self.bases = [s // TILE * TILE for s in starts]
        self.shifts = [s % TILE for s in starts]
        top = max(self.shifts)
        self.width = -(-(self.tok + top) // TILE) * TILE
        self.wide = self.width + TILE
        self.pairs = self.n_img // 2
        self.in_cuts = [0] + [-(-(2 * PATCHES * (k + 1) + top) // TILE) * TILE for k in range(self.pairs)]
        self.out_cuts = [0] + [2 * PATCHES * (k + 1) // TILE * TILE for k in range(self.pairs - 1)] + [self.width]
        self.vrows = len(VECS) + self.FFS // self.CS
        self.off = {}
        at = 0
        for name in VECS + ("fb1",):
            w = self.FF if name == "fb1" else self.C
            self.off[name] = (at, w)
            at += w
        self.total = at
        self.long = (self.FFS // TILE, TILE) if self.FFS % TILE == 0 else (1, self.FFS)
        half = self.CS // 2
        self.groups = ((2, self.pieces(self.FFS // 2, n_dp // 2), True),
                       (2, self.pieces(half * (self.FF // self.C + 1), n_dp // 2), True))
        self.groups += ((1, self.pieces(self.CS, n_dp), False),) * 3
    def pieces(self, rows, cuts):
        return -(-rows // (16 * cuts)) * 16 * cuts

    def group_scratch(self, ny, half, lent):
        V = pltpu.VMEM
        nx, more, lanes, nz = self.nx, max(self.nx - 1, 1), self.C, self.n_dp // ny
        second = half if ny > 1 else 16
        return [V((16 if lent else nx * ny * half, lanes), BF16), V((nx, ny * half, lanes), BF16),
                V((nx, second, lanes), BF16), V((nx, second, lanes), BF16), V((more, half, lanes), BF16),
                V((more, half, lanes), BF16), V((half, lanes), BF16), V((nz, half // nz, lanes), BF16),
                V((half, lanes), BF16)]


class Group:
    def __init__(self, pn, ny, refs, blocks):
        self.pn, self.ny, self.blocks = pn, ny, blocks
        self.nz = pn.n_dp // ny
        self.s1, self.r1, self.s2, self.r2, self.s3, self.r3, self.s4, self.r4, self.s5, self.out = refs
        self.half = self.s4.shape[0]
        self.piece = self.half // self.nz

    def build(self, remote, local_copy, xi, core, sibling, dp):
        pn, half, ny = self.pn, self.half, self.ny
        self.xi, self.core = xi, core
        self.y, self.z = (dp % 2, dp // 2) if ny > 1 else (0, dp)
        other = dp + 1 - 2 * self.y
        used = pn.CS if ny == 1 else ny * half
        self.c1 = [remote(self.s1.at[pl.ds(ny * half * x, used), :], self.r1.at[x, pl.ds(0, used), :], {"mp": sibling})
                   for x in range(pn.nx)]
        self.c2 = []
        if ny > 1:
            self.c2 = [remote(self.s2.at[x], self.r2.at[x], {"dp": other}) for x in range(pn.nx)]
        used = pn.CS if ny == 1 else half
        self.c3 = [remote(self.s3.at[d - 1, pl.ds(0, used), :], self.r3.at[d - 1, pl.ds(0, used), :], {"mp": ((xi + d) % pn.nx) * 2 + core})
                   for d in range(1, pn.nx)]
        self.c4, self.c5 = [], []
        own = self.s5.at[self.rows(self.z)]
        for e in range(1, self.nz):
            to = (self.z + e) % self.nz
            self.c4.append(remote(self.s4.at[self.rows(to)], self.r4.at[e], {"dp": ny * to + self.y}))
            self.c5.append(remote(own, own, {"dp": ny * to + self.y}))
        there = self.out.at[pl.ds(pl.multiple_of(self.y * half, 16), half), :]
        self.c6 = [local_copy(self.s5, there)]
        if ny > 1:
            self.c6.append(remote(self.s5, there, {"dp": other}))

    def rows(self, q):
        return pl.ds(pl.multiple_of(q * self.piece, 16), self.piece)

    def fill(self, dst, j, y, add):
        lo = 0
        for v in self.blocks(j, y):
            at = slice(lo, lo + v.shape[0])
            dst[at, :] = add(at, v).astype(BF16)
            lo = at.stop

    def over_cores(self):
        half = self.half
        for x in range(self.pn.nx):
            for y in range(self.ny):
                self.fill(self.s1.at[pl.ds((self.ny * x + y) * half, half), :], 2 * x + 1 - self.core, y, lambda at, v: v)
            self.c1[x].start()

    def from_core(self, x, y, at):
        if self.ny == 1:
            return self.r1[x, at, :].astype(F32)
        upper = slice(at.start + self.half, at.stop + self.half)
        return jnp.where(y == 0, self.r1[x, at, :].astype(F32), self.r1[x, upper, :].astype(F32))

    def over_y(self):
        y = 1 - self.y
        for x in range(self.pn.nx):
            self.c1[x].wait_recv()
            self.fill(self.s2.at[x], 2 * x + self.core, y, lambda at, v: v + self.from_core(x, y, at))
            self.c2[x].start()

    def so_far(self, x, at, v):
        v = v + self.from_core(x, self.y, at)
        return v + self.r2[x, at, :].astype(F32) if self.ny > 1 else v

    def over_x(self):
        for c in self.c2 if self.ny > 1 else self.c1:
            c.wait_recv()
        for d in range(1, self.pn.nx):
            x = (self.xi + d) % self.pn.nx
            self.fill(self.s3.at[d - 1], 2 * x + self.core, self.y, lambda at, v: self.so_far(x, at, v))
            self.c3[d - 1].start()

    def over_z(self):
        for c in self.c3:
            c.wait_recv()

        def add(at, v):
            v = self.so_far(self.xi, at, v)
            for d in range(1, self.pn.nx):
                v = v + self.r3[d - 1, at, :].astype(F32)
            return v

        self.fill(self.s4, 2 * self.xi + self.core, self.y, add)
        for c in self.c4:
            c.start()

    def back_z(self):
        v = self.s4[self.rows(self.z), :].astype(F32)
        for e in range(1, self.nz):
            self.c4[e - 1].wait_recv()
            v = v + self.r4[e].astype(F32)
        self.s5[self.rows(self.z), :] = v.astype(BF16)
        for c in self.c5:
            c.start()

    def back_y(self):
        for c in self.c5:
            c.wait_recv()
        for c in self.c6:
            c.start()

    def finish(self):
        self.c6[0].wait()
        for c in self.c6[1:]:
            c.wait_recv()


def layer_kernel(pn, x_hbm, c_hbm, wqkv_hbm, wproj_hbm, wfc1_hbm, wfc2_hbm, keep_ref, pre_ref, post_ref, *rest):
    vec_refs, rest = rest[:len(VECS) + 1], rest[len(VECS) + 1:]
    layer_body(pn, x_hbm, c_hbm, wqkv_hbm, wproj_hbm, wfc1_hbm, wfc2_hbm, keep_ref, pre_ref, post_ref, vec_refs,
               *rest)


def layer_body(pn, x_hbm, c_hbm, wqkv_hbm, wproj_hbm, wfc1_hbm, wfc2_hbm, keep_ref, pre_ref, post_ref, vec_refs,
                 orecv_s, irecv_s, small_ref, r4_fc2, r4_fc1, r4_v, r4_k, r4_q,
                 xw_s, cw_s, pv_s, wqkv_s, wproj_s, wfc1_s, wfc2_s, wqkvT_s, wprojT_s, wfc1T_s, wfc2T_s,
                 x_s, first_s, qkv_s, p_s, a_s, gm_s, col_s, act_s, slope_s, gh_s, two_s, mrow_s, mask_s,
                 dqkv_ref, dproj_ref, dfc1_ref, dfc2_ref, dvec_ref, dmix_ref,
                 pack_s, hop1_s, pack2_s, hop2_s, pvec_ref, *rest):
    group_refs = [list(rest[9 * i:9 * i + 9]) + [r] for i, r in enumerate((r4_fc2, r4_fc1, r4_v, r4_k, r4_q))]
    group_refs[0][0], group_refs[1][0] = wfc1T_s, wfc2_s
    ssem, rsem, lsem = rest[45:]
    ow_s, iw_s = xw_s, cw_s
    C, CS, FF, n_img, n_mp, nx = pn.C, pn.CS, pn.FF, pn.n_img, pn.n_mp, pn.nx
    inv_c = 1.0 / C
    n_dp = pn.n_dp
    dp = lax.axis_index("dp")
    me = lax.axis_index("mp")
    core = me % 2
    xi = me // 2
    sibling = me + 1 - 2 * core
    my_shift = (pn.tok * me) % TILE

    count = [0, 0]
    sent = []

    def remote(src, dst, dev):
        i = count[0]
        count[0] += 1
        copy = pltpu.make_async_remote_copy(src_ref=src, dst_ref=dst, send_sem=ssem.at[i], recv_sem=rsem.at[i],
                                            device_id=dev, device_id_type=MESH)
        sent.append(copy)
        return copy

    def local_copy(src, dst):
        i = count[1]
        count[1] += 1
        return pltpu.make_async_copy(src, dst, lsem.at[i])

    def peer(d):
        return (me + d) % n_mp

    def aligned(v, n):
        return pl.multiple_of(v, n)

    def window(src, dst, k):
        lo, hi = pn.in_cuts[k], pn.in_cuts[k + 1]
        mine = dst.at[pl.ds(aligned(me * CS, CS), CS), pl.ds(lo, hi - lo)]

        def part(m):
            base = (pn.tok * m) // TILE * TILE
            return src.at[:, pl.ds(aligned(base + lo, TILE), hi - lo)]

        return [local_copy(part(me), mine)] + [remote(part(peer(d)), mine, {"mp": peer(d)}) for d in range(1, n_mp)]

    x_parts = [window(x_hbm, xw_s, k) for k in range(pn.pairs)]
    c_parts = [window(c_hbm, cw_s, k) for k in range(pn.pairs)]
    vec_parts = [local_copy(pvec_ref, pv_s.at[me])]
    vec_parts += [remote(pvec_ref, pv_s.at[me], {"mp": peer(d)}) for d in range(1, n_mp)]

    def weight(src, dst):
        rows = src.shape[0]

        def shard(m):
            return dst.at[pl.ds(aligned(m * rows, rows), rows), :]

        own = local_copy(src, shard(me))
        across = [remote(src, shard(me), {"mp": ((xi + d) % nx) * 2 + core}) for d in range(1, nx)]
        beside = remote(src, shard(me), {"mp": sibling})
        relay = []
        for d in range(1, nx):
            s = shard(((xi + nx - d) % nx) * 2 + core)
            relay.append(remote(s, s, {"mp": sibling}))
        return own, across, beside, relay

    def spread_weight(src, dst, block):
        rows = src.shape[0]

        def shard(m):
            return dst.at[pl.ds(aligned(m * rows, rows), rows), :]

        own = local_copy(src, shard(me))
        beside = remote(src, shard(me), {"mp": sibling})
        across = [remote(block(src, 0, quarter), block(dst, me * rows, quarter), {"mp": ((xi + d) % nx) * 2 + core})
                  for d in range(1, nx)]
        along, relay = [], []
        for d in range(1, nx):
            m = ((xi + nx - d) % nx) * 2 + core
            mine = block(dst, m * rows, quarter)
            along += [remote(mine, mine, {"dp": dp - quarter + (quarter + e) % 4}) for e in range(1, 4)]
            relay.append(remote(shard(m), shard(m), {"mp": sibling}))
        return own, across, beside, relay, along

    quarter = dp % 4

    def fc1_block(ref, row, q):
        return ref.at[pl.ds(aligned(row, 16), CS), pl.ds(aligned(q * (FF // 4), TILE), FF // 4)]

    def fc2_block(ref, row, q):
        rows = pn.FFS // 4
        return ref.at[pl.ds(aligned(row + q * rows, 16), rows), :]

    w_parts = [weight(s, d) for s, d in ((wqkv_hbm, wqkv_s), (wproj_hbm, wproj_s))]
    for s, d, block in ((wfc1_hbm, wfc1_s, fc1_block), (wfc2_hbm, wfc2_s, fc2_block)):
        w_parts.append(spread_weight(s, d, block))

    def result(src, dst, k):
        lo, hi = pn.out_cuts[k], pn.out_cuts[k + 1]
        there = dst.at[me, :, pl.ds(lo, hi - lo)]

        def part(m):
            return src.at[pl.ds(aligned(m * CS, CS), CS), pl.ds(lo, hi - lo)]

        return [local_copy(part(me), there)] + [remote(part(peer(d)), there, {"mp": peer(d)}) for d in range(1, n_mp)]

    o_parts = [result(ow_s, orecv_s, k) for k in range(pn.pairs)]
    i_parts = [result(iw_s, irecv_s, k) for k in range(pn.pairs)]

    def rows_of(j, y, rows):
        return pl.ds(aligned(j * rows + y * (rows // 2), 8), rows // 2)

    def fc2_blocks(j, y):
        return [dfc2_ref[rows_of(j, y, pn.FFS), :]]

    def fc1_blocks(j, y):
        at = rows_of(j, y, CS)
        return [dfc1_ref[at, i * C:(i + 1) * C] for i in range(FF // C)] + [dproj_ref[at, :]]

    def third(i):
        return lambda j, y: [dqkv_ref[pl.ds(aligned(j * CS, 8), CS), i * C:(i + 1) * C]]

    blocks = (fc2_blocks, fc1_blocks, third(2), third(1), third(0))
    groups = [Group(pn, g[0], r, f) for g, r, f in zip(pn.groups, group_refs, blocks)]
    for g in groups:
        g.build(remote, local_copy, xi, core, sibling, dp)
    g_fc2, g_fc1, g_v, g_k, g_q = groups
    hop1 = [remote(pack_s.at[peer(d)], hop1_s.at[me], {"mp": peer(d)}) for d in range(1, n_mp)]
    hop2 = [remote(pack2_s, hop2_s.at[dp], {"dp": (dp + e) % n_dp}) for e in range(1, n_dp)]

    def start(copies):
        for c in copies:
            c.start()

    def arrive(copies):
        copies[0].wait()
        for c in copies[1:]:
            c.wait_recv()

    def start_weight(w):
        start(w[1])
        w[0].start()
        w[2].start()

    def spread_along(w):
        if len(w) > 4:
            for a in w[1]:
                a.wait_recv()
            start(w[4])

    def relay_weight(w):
        for a in w[4] if len(w) > 4 else w[1]:
            a.wait_recv()
        start(w[3])

    def have_weight(w):
        own, _, beside, relay = w[:4]
        own.wait()
        beside.wait_recv()
        for r in relay:
            r.wait_recv()

    pvec_ref[...] = jnp.zeros_like(pvec_ref)
    for i, r in enumerate(vec_refs[:-1]):
        pvec_ref[i:i + 1, 0:CS] = r[...].astype(F32)
    long = [vec_refs[-1][i:i + 1, :].astype(F32) for i in range(vec_refs[-1].shape[0])]
    long = jnp.concatenate(long, axis=1)
    for i in range(pn.FFS // CS):
        pvec_ref[len(VECS) + i:len(VECS) + i + 1, 0:CS] = long[:, i * CS:(i + 1) * CS]

    barrier = pltpu.get_barrier_semaphore()
    for d in range(1, n_mp):
        pl.semaphore_signal(barrier, inc=1, device_id={"mp": peer(d)}, device_id_type=MESH)
    for e in range(1, n_dp):
        pl.semaphore_signal(barrier, inc=1, device_id={"dp": (dp + e) % n_dp}, device_id_type=MESH)
    pl.semaphore_wait(barrier, n_mp - 1 + n_dp - 1)

    start(vec_parts)
    start_weight(w_parts[0])
    start(x_parts[0])

    hd = C // HEADS
    factor = hd ** (-0.5)
    head_of = lax.broadcasted_iota(jnp.int32, (1, C), 1) // hd
    for h in range(HEADS):
        pre = post = jnp.zeros((1, C), F32)
        for g in range(HEADS):
            pre = jnp.where(head_of == g, pre_ref[h, g] * factor, pre)
            post = jnp.where(head_of == g, post_ref[g, h], post)
        mrow_s[h:h + 1, :] = pre
        mrow_s[HEADS + h:HEADS + h + 1, :] = post
    mask_s[...] = jnp.full_like(mask_s, MASKED)
    for i in range(n_img):
        keep = keep_ref[pl.ds(me * n_img + i, 1), :]
        mask_s[i:i + 1, 0:PATCHES] = jnp.where(keep > 0, 0.0, MASKED)
    for r in (dqkv_ref, dproj_ref, dfc1_ref, dfc2_ref, dvec_ref, dmix_ref):
        r[...] = jnp.zeros_like(r)

    arrive(vec_parts)
    for m in range(n_mp):
        t = jnp.transpose(jnp.concatenate([pv_s[m], jnp.zeros((TILE - 16, TILE), F32)], axis=0))
        for i in range(pn.vrows):
            if i < len(VECS):
                at = pn.off[VECS[i]][0] + m * CS
            else:
                at = pn.off["fb1"][0] + m * pn.FFS + (i - len(VECS)) * CS
            col_s[at:at + CS, :] = jnp.broadcast_to(t[:CS, i:i + 1], (CS, TILE)).astype(BF16)

    def turn(src, dst):
        rows, cols = src.shape
        for r in range(0, rows, 384):
            for c in range(0, cols, 384):
                dst[c:c + 384, r:r + 384] = jnp.transpose(src[r:r + 384, c:c + 384])

    relay_weight(w_parts[0])
    start(x_parts[1])
    have_weight(w_parts[0])
    turn(wqkv_s, wqkvT_s)

    def col(name, lo=0, hi=None, width=2 * LANES):
        o, w = pn.off[name]
        hi = w if hi is None else hi
        v = twice(col_s[o + lo:o + hi, :].astype(F32))
        return v if width == LANES else twice(v)

    def lanes_of(b):
        return pl.ds(pl.multiple_of(b * LANES, LANES), LANES)

    def lanes_of_pair(k):
        return pl.ds(pl.multiple_of(k * 2 * LANES, 2 * LANES), 2 * LANES)

    def both(f, k):
        return jnp.concatenate([f(2 * k), f(2 * k + 1)], axis=1)

    lane = lax.broadcasted_iota(jnp.int32, (C, TILE), 1)

    def take(src, b):
        s = b * PATCHES + my_shift
        r = s % TILE
        t = s // TILE
        left = (TILE - r) % TILE
        last = (s + PATCHES - 1) // TILE
        parts = [pltpu.roll(src[:, pl.ds(aligned(i * TILE, TILE), TILE)].astype(F32), left, 1)
                 for i in (t, t + 1, last)]
        lo = jnp.where(lane < TILE - r, parts[0], parts[1])
        hi = jnp.where(lane < TILE - r, parts[1], parts[2])
        hi = jnp.where(lane < PATCHES - TILE, hi, 0.0)
        return jnp.concatenate([lo, hi], axis=1)

    def put(dst, b, v):
        s = b * PATCHES + my_shift
        r = s % TILE
        t = s // TILE
        at = [pl.ds(aligned((t + i) * TILE, TILE), TILE) for i in range(3)]
        lo = pltpu.roll(v[:, :TILE], r, 1)
        hi = pltpu.roll(v[:, TILE:], r, 1)
        old = dst[:, at[0]].astype(F32)
        dst[:, at[0]] = jnp.where(lane < r, old, lo).astype(BF16)
        dst[:, at[1]] = jnp.where(lane < r, lo, hi).astype(BF16)
        dst[:, at[2]] = hi.astype(BF16)

    def norm(x):
        mean = jnp.sum(x, axis=0, keepdims=True) * inv_c
        d = x - mean
        inv = lax.rsqrt(jnp.sum(d * d, axis=0, keepdims=True) * inv_c + EPSILON)
        return d * inv, inv

    def norm_back(u, n, inv, g):
        s = u * g
        m1 = jnp.sum(s, axis=0, keepdims=True) * inv_c
        m2 = jnp.sum(s * n, axis=0, keepdims=True) * inv_c
        return inv * (s - m1 - n * m2)

    def add_vec(name, v, lo=0):
        o = pn.off[name][0] + lo
        dvec_ref[o:o + v.shape[0], :] += fold(v)

    def when_each(k, do):
        for j in range(pn.pairs):
            pl.when(k == j)(functools.partial(do, j))

    def steps(k, plan):
        for at, do in plan:
            pl.when(k == at * pn.pairs // 4)(do)

    def start_weights():
        for w in w_parts[1:]:
            start_weight(w)

    def along_weights():
        for w in w_parts[2:]:
            spread_along(w)

    def relay_weights():
        for w in w_parts[1:]:
            relay_weight(w)

    mixed = gh_s.at[0:HEADS * KEYS, 0:C]

    def phase_a(k, _):
        when_each(k, lambda j: arrive(x_parts[j]))
        pl.when(k == 0)(start_weights)
        pl.when(k == min(2, pn.pairs - 1))(along_weights)
        for j in range(2, pn.pairs):
            pl.when(k == j - 1)(functools.partial(start, x_parts[j]))
        for j in range(pn.pairs // 2):
            pl.when(k == j + pn.pairs // 2)(functools.partial(start, c_parts[j]))
        for b in (2 * k, 2 * k + 1):
            at = lanes_of(b)
            x = take(xw_s, b)
            x_s[:, at] = x.astype(BF16)
            n1, _inv = norm(x)
            first = (n1 * col("g1", width=LANES) + col("b1", width=LANES)).astype(BF16)
            first_s[:, at] = first
            q = (dot(wqkvT_s[0:C, :], first) + col("qb", width=LANES)).astype(BF16)
            qkv_s[0:C, at] = q
            kT = dot(wqkvT_s[C:2 * C, :], first).astype(BF16)
            qkv_s[C:2 * C, at] = kT
            vT = (dot(wqkvT_s[2 * C:3 * C, :], first) + col("vb", width=LANES)).astype(BF16)
            qkv_s[2 * C:3 * C, at] = vT
            maskc = twice(lane_column(mask_s[pl.ds(b, 1), :])[:KEYS])
            kr = jnp.transpose(kT.astype(F32))[:KEYS]
            vr = jnp.transpose(vT.astype(F32))[:KEYS]
            for h in range(HEADS):
                rows = slice(h * KEYS, (h + 1) * KEYS)
                kmix = (kr * mrow_s[h:h + 1, :]).astype(BF16)
                logit = dot(kmix, q) + maskc
                top = jnp.max(logit, axis=0, keepdims=True)
                e = jnp.exp(logit - top)
                inv = 1.0 / jnp.sum(e, axis=0, keepdims=True)
                p_s[b, rows, :] = (e * inv).astype(BF16)
                mixed[rows, :] = (vr * mrow_s[HEADS + h:HEADS + h + 1, :]).astype(BF16)
            a_s[:, at] = dot_tn(mixed[...], p_s[b]).astype(BF16)
        return 0

    lax.fori_loop(0, pn.pairs, phase_a, 0)

    relay_weights()
    for w, s, d in zip(w_parts[1:], (wproj_s, wfc1_s, wfc2_s), (wprojT_s, wfc1T_s, wfc2T_s)):
        have_weight(w)
        turn(s, d)

    def phase_b(k, _):
        when_each(k, lambda j: arrive(c_parts[j]))
        for j in range(pn.pairs // 2, pn.pairs):
            pl.when(k == j - pn.pairs // 2)(functools.partial(start, c_parts[j]))
        at = lanes_of_pair(k)
        x = x_s[:, at].astype(F32)
        att = a_s[:, at]
        branch = dot(wprojT_s[...], att) + col("pb")
        middle = x + col("s1") * branch
        n2, inv2 = norm(middle)
        second = (n2 * col("g2") + col("b2")).astype(BF16)
        step = 256
        for r in range(0, FF, step):
            hid = dot(wfc1T_s[r:r + step, :], second) + col("fb1", r, r + step)
            cum, slope = gelu_parts(hid)
            act_s[r:r + step, :] = (hid * cum).astype(BF16)
            slope_s[r:r + step, :] = slope
        mlp = dot(wfc2T_s[...], act_s[0:FF, :]) + col("fb2")
        cot = both(lambda b: take(cw_s, b), k)
        result = middle + col("s2") * mlp
        put(ow_s, 2 * k, result[:, :LANES])
        put(ow_s, 2 * k + 1, result[:, LANES:])
        when_each(k, lambda j: start(o_parts[j]))
        add_vec("s2", cot * mlp)
        g_mlp = (col("s2") * cot).astype(BF16)
        add_vec("fb2", g_mlp.astype(F32))
        for r in range(0, FF, step):
            g_act = dot(wfc2_s[r:r + step, :], g_mlp)
            gh = (g_act * slope_s[r:r + step, :]).astype(BF16)
            gh_s[r:r + step, :] = gh
            add_vec("fb1", gh.astype(F32), r)
            dfc2_ref[r:r + step, :] += dot_nt(act_s[r:r + step, :], g_mlp)
        gh = gh_s[0:FF, :]
        dfc1_ref[...] += dot_nt(second, gh)
        g_second = dot(wfc1_s[...], gh)
        add_vec("g2", g_second * n2)
        add_vec("b2", g_second)
        g_mid = cot + norm_back(g_second, n2, inv2, col("g2"))
        gm_s[:, at] = g_mid
        add_vec("s1", g_mid * branch)
        g_br = (col("s1") * g_mid).astype(BF16)
        add_vec("pb", g_br.astype(F32))
        dproj_ref[...] += dot_nt(att, g_br)
        a_s[:, at] = dot(wproj_s[...], g_br).astype(BF16)
        return 0

    lax.fori_loop(0, pn.pairs, phase_b, 0)

    gt_s = act_s.at[0:HEADS * KEYS, 0:LANES]
    one_s = slope_s.at[0:HEADS * KEYS, 0:C]
    block = 16

    def unmix(wide, rows, side, out):
        parts = []
        for j in range(0, KEYS, block):
            total = jnp.zeros((block, C), F32)
            vj = side[j:j + block]
            for h in range(HEADS):
                wj = wide[h * KEYS + j:h * KEYS + j + block, :]
                total = total + mrow_s[rows + h:rows + h + 1, :] * wj
                t = wj * vj
                dmix_ref[rows + h] += t[:8] + t[8:]
            parts.append(total)
        parts.append(jnp.zeros((LANES - KEYS, C), F32))
        return jnp.transpose(jnp.concatenate(parts, axis=0)).astype(BF16)

    def phase_d(k, _):
        at = lanes_of_pair(k)
        g_first = dot(wqkv_s[...], qkv_s[:, at])
        n1, inv1 = norm(x_s[:, at].astype(F32))
        add_vec("g1", g_first * n1)
        add_vec("b1", g_first)
        grad = gm_s[:, at] + norm_back(g_first, n1, inv1, col("g1"))
        put(iw_s, 2 * k, grad[:, :LANES])
        put(iw_s, 2 * k + 1, grad[:, LANES:])
        when_each(k, lambda j: start(i_parts[j]))
        return 0

    def behind(k):
        phase_d(k, 0)

    def phase_c(k, _):
        for b in (2 * k, 2 * k + 1):
            at = lanes_of(b)
            da = a_s[:, at]
            q = qkv_s[0:C, at]
            kr = jnp.transpose(qkv_s[C:2 * C, at].astype(F32))[:KEYS]
            vr = jnp.transpose(qkv_s[2 * C:3 * C, at].astype(F32))[:KEYS]
            for h in range(HEADS):
                rows = slice(h * KEYS, (h + 1) * KEYS)
                vmix = (vr * mrow_s[HEADS + h:HEADS + h + 1, :]).astype(BF16)
                gs = dot(vmix, da)
                p = p_s[b, rows, :].astype(F32)
                d = jnp.sum(gs * p, axis=0, keepdims=True)
                gt_s[rows, :] = (p * (gs - d)).astype(BF16)
                mixed[rows, :] = (kr * mrow_s[h:h + 1, :]).astype(BF16)
            gq = dot_tn(mixed[...], gt_s[...]).astype(BF16)
            one_s[...] = dot_nt(p_s[b], da)
            two_s[...] = dot_nt(gt_s[...], q)
            gv = unmix(one_s, HEADS, vr, None)
            gk = unmix(two_s, 0, kr, None)
            add_vec("qb", gq.astype(F32))
            add_vec("vb", gv.astype(F32))
            qkv_s[0:C, at] = gq
            qkv_s[C:2 * C, at] = gk
            qkv_s[2 * C:3 * C, at] = gv
        at = lanes_of_pair(k)
        dqkv_ref[...] += dot_nt(first_s[:, at], qkv_s[:, at])
        steps(k, ((0, g_fc2.over_x), (1, g_fc2.over_z), (2, g_fc2.back_z), (2, g_fc1.over_x), (3, g_fc2.back_y),
                  (3, g_fc1.over_z)))
        pl.when(k > 0)(lambda: behind(k - 1))
        return 0

    lent = [c for w in w_parts[1:] for c in w[3] + (w[4] if len(w) > 4 else [])]
    for c in lent:
        c.wait_send()
    g_fc2.over_cores()
    g_fc1.over_cores()
    g_fc2.over_y()
    g_fc1.over_y()
    lax.fori_loop(0, pn.pairs, phase_c, 0)
    for g in (g_v, g_k, g_q):
        g.over_cores()
    lax.fori_loop(pn.pairs - 1, pn.pairs, phase_d, 0)
    for g in (g_v, g_k, g_q):
        g.over_x()

    for m in range(n_mp):
        for i in range(pn.vrows):
            if i < len(VECS):
                o = pn.off[VECS[i]][0] + m * CS
            else:
                o = pn.off["fb1"][0] + m * pn.FFS + (i - len(VECS)) * CS
            block = jnp.concatenate([dvec_ref[o:o + CS, :], jnp.zeros((TILE - CS, TILE), F32)], axis=0)
            pack_s[m, i:i + 1, :] = jnp.sum(jnp.transpose(block), axis=0, keepdims=True)
        pack_s[m, pn.vrows:16, :] = jnp.zeros((16 - pn.vrows, TILE), F32)
    lane_of = lax.broadcasted_iota(jnp.int32, (2 * HEADS, TILE), 1)
    heads = lax.broadcasted_iota(jnp.int32, (2 * HEADS, C), 1) // hd
    dmix = jnp.sum(dmix_ref[...], axis=1)
    mix = jnp.zeros((2 * HEADS, TILE), F32)
    for g in range(HEADS):
        mix = jnp.where(lane_of == g, jnp.sum(jnp.where(heads == g, dmix, 0.0), axis=1, keepdims=True), mix)
    for m in range(n_mp):
        pack_s[m, 16:32, :] = mix
    start(hop1)
    g_fc1.back_z()
    for g in (g_v, g_k, g_q):
        g.over_z()
    hop1_s[me] = pack_s[me]
    for c in hop1:
        c.wait_recv()
    both_hops = hop1_s[0]
    for m in range(1, n_mp):
        both_hops = both_hops + hop1_s[m]
    pack2_s[...] = both_hops
    start(hop2)
    g_fc1.back_y()
    for g in (g_v, g_k, g_q):
        g.back_z()
    hop2_s[dp] = both_hops
    for c in hop2:
        c.wait_recv()
    both_hops = hop2_s[0]
    for e in range(1, n_dp):
        both_hops = both_hops + hop2_s[e]
    small_ref[...] = both_hops
    for g in (g_v, g_k, g_q):
        g.back_y()

    for k in range(pn.pairs):
        arrive(o_parts[k])
        arrive(i_parts[k])
    for g in groups:
        g.finish()
    lent = [id(c) for c in lent]
    for c in sent:
        if id(c) not in lent:
            c.wait_send()


def layer_call(pn, x, cot, ws, keep, pre, post, vecs):
    C, CS, FF, n_img, n_mp, n_dp = pn.C, pn.CS, pn.FF, pn.n_img, pn.n_mp, pn.n_dp
    S = jax.ShapeDtypeStruct
    T = n_img * LANES
    outs = (S((n_mp, CS, pn.width), BF16), S((n_mp, CS, pn.width), BF16), S((32, TILE), F32))
    outs += tuple(S((ny * half, C), BF16) for ny, half, _ in pn.groups)
    V = pltpu.VMEM
    remotes = (4 * pn.pairs + 2) * (n_mp - 1) + 4 * (2 * (pn.nx - 1) + 1)
    remotes += 2 * (3 * pn.nx - 1 + 2 * (n_dp // 2 - 1) + 1) + 3 * (2 * pn.nx - 1 + 2 * (n_dp - 1)) + n_dp - 1
    remotes += 2 * (pn.nx - 1) * 3
    locals_ = 4 * pn.pairs + 1 + 4 + 5
    tall = max(FF, HEADS * KEYS)
    scratch = [V((C, pn.wide), BF16), V((C, pn.wide), BF16), V((n_mp, 16, TILE), F32),
               V((C, 3 * C), BF16), V((C, C), BF16), V((C, FF), BF16), V((FF, C), BF16),
               V((3 * C, C), BF16), V((C, C), BF16), V((FF, C), BF16), V((C, FF), BF16),
               V((C, T), BF16), V((C, T), BF16), V((3 * C, T), BF16), V((n_img, HEADS * KEYS, LANES), BF16),
               V((C, T), BF16), V((C, T), F32), V((pn.total, TILE), BF16), V((tall, 2 * LANES), BF16),
               V((tall, 2 * LANES), F32), V((tall, 2 * LANES), BF16), V((HEADS * KEYS, C), F32),
               V((2 * HEADS, C), F32), V((max(n_img, 8), LANES), F32),
               V((C, 3 * C), F32), V((C, C), F32), V((C, FF), F32), V((FF, C), F32), V((pn.total, TILE), F32),
               V((2 * HEADS, 8, C), F32),
               V((n_mp, 32, TILE), F32), V((n_mp, 32, TILE), F32), V((32, TILE), F32), V((n_dp, 32, TILE), F32),
               V((16, TILE), F32)]
    for g in pn.groups:
        scratch += pn.group_scratch(*g)
    scratch += [pltpu.SemaphoreType.DMA((remotes,)), pltpu.SemaphoreType.DMA((remotes,)),
                pltpu.SemaphoreType.DMA((locals_,))]
    vm = pl.BlockSpec(memory_space=pltpu.VMEM)
    sm = pl.BlockSpec(memory_space=pltpu.SMEM)
    hbm = pl.BlockSpec(memory_space=pl.ANY)
    return pl.pallas_call(
        functools.partial(layer_kernel, pn),
        out_shape=outs,
        in_specs=[hbm] * 6 + [vm] + [sm] * 2 + [vm] * len(vecs),
        out_specs=[hbm, hbm, vm] + [hbm] * len(pn.groups),
        scratch_shapes=scratch,
        compiler_params=pltpu.CompilerParams(vmem_limit_bytes=VMEM_BYTES, collective_id=0, has_side_effects=True),
        name="layer",
    )(x, cot, *ws, keep, pre, post, *vecs)


def finish_kernel(pn, orecv, irecv, small, r_fc2, r_fc1, r_v, r_k, r_q, out_hbm, ig_hbm, gqkv_hbm, gproj_hbm, gfc1_hbm,
                  gfc2_hbm, pre_ref, post_ref, fb1_ref, *rest):
    C, CS, FF = pn.C, pn.CS, pn.FF
    vec_refs, rest = rest[:len(VECS)], rest[len(VECS):]
    o_s, i_s, fc2_s, fc1_s, v_s, k_s, q_s, out_s, ig_s, gqkv_s, gproj_s, gfc1_s, gfc2_s, long_s, sem = rest
    ins = [pltpu.make_async_copy(a, b, sem.at[i]) for i, (a, b) in enumerate(
        ((orecv, o_s), (irecv, i_s), (r_fc2, fc2_s), (r_fc1, fc1_s), (r_v, v_s), (r_k, k_s), (r_q, q_s)))]
    outs = [pltpu.make_async_copy(a, b, sem.at[7 + i]) for i, (a, b) in enumerate(
        ((out_s, out_hbm), (ig_s, ig_hbm), (gfc2_s, gfc2_hbm), (gfc1_s, gfc1_hbm), (gproj_s, gproj_hbm),
         (gqkv_s, gqkv_hbm)))]
    for c in ins:
        c.start()
    lane_out = lax.broadcasted_iota(jnp.int32, (CS, TILE), 1)

    def join(recv, dst):
        for j in range(pn.cols // TILE):
            parts = [(m, j - pn.bases[m] // TILE) for m in range(pn.n_mp)
                     if pn.bases[m] <= j * TILE and j * TILE < pn.bases[m] + pn.shifts[m] + pn.tok]
            v = None
            for m, l in parts:
                w = recv[m, :, l * TILE:(l + 1) * TILE]
                v = w if v is None else jnp.where(lane_out < pn.shifts[m], v.astype(F32), w.astype(F32)).astype(BF16)
            dst[:, j * TILE:(j + 1) * TILE] = v

    def unpack(src, dst, at, lanes, rows):
        for y in range(2):
            lo = y * (src.shape[0] // 2) + at * (rows // 2)
            dst[y * (rows // 2):(y + 1) * (rows // 2), lanes] = src[lo:lo + rows // 2, :].astype(F32)

    pre_ref[...] = small[16:16 + HEADS, 0:HEADS] * (C // HEADS) ** (-0.5)
    pad = jnp.zeros((TILE - HEADS, TILE), F32)
    post_ref[...] = jnp.transpose(jnp.concatenate([small[16 + HEADS:16 + 2 * HEADS, :], pad], axis=0))[0:HEADS, 0:HEADS]
    for i, r in enumerate(vec_refs):
        r[...] = small[i:i + 1, 0:CS]
    for i in range(pn.FFS // CS):
        long_s[0:1, i * CS:(i + 1) * CS] = small[len(VECS) + i:len(VECS) + i + 1, 0:CS]
    rows, lanes = fb1_ref.shape
    for i in range(rows):
        fb1_ref[i:i + 1, :] = long_s[0:1, i * lanes:(i + 1) * lanes]
    ins[0].wait()
    join(o_s, out_s)
    outs[0].start()
    ins[1].wait()
    join(i_s, ig_s)
    outs[1].start()
    ins[2].wait()
    unpack(fc2_s, gfc2_s, 0, slice(0, C), pn.FFS)
    outs[2].start()
    ins[3].wait()
    for i in range(FF // C):
        unpack(fc1_s, gfc1_s, i, slice(i * C, (i + 1) * C), CS)
    outs[3].start()
    unpack(fc1_s, gproj_s, FF // C, slice(0, C), CS)
    outs[4].start()
    for c, src, i in zip(ins[4:], (v_s, k_s, q_s), (2, 1, 0)):
        c.wait()
        gqkv_s[:, i * C:(i + 1) * C] = src[0:CS, :].astype(F32)
    outs[5].start()
    for c in outs:
        c.wait()


def finish_call(pn, parts):
    S = jax.ShapeDtypeStruct
    V = pltpu.VMEM
    C, CS = pn.C, pn.CS
    big = ((CS, pn.cols), (CS, pn.cols), (CS, 3 * C), (CS, C), (CS, pn.FF), (pn.FFS, C))
    outs = tuple(S(b, BF16 if i < 2 else F32) for i, b in enumerate(big))
    outs += (S((HEADS, HEADS), F32), S((HEADS, HEADS), F32), S(pn.long, F32))
    outs += (S((1, CS), F32),) * len(VECS)
    vm = pl.BlockSpec(memory_space=pltpu.VMEM)
    hbm = pl.BlockSpec(memory_space=pl.ANY)
    scratch = [V(p.shape, BF16) for i, p in enumerate(parts) if i != 2]
    scratch += [V(b, BF16 if i < 2 else F32) for i, b in enumerate(big)]
    return pl.pallas_call(
        functools.partial(finish_kernel, pn),
        out_shape=outs,
        in_specs=[hbm, hbm, vm] + [hbm] * (len(parts) - 3),
        out_specs=[hbm] * len(big) + [vm] * (len(outs) - len(big)),
        scratch_shapes=scratch + [V((8, pn.FFS), F32), pltpu.SemaphoreType.DMA((13,))],
        compiler_params=pltpu.CompilerParams(vmem_limit_bytes=VMEM_BYTES),
        name="finish",
    )(*parts)


def local(patches, keep_mask, ln1_gain, ln1_bias, w_qkv, q_bias, v_bias, mix_pre, mix_post, w_proj, proj_bias,
          gamma1, ln2_gain, ln2_bias, w_fc1, fc1_bias, w_fc2, fc2_bias, gamma2, cotangent):
    n_mp, n_dp = lax.axis_size("mp"), lax.axis_size("dp")
    pn = Plan(n_dp, n_mp, patches.shape, keep_mask.shape, w_fc2.shape)
    vecs = (ln1_gain, ln1_bias, q_bias, v_bias, proj_bias, gamma1, ln2_gain, ln2_bias, fc2_bias, gamma2, fc1_bias)
    parts = layer_call(pn, patches, cotangent, (w_qkv, w_proj, w_fc1, w_fc2), keep_mask, mix_pre, mix_post,
                       [v.reshape(1, -1) for v in vecs[:-1]] + [vecs[-1].reshape(pn.long)])
    out, ig, gqkv, gproj, gfc1, gfc2, pre_total, post_total, gfb1, *gs = finish_call(pn, parts)
    gfb1 = gfb1.reshape(-1)
    gs = [g.reshape(-1) for g in gs]
    return (out, ig, gs[0], gs[1], gqkv, gs[2], gs[3], pre_total, post_total, gproj, gs[4], gs[5],
            gs[6], gs[7], gfc1, gfb1, gfc2, gs[8], gs[9])


def solution(mesh):
    m, mn = P("mp"), P("mp", None)
    big = P("mp", "dp")
    in_specs = (big, P("dp", None), m, m, mn, m, m, P(), P(), mn, m, m, m, m, mn, m, mn, m, m, big)
    out_specs = (big, big, m, m, mn, m, m, P(), P(), mn, m, m, m, m, mn, m, mn, m, m)
    return jax.shard_map(local, mesh=mesh, in_specs=in_specs, out_specs=out_specs, check_vma=False)
```

```python
import functools
import jax
import jax.numpy as jnp
from jax import lax
from jax.experimental import pallas as pl
from jax.experimental.pallas import tpu as pltpu
from jax.sharding import PartitionSpec as P

PATCHES = 196
HEADS = 8
EPSILON = 1e-06
MASKED = -1000000000.0
F32 = jnp.float32
BF16 = jnp.bfloat16
VMEM_BYTES = 63 * 2 ** 20
LANES = 256
KEYS = 208


def dot(a, b):
    return lax.dot_general(a, b, (((1,), (0,)), ((), ())), preferred_element_type=F32)


def dot_nt(a, b):
    return lax.dot_general(a, b, (((1,), (1,)), ((), ())), preferred_element_type=F32)


def dot_tn(a, b):
    return lax.dot_general(a, b, (((0,), (0,)), ((), ())), preferred_element_type=F32)


def twice(col):
    return jnp.concatenate([col, col], axis=1)


def fold(v):
    r = v[:, :128]
    for i in range(128, v.shape[1], 128):
        r = r + v[:, i:i + 128]
    return r


def lane_column(row):
    return jnp.transpose(jnp.broadcast_to(row, (128, row.shape[1])))


def gelu_parts(h):
    e = jnp.exp(-0.5 * h * h)
    cum = 0.5 * (1.0 + lax.erf(h * 0.7071067811865476))
    return cum, cum + h * (e * 0.3989422804014327)


MESH = pl.DeviceIdType.MESH
TILE = 128
VECS = ("g1", "b1", "qb", "vb", "pb", "s1", "g2", "b2", "fb2", "s2")


class Plan:
    def __init__(self, n_dp, n_mp, patches, keep_mask, w_fc2):
        self.n_dp = n_dp
        self.n_mp = n_mp
        self.nx = n_mp // 2
        self.CS, self.cols = patches
        self.C = self.CS * n_mp
        self.FFS = w_fc2[0]
        self.FF = self.FFS * n_mp
        self.n_img = keep_mask[0] // n_mp
        self.tok = self.n_img * PATCHES
        starts = [self.tok * m for m in range(n_mp)]
        self.bases = [s // TILE * TILE for s in starts]
        self.shifts = [s % TILE for s in starts]
        top = max(self.shifts)
        self.width = -(-(self.tok + top) // TILE) * TILE
        self.wide = self.width + TILE
        self.pairs = self.n_img // 2
        self.in_cuts = [0] + [-(-(2 * PATCHES * (k + 1) + top) // TILE) * TILE for k in range(self.pairs)]
        self.out_cuts = [0] + [2 * PATCHES * (k + 1) // TILE * TILE for k in range(self.pairs - 1)] + [self.width]
        self.vrows = len(VECS) + self.FFS // self.CS
        self.off = {}
        at = 0
        for name in VECS + ("fb1",):
            w = self.FF if name == "fb1" else self.C
            self.off[name] = (at, w)
            at += w
        self.total = at
        self.long = (self.FFS // TILE, TILE) if self.FFS % TILE == 0 else (1, self.FFS)
        half = self.CS // 2
        self.groups = ((2, self.pieces(self.FFS // 2, n_dp // 2), True),
                       (2, self.pieces(half * (self.FF // self.C + 1), n_dp // 2), True))
        self.groups += ((1, self.pieces(self.CS, n_dp), False),) * 3
    def pieces(self, rows, cuts):
        return -(-rows // (16 * cuts)) * 16 * cuts

    def group_scratch(self, ny, half, lent):
        V = pltpu.VMEM
        nx, more, lanes, nz = self.nx, max(self.nx - 1, 1), self.C, self.n_dp // ny
        second = half if ny > 1 else 16
        return [V((16 if lent else nx * ny * half, lanes), BF16), V((nx, ny * half, lanes), BF16),
                V((nx, second, lanes), BF16), V((nx, second, lanes), BF16), V((more, half, lanes), BF16),
                V((more, half, lanes), BF16), V((half, lanes), BF16), V((nz, half // nz, lanes), BF16),
                V((half, lanes), BF16)]


class Group:
    def __init__(self, pn, ny, refs, blocks):
        self.pn, self.ny, self.blocks = pn, ny, blocks
        self.nz = pn.n_dp // ny
        self.s1, self.r1, self.s2, self.r2, self.s3, self.r3, self.s4, self.r4, self.s5, self.out = refs
        self.half = self.s4.shape[0]
        self.piece = self.half // self.nz

    def build(self, remote, local_copy, xi, core, sibling, dp):
        pn, half, ny = self.pn, self.half, self.ny
        self.xi, self.core = xi, core
        self.y, self.z = (dp % 2, dp // 2) if ny > 1 else (0, dp)
        other = dp + 1 - 2 * self.y
        used = pn.CS if ny == 1 else ny * half
        self.c1 = [remote(self.s1.at[pl.ds(ny * half * x, used), :], self.r1.at[x, pl.ds(0, used), :], {"mp": sibling})
                   for x in range(pn.nx)]
        self.c2 = []
        if ny > 1:
            self.c2 = [remote(self.s2.at[x], self.r2.at[x], {"dp": other}) for x in range(pn.nx)]
        used = pn.CS if ny == 1 else half
        self.c3 = [remote(self.s3.at[d - 1, pl.ds(0, used), :], self.r3.at[d - 1, pl.ds(0, used), :], {"mp": ((xi + d) % pn.nx) * 2 + core})
                   for d in range(1, pn.nx)]
        self.c4, self.c5 = [], []
        own = self.s5.at[self.rows(self.z)]
        for e in range(1, self.nz):
            to = (self.z + e) % self.nz
            self.c4.append(remote(self.s4.at[self.rows(to)], self.r4.at[e], {"dp": ny * to + self.y}))
            self.c5.append(remote(own, own, {"dp": ny * to + self.y}))
        there = self.out.at[pl.ds(pl.multiple_of(self.y * half, 16), half), :]
        self.c6 = [local_copy(self.s5, there)]
        if ny > 1:
            self.c6.append(remote(self.s5, there, {"dp": other}))

    def rows(self, q):
        return pl.ds(pl.multiple_of(q * self.piece, 16), self.piece)

    def fill(self, dst, j, y, add):
        lo = 0
        for v in self.blocks(j, y):
            at = slice(lo, lo + v.shape[0])
            dst[at, :] = add(at, v).astype(BF16)
            lo = at.stop

    def over_cores(self):
        half = self.half
        for x in range(self.pn.nx):
            for y in range(self.ny):
                self.fill(self.s1.at[pl.ds((self.ny * x + y) * half, half), :], 2 * x + 1 - self.core, y, lambda at, v: v)
            self.c1[x].start()

    def from_core(self, x, y, at):
        if self.ny == 1:
            return self.r1[x, at, :].astype(F32)
        upper = slice(at.start + self.half, at.stop + self.half)
        return jnp.where(y == 0, self.r1[x, at, :].astype(F32), self.r1[x, upper, :].astype(F32))

    def over_y(self):
        y = 1 - self.y
        for x in range(self.pn.nx):
            self.c1[x].wait_recv()
            self.fill(self.s2.at[x], 2 * x + self.core, y, lambda at, v: v + self.from_core(x, y, at))
            self.c2[x].start()

    def so_far(self, x, at, v):
        v = v + self.from_core(x, self.y, at)
        return v + self.r2[x, at, :].astype(F32) if self.ny > 1 else v

    def over_x(self):
        for c in self.c2 if self.ny > 1 else self.c1:
            c.wait_recv()
        for d in range(1, self.pn.nx):
            x = (self.xi + d) % self.pn.nx
            self.fill(self.s3.at[d - 1], 2 * x + self.core, self.y, lambda at, v: self.so_far(x, at, v))
            self.c3[d - 1].start()

    def over_z(self):
        for c in self.c3:
            c.wait_recv()

        def add(at, v):
            v = self.so_far(self.xi, at, v)
            for d in range(1, self.pn.nx):
                v = v + self.r3[d - 1, at, :].astype(F32)
            return v

        self.fill(self.s4, 2 * self.xi + self.core, self.y, add)
        for c in self.c4:
            c.start()

    def back_z(self):
        v = self.s4[self.rows(self.z), :].astype(F32)
        for e in range(1, self.nz):
            self.c4[e - 1].wait_recv()
            v = v + self.r4[e].astype(F32)
        self.s5[self.rows(self.z), :] = v.astype(BF16)
        for c in self.c5:
            c.start()

    def back_y(self):
        for c in self.c5:
            c.wait_recv()
        for c in self.c6:
            c.start()

    def finish(self):
        self.c6[0].wait()
        for c in self.c6[1:]:
            c.wait_recv()


def layer_kernel(pn, x_hbm, c_hbm, wqkv_hbm, wproj_hbm, wfc1_hbm, wfc2_hbm, keep_ref, pre_ref, post_ref, *rest):
    vec_refs, rest = rest[:len(VECS) + 1], rest[len(VECS) + 1:]
    layer_body(pn, x_hbm, c_hbm, wqkv_hbm, wproj_hbm, wfc1_hbm, wfc2_hbm, keep_ref, pre_ref, post_ref, vec_refs,
               *rest)


def layer_body(pn, x_hbm, c_hbm, wqkv_hbm, wproj_hbm, wfc1_hbm, wfc2_hbm, keep_ref, pre_ref, post_ref, vec_refs,
                 orecv_s, irecv_s, small_ref, r4_fc2, r4_fc1, r4_v, r4_k, r4_q,
                 xw_s, cw_s, pv_s, wqkv_s, wproj_s, wfc1_s, wfc2_s, wqkvT_s, wprojT_s, wfc1T_s, wfc2T_s,
                 x_s, first_s, qkv_s, p_s, a_s, gm_s, col_s, act_s, slope_s, gh_s, two_s, mrow_s, mask_s,
                 dqkv_ref, dproj_ref, dfc1_ref, dfc2_ref, dvec_ref, dmix_ref,
                 pack_s, hop1_s, pack2_s, hop2_s, pvec_ref, *rest):
    group_refs = [list(rest[9 * i:9 * i + 9]) + [r] for i, r in enumerate((r4_fc2, r4_fc1, r4_v, r4_k, r4_q))]
    group_refs[0][0], group_refs[1][0] = wfc1T_s, wfc2_s
    ssem, rsem, lsem = rest[45:]
    ow_s, iw_s = xw_s, cw_s
    C, CS, FF, n_img, n_mp, nx = pn.C, pn.CS, pn.FF, pn.n_img, pn.n_mp, pn.nx
    inv_c = 1.0 / C
    n_dp = pn.n_dp
    dp = lax.axis_index("dp")
    me = lax.axis_index("mp")
    core = me % 2
    xi = me // 2
    sibling = me + 1 - 2 * core
    my_shift = (pn.tok * me) % TILE

    count = [0, 0]
    sent = []

    def remote(src, dst, dev):
        i = count[0]
        count[0] += 1
        copy = pltpu.make_async_remote_copy(src_ref=src, dst_ref=dst, send_sem=ssem.at[i], recv_sem=rsem.at[i],
                                            device_id=dev, device_id_type=MESH)
        sent.append(copy)
        return copy

    def local_copy(src, dst):
        i = count[1]
        count[1] += 1
        return pltpu.make_async_copy(src, dst, lsem.at[i])

    def peer(d):
        return (me + d) % n_mp

    def aligned(v, n):
        return pl.multiple_of(v, n)

    def window(src, dst, k):
        lo, hi = pn.in_cuts[k], pn.in_cuts[k + 1]
        mine = dst.at[pl.ds(aligned(me * CS, CS), CS), pl.ds(lo, hi - lo)]

        def part(m):
            base = (pn.tok * m) // TILE * TILE
            return src.at[:, pl.ds(aligned(base + lo, TILE), hi - lo)]

        return [local_copy(part(me), mine)] + [remote(part(peer(d)), mine, {"mp": peer(d)}) for d in range(1, n_mp)]

    x_parts = [window(x_hbm, xw_s, k) for k in range(pn.pairs)]
    c_parts = [window(c_hbm, cw_s, k) for k in range(pn.pairs)]
    vec_parts = [local_copy(pvec_ref, pv_s.at[me])]
    vec_parts += [remote(pvec_ref, pv_s.at[me], {"mp": peer(d)}) for d in range(1, n_mp)]

    def weight(src, dst):
        rows = src.shape[0]

        def shard(m):
            return dst.at[pl.ds(aligned(m * rows, rows), rows), :]

        own = local_copy(src, shard(me))
        across = [remote(src, shard(me), {"mp": ((xi + d) % nx) * 2 + core}) for d in range(1, nx)]
        beside = remote(src, shard(me), {"mp": sibling})
        relay = []
        for d in range(1, nx):
            s = shard(((xi + nx - d) % nx) * 2 + core)
            relay.append(remote(s, s, {"mp": sibling}))
        return own, across, beside, relay

    def spread_weight(src, dst, block):
        rows = src.shape[0]

        def shard(m):
            return dst.at[pl.ds(aligned(m * rows, rows), rows), :]

        own = local_copy(src, shard(me))
        beside = remote(src, shard(me), {"mp": sibling})
        across = [remote(block(src, 0, quarter), block(dst, me * rows, quarter), {"mp": ((xi + d) % nx) * 2 + core})
                  for d in range(1, nx)]
        along, relay = [], []
        for d in range(1, nx):
            m = ((xi + nx - d) % nx) * 2 + core
            mine = block(dst, m * rows, quarter)
            along += [remote(mine, mine, {"dp": dp - quarter + (quarter + e) % 4}) for e in range(1, 4)]
            relay.append(remote(shard(m), shard(m), {"mp": sibling}))
        return own, across, beside, relay, along

    quarter = dp % 4

    def fc1_block(ref, row, q):
        return ref.at[pl.ds(aligned(row, 16), CS), pl.ds(aligned(q * (FF // 4), TILE), FF // 4)]

    def fc2_block(ref, row, q):
        rows = pn.FFS // 4
        return ref.at[pl.ds(aligned(row + q * rows, 16), rows), :]

    w_parts = [weight(s, d) for s, d in ((wqkv_hbm, wqkv_s), (wproj_hbm, wproj_s))]
    for s, d, block in ((wfc1_hbm, wfc1_s, fc1_block), (wfc2_hbm, wfc2_s, fc2_block)):
        w_parts.append(spread_weight(s, d, block))

    def result(src, dst, k):
        lo, hi = pn.out_cuts[k], pn.out_cuts[k + 1]
        there = dst.at[me, :, pl.ds(lo, hi - lo)]

        def part(m):
            return src.at[pl.ds(aligned(m * CS, CS), CS), pl.ds(lo, hi - lo)]

        return [local_copy(part(me), there)] + [remote(part(peer(d)), there, {"mp": peer(d)}) for d in range(1, n_mp)]

    o_parts = [result(ow_s, orecv_s, k) for k in range(pn.pairs)]
    i_parts = [result(iw_s, irecv_s, k) for k in range(pn.pairs)]

    def rows_of(j, y, rows):
        return pl.ds(aligned(j * rows + y * (rows // 2), 8), rows // 2)

    def fc2_blocks(j, y):
        return [dfc2_ref[rows_of(j, y, pn.FFS), :]]

    def fc1_blocks(j, y):
        at = rows_of(j, y, CS)
        return [dfc1_ref[at, i * C:(i + 1) * C] for i in range(FF // C)] + [dproj_ref[at, :]]

    def third(i):
        return lambda j, y: [dqkv_ref[pl.ds(aligned(j * CS, 8), CS), i * C:(i + 1) * C]]

    blocks = (fc2_blocks, fc1_blocks, third(2), third(1), third(0))
    groups = [Group(pn, g[0], r, f) for g, r, f in zip(pn.groups, group_refs, blocks)]
    for g in groups:
        g.build(remote, local_copy, xi, core, sibling, dp)
    g_fc2, g_fc1, g_v, g_k, g_q = groups
    hop1 = [remote(pack_s.at[peer(d)], hop1_s.at[me], {"mp": peer(d)}) for d in range(1, n_mp)]
    hop2 = [remote(pack2_s, hop2_s.at[dp], {"dp": (dp + e) % n_dp}) for e in range(1, n_dp)]

    def start(copies):
        for c in copies:
            c.start()

    def arrive(copies):
        copies[0].wait()
        for c in copies[1:]:
            c.wait_recv()

    def start_weight(w):
        start(w[1])
        w[0].start()
        w[2].start()

    def spread_along(w):
        if len(w) > 4:
            for a in w[1]:
                a.wait_recv()
            start(w[4])

    def relay_weight(w):
        for a in w[4] if len(w) > 4 else w[1]:
            a.wait_recv()
        start(w[3])

    def have_weight(w):
        own, _, beside, relay = w[:4]
        own.wait()
        beside.wait_recv()
        for r in relay:
            r.wait_recv()

    pvec_ref[...] = jnp.zeros_like(pvec_ref)
    for i, r in enumerate(vec_refs[:-1]):
        pvec_ref[i:i + 1, 0:CS] = r[...].astype(F32)
    long = [vec_refs[-1][i:i + 1, :].astype(F32) for i in range(vec_refs[-1].shape[0])]
    long = jnp.concatenate(long, axis=1)
    for i in range(pn.FFS // CS):
        pvec_ref[len(VECS) + i:len(VECS) + i + 1, 0:CS] = long[:, i * CS:(i + 1) * CS]

    barrier = pltpu.get_barrier_semaphore()
    for d in range(1, n_mp):
        pl.semaphore_signal(barrier, inc=1, device_id={"mp": peer(d)}, device_id_type=MESH)
    for e in range(1, n_dp):
        pl.semaphore_signal(barrier, inc=1, device_id={"dp": (dp + e) % n_dp}, device_id_type=MESH)
    pl.semaphore_wait(barrier, n_mp - 1 + n_dp - 1)

    start(vec_parts)
    start_weight(w_parts[0])
    start(x_parts[0])

    hd = C // HEADS
    factor = hd ** (-0.5)
    head_of = lax.broadcasted_iota(jnp.int32, (1, C), 1) // hd
    for h in range(HEADS):
        pre = post = jnp.zeros((1, C), F32)
        for g in range(HEADS):
            pre = jnp.where(head_of == g, pre_ref[h, g] * factor, pre)
            post = jnp.where(head_of == g, post_ref[g, h], post)
        mrow_s[h:h + 1, :] = pre
        mrow_s[HEADS + h:HEADS + h + 1, :] = post
    mask_s[...] = jnp.full_like(mask_s, MASKED)
    for i in range(n_img):
        keep = keep_ref[pl.ds(me * n_img + i, 1), :]
        mask_s[i:i + 1, 0:PATCHES] = jnp.where(keep > 0, 0.0, MASKED)
    for r in (dqkv_ref, dproj_ref, dfc1_ref, dfc2_ref, dvec_ref, dmix_ref):
        r[...] = jnp.zeros_like(r)

    arrive(vec_parts)
    for m in range(n_mp):
        t = jnp.transpose(jnp.concatenate([pv_s[m], jnp.zeros((TILE - 16, TILE), F32)], axis=0))
        for i in range(pn.vrows):
            if i < len(VECS):
                at = pn.off[VECS[i]][0] + m * CS
            else:
                at = pn.off["fb1"][0] + m * pn.FFS + (i - len(VECS)) * CS
            col_s[at:at + CS, :] = jnp.broadcast_to(t[:CS, i:i + 1], (CS, TILE)).astype(BF16)

    def turn(src, dst):
        rows, cols = src.shape
        for r in range(0, rows, 384):
            for c in range(0, cols, 384):
                dst[c:c + 384, r:r + 384] = jnp.transpose(src[r:r + 384, c:c + 384])

    relay_weight(w_parts[0])
    start(x_parts[1])
    have_weight(w_parts[0])
    turn(wqkv_s, wqkvT_s)

    def col(name, lo=0, hi=None, width=2 * LANES):
        o, w = pn.off[name]
        hi = w if hi is None else hi
        v = twice(col_s[o + lo:o + hi, :].astype(F32))
        return v if width == LANES else twice(v)

    def lanes_of(b):
        return pl.ds(pl.multiple_of(b * LANES, LANES), LANES)

    def lanes_of_pair(k):
        return pl.ds(pl.multiple_of(k * 2 * LANES, 2 * LANES), 2 * LANES)

    def both(f, k):
        return jnp.concatenate([f(2 * k), f(2 * k + 1)], axis=1)

    lane = lax.broadcasted_iota(jnp.int32, (C, TILE), 1)

    def take(src, b):
        s = b * PATCHES + my_shift
        r = s % TILE
        t = s // TILE
        left = (TILE - r) % TILE
        last = (s + PATCHES - 1) // TILE
        parts = [pltpu.roll(src[:, pl.ds(aligned(i * TILE, TILE), TILE)].astype(F32), left, 1)
                 for i in (t, t + 1, last)]
        lo = jnp.where(lane < TILE - r, parts[0], parts[1])
        hi = jnp.where(lane < TILE - r, parts[1], parts[2])
        hi = jnp.where(lane < PATCHES - TILE, hi, 0.0)
        return jnp.concatenate([lo, hi], axis=1)

    def put(dst, b, v):
        s = b * PATCHES + my_shift
        r = s % TILE
        t = s // TILE
        at = [pl.ds(aligned((t + i) * TILE, TILE), TILE) for i in range(3)]
        lo = pltpu.roll(v[:, :TILE], r, 1)
        hi = pltpu.roll(v[:, TILE:], r, 1)
        old = dst[:, at[0]].astype(F32)
        dst[:, at[0]] = jnp.where(lane < r, old, lo).astype(BF16)
        dst[:, at[1]] = jnp.where(lane < r, lo, hi).astype(BF16)
        dst[:, at[2]] = hi.astype(BF16)

    def norm(x):
        mean = jnp.sum(x, axis=0, keepdims=True) * inv_c
        d = x - mean
        inv = lax.rsqrt(jnp.sum(d * d, axis=0, keepdims=True) * inv_c + EPSILON)
        return d * inv, inv

    def norm_back(u, n, inv, g):
        s = u * g
        m1 = jnp.sum(s, axis=0, keepdims=True) * inv_c
        m2 = jnp.sum(s * n, axis=0, keepdims=True) * inv_c
        return inv * (s - m1 - n * m2)

    def add_vec(name, v, lo=0):
        o = pn.off[name][0] + lo
        dvec_ref[o:o + v.shape[0], :] += fold(v)

    def when_each(k, do):
        for j in range(pn.pairs):
            pl.when(k == j)(functools.partial(do, j))

    def steps(k, plan):
        for at, do in plan:
            pl.when(k == at * pn.pairs // 4)(do)

    def start_weights():
        for w in w_parts[1:]:
            start_weight(w)

    def along_weights():
        for w in w_parts[2:]:
            spread_along(w)

    def relay_weights():
        for w in w_parts[1:]:
            relay_weight(w)

    mixed = gh_s.at[0:HEADS * KEYS, 0:C]

    def phase_a(k, _):
        when_each(k, lambda j: arrive(x_parts[j]))
        pl.when(k == 0)(start_weights)
        pl.when(k == min(2, pn.pairs - 1))(along_weights)
        for j in range(2, pn.pairs):
            pl.when(k == j - 1)(functools.partial(start, x_parts[j]))
        for j in range(pn.pairs // 2):
            pl.when(k == j + pn.pairs // 2)(functools.partial(start, c_parts[j]))
        for b in (2 * k, 2 * k + 1):
            at = lanes_of(b)
            x = take(xw_s, b)
            x_s[:, at] = x.astype(BF16)
            n1, _inv = norm(x)
            first = (n1 * col("g1", width=LANES) + col("b1", width=LANES)).astype(BF16)
            first_s[:, at] = first
            q = (dot(wqkvT_s[0:C, :], first) + col("qb", width=LANES)).astype(BF16)
            qkv_s[0:C, at] = q
            kT = dot(wqkvT_s[C:2 * C, :], first).astype(BF16)
            qkv_s[C:2 * C, at] = kT
            vT = (dot(wqkvT_s[2 * C:3 * C, :], first) + col("vb", width=LANES)).astype(BF16)
            qkv_s[2 * C:3 * C, at] = vT
            maskc = twice(lane_column(mask_s[pl.ds(b, 1), :])[:KEYS])
            kr = jnp.transpose(kT.astype(F32))[:KEYS]
            vr = jnp.transpose(vT.astype(F32))[:KEYS]
            for h in range(HEADS):
                rows = slice(h * KEYS, (h + 1) * KEYS)
                kmix = (kr * mrow_s[h:h + 1, :]).astype(BF16)
                logit = dot(kmix, q) + maskc
                top = jnp.max(logit, axis=0, keepdims=True)
                e = jnp.exp(logit - top)
                inv = 1.0 / jnp.sum(e, axis=0, keepdims=True)
                p_s[b, rows, :] = (e * inv).astype(BF16)
                mixed[rows, :] = (vr * mrow_s[HEADS + h:HEADS + h + 1, :]).astype(BF16)
            a_s[:, at] = dot_tn(mixed[...], p_s[b]).astype(BF16)
        return 0

    lax.fori_loop(0, pn.pairs, phase_a, 0)

    relay_weights()
    for w, s, d in zip(w_parts[1:], (wproj_s, wfc1_s, wfc2_s), (wprojT_s, wfc1T_s, wfc2T_s)):
        have_weight(w)
        turn(s, d)

    def phase_b(k, _):
        when_each(k, lambda j: arrive(c_parts[j]))
        for j in range(pn.pairs // 2, pn.pairs):
            pl.when(k == j - pn.pairs // 2)(functools.partial(start, c_parts[j]))
        at = lanes_of_pair(k)
        x = x_s[:, at].astype(F32)
        att = a_s[:, at]
        branch = dot(wprojT_s[...], att) + col("pb")
        middle = x + col("s1") * branch
        n2, inv2 = norm(middle)
        second = (n2 * col("g2") + col("b2")).astype(BF16)
        step = 256
        for r in range(0, FF, step):
            hid = dot(wfc1T_s[r:r + step, :], second) + col("fb1", r, r + step)
            cum, slope = gelu_parts(hid)
            act_s[r:r + step, :] = (hid * cum).astype(BF16)
            slope_s[r:r + step, :] = slope
        mlp = dot(wfc2T_s[...], act_s[0:FF, :]) + col("fb2")
        cot = both(lambda b: take(cw_s, b), k)
        result = middle + col("s2") * mlp
        put(ow_s, 2 * k, result[:, :LANES])
        put(ow_s, 2 * k + 1, result[:, LANES:])
        when_each(k, lambda j: start(o_parts[j]))
        add_vec("s2", cot * mlp)
        g_mlp = (col("s2") * cot).astype(BF16)
        add_vec("fb2", g_mlp.astype(F32))
        for r in range(0, FF, step):
            g_act = dot(wfc2_s[r:r + step, :], g_mlp)
            gh = (g_act * slope_s[r:r + step, :]).astype(BF16)
            gh_s[r:r + step, :] = gh
            add_vec("fb1", gh.astype(F32), r)
            dfc2_ref[r:r + step, :] += dot_nt(act_s[r:r + step, :], g_mlp)
        gh = gh_s[0:FF, :]
        dfc1_ref[...] += dot_nt(second, gh)
        g_second = dot(wfc1_s[...], gh)
        add_vec("g2", g_second * n2)
        add_vec("b2", g_second)
        g_mid = cot + norm_back(g_second, n2, inv2, col("g2"))
        gm_s[:, at] = g_mid
        add_vec("s1", g_mid * branch)
        g_br = (col("s1") * g_mid).astype(BF16)
        add_vec("pb", g_br.astype(F32))
        dproj_ref[...] += dot_nt(att, g_br)
        a_s[:, at] = dot(wproj_s[...], g_br).astype(BF16)
        return 0

    lax.fori_loop(0, pn.pairs, phase_b, 0)

    gt_s = act_s.at[0:HEADS * KEYS, 0:LANES]
    one_s = slope_s.at[0:HEADS * KEYS, 0:C]
    block = 16

    def unmix(wide, rows, side, out):
        parts = []
        for j in range(0, KEYS, block):
            total = jnp.zeros((block, C), F32)
            vj = side[j:j + block]
            for h in range(HEADS):
                wj = wide[h * KEYS + j:h * KEYS + j + block, :]
                total = total + mrow_s[rows + h:rows + h + 1, :] * wj
                t = wj * vj
                dmix_ref[rows + h] += t[:8] + t[8:]
            parts.append(total)
        parts.append(jnp.zeros((LANES - KEYS, C), F32))
        return jnp.transpose(jnp.concatenate(parts, axis=0)).astype(BF16)

    def phase_d(k, _):
        at = lanes_of_pair(k)
        g_first = dot(wqkv_s[...], qkv_s[:, at])
        n1, inv1 = norm(x_s[:, at].astype(F32))
        add_vec("g1", g_first * n1)
        add_vec("b1", g_first)
        grad = gm_s[:, at] + norm_back(g_first, n1, inv1, col("g1"))
        put(iw_s, 2 * k, grad[:, :LANES])
        put(iw_s, 2 * k + 1, grad[:, LANES:])
        when_each(k, lambda j: start(i_parts[j]))
        return 0

    def behind(k):
        phase_d(k, 0)

    def phase_c(k, _):
        for b in (2 * k, 2 * k + 1):
            at = lanes_of(b)
            da = a_s[:, at]
            q = qkv_s[0:C, at]
            kr = jnp.transpose(qkv_s[C:2 * C, at].astype(F32))[:KEYS]
            vr = jnp.transpose(qkv_s[2 * C:3 * C, at].astype(F32))[:KEYS]
            for h in range(HEADS):
                rows = slice(h * KEYS, (h + 1) * KEYS)
                vmix = (vr * mrow_s[HEADS + h:HEADS + h + 1, :]).astype(BF16)
                gs = dot(vmix, da)
                p = p_s[b, rows, :].astype(F32)
                d = jnp.sum(gs * p, axis=0, keepdims=True)
                gt_s[rows, :] = (p * (gs - d)).astype(BF16)
                mixed[rows, :] = (kr * mrow_s[h:h + 1, :]).astype(BF16)
            gq = dot_tn(mixed[...], gt_s[...]).astype(BF16)
            one_s[...] = dot_nt(p_s[b], da)
            two_s[...] = dot_nt(gt_s[...], q)
            gv = unmix(one_s, HEADS, vr, None)
            gk = unmix(two_s, 0, kr, None)
            add_vec("qb", gq.astype(F32))
            add_vec("vb", gv.astype(F32))
            qkv_s[0:C, at] = gq
            qkv_s[C:2 * C, at] = gk
            qkv_s[2 * C:3 * C, at] = gv
        at = lanes_of_pair(k)
        dqkv_ref[...] += dot_nt(first_s[:, at], qkv_s[:, at])
        steps(k, ((0, g_fc2.over_x), (1, g_fc2.over_z), (2, g_fc2.back_z), (2, g_fc1.over_x), (3, g_fc2.back_y),
                  (3, g_fc1.over_z)))
        pl.when(k > 0)(lambda: behind(k - 1))
        return 0

    lent = [c for w in w_parts[1:] for c in w[3] + (w[4] if len(w) > 4 else [])]
    for c in lent:
        c.wait_send()
    g_fc2.over_cores()
    g_fc1.over_cores()
    g_fc2.over_y()
    g_fc1.over_y()
    lax.fori_loop(0, pn.pairs, phase_c, 0)
    for g in (g_v, g_k, g_q):
        g.over_cores()
    for g in (g_v, g_k, g_q):
        g.over_x()
    lax.fori_loop(pn.pairs - 1, pn.pairs, phase_d, 0)

    for m in range(n_mp):
        for i in range(pn.vrows):
            if i < len(VECS):
                o = pn.off[VECS[i]][0] + m * CS
            else:
                o = pn.off["fb1"][0] + m * pn.FFS + (i - len(VECS)) * CS
            block = jnp.concatenate([dvec_ref[o:o + CS, :], jnp.zeros((TILE - CS, TILE), F32)], axis=0)
            pack_s[m, i:i + 1, :] = jnp.sum(jnp.transpose(block), axis=0, keepdims=True)
        pack_s[m, pn.vrows:16, :] = jnp.zeros((16 - pn.vrows, TILE), F32)
    lane_of = lax.broadcasted_iota(jnp.int32, (2 * HEADS, TILE), 1)
    heads = lax.broadcasted_iota(jnp.int32, (2 * HEADS, C), 1) // hd
    dmix = jnp.sum(dmix_ref[...], axis=1)
    mix = jnp.zeros((2 * HEADS, TILE), F32)
    for g in range(HEADS):
        mix = jnp.where(lane_of == g, jnp.sum(jnp.where(heads == g, dmix, 0.0), axis=1, keepdims=True), mix)
    for m in range(n_mp):
        pack_s[m, 16:32, :] = mix
    start(hop1)
    g_fc1.back_z()
    for g in (g_v, g_k, g_q):
        g.over_z()
    hop1_s[me] = pack_s[me]
    for c in hop1:
        c.wait_recv()
    both_hops = hop1_s[0]
    for m in range(1, n_mp):
        both_hops = both_hops + hop1_s[m]
    pack2_s[...] = both_hops
    start(hop2)
    g_fc1.back_y()
    for g in (g_v, g_k, g_q):
        g.back_z()
    hop2_s[dp] = both_hops
    for c in hop2:
        c.wait_recv()
    both_hops = hop2_s[0]
    for e in range(1, n_dp):
        both_hops = both_hops + hop2_s[e]
    small_ref[...] = both_hops
    for g in (g_v, g_k, g_q):
        g.back_y()

    for k in range(pn.pairs):
        arrive(o_parts[k])
        arrive(i_parts[k])
    for g in groups:
        g.finish()
    lent = [id(c) for c in lent]
    for c in sent:
        if id(c) not in lent:
            c.wait_send()


def layer_call(pn, x, cot, ws, keep, pre, post, vecs):
    C, CS, FF, n_img, n_mp, n_dp = pn.C, pn.CS, pn.FF, pn.n_img, pn.n_mp, pn.n_dp
    S = jax.ShapeDtypeStruct
    T = n_img * LANES
    outs = (S((n_mp, CS, pn.width), BF16), S((n_mp, CS, pn.width), BF16), S((32, TILE), F32))
    outs += tuple(S((ny * half, C), BF16) for ny, half, _ in pn.groups)
    V = pltpu.VMEM
    remotes = (4 * pn.pairs + 2) * (n_mp - 1) + 4 * (2 * (pn.nx - 1) + 1)
    remotes += 2 * (3 * pn.nx - 1 + 2 * (n_dp // 2 - 1) + 1) + 3 * (2 * pn.nx - 1 + 2 * (n_dp - 1)) + n_dp - 1
    remotes += 2 * (pn.nx - 1) * 3
    locals_ = 4 * pn.pairs + 1 + 4 + 5
    tall = max(FF, HEADS * KEYS)
    scratch = [V((C, pn.wide), BF16), V((C, pn.wide), BF16), V((n_mp, 16, TILE), F32),
               V((C, 3 * C), BF16), V((C, C), BF16), V((C, FF), BF16), V((FF, C), BF16),
               V((3 * C, C), BF16), V((C, C), BF16), V((FF, C), BF16), V((C, FF), BF16),
               V((C, T), BF16), V((C, T), BF16), V((3 * C, T), BF16), V((n_img, HEADS * KEYS, LANES), BF16),
               V((C, T), BF16), V((C, T), F32), V((pn.total, TILE), BF16), V((tall, 2 * LANES), BF16),
               V((tall, 2 * LANES), F32), V((tall, 2 * LANES), BF16), V((HEADS * KEYS, C), F32),
               V((2 * HEADS, C), F32), V((max(n_img, 8), LANES), F32),
               V((C, 3 * C), F32), V((C, C), F32), V((C, FF), F32), V((FF, C), F32), V((pn.total, TILE), F32),
               V((2 * HEADS, 8, C), F32),
               V((n_mp, 32, TILE), F32), V((n_mp, 32, TILE), F32), V((32, TILE), F32), V((n_dp, 32, TILE), F32),
               V((16, TILE), F32)]
    for g in pn.groups:
        scratch += pn.group_scratch(*g)
    scratch += [pltpu.SemaphoreType.DMA((remotes,)), pltpu.SemaphoreType.DMA((remotes,)),
                pltpu.SemaphoreType.DMA((locals_,))]
    vm = pl.BlockSpec(memory_space=pltpu.VMEM)
    sm = pl.BlockSpec(memory_space=pltpu.SMEM)
    hbm = pl.BlockSpec(memory_space=pl.ANY)
    return pl.pallas_call(
        functools.partial(layer_kernel, pn),
        out_shape=outs,
        in_specs=[hbm] * 6 + [vm] + [sm] * 2 + [vm] * len(vecs),
        out_specs=[hbm, hbm, vm] + [hbm] * len(pn.groups),
        scratch_shapes=scratch,
        compiler_params=pltpu.CompilerParams(vmem_limit_bytes=VMEM_BYTES, collective_id=0, has_side_effects=True),
        name="layer",
    )(x, cot, *ws, keep, pre, post, *vecs)


def finish_kernel(pn, orecv, irecv, small, r_fc2, r_fc1, r_v, r_k, r_q, out_hbm, ig_hbm, gqkv_hbm, gproj_hbm, gfc1_hbm,
                  gfc2_hbm, pre_ref, post_ref, fb1_ref, *rest):
    C, CS, FF = pn.C, pn.CS, pn.FF
    vec_refs, rest = rest[:len(VECS)], rest[len(VECS):]
    o_s, i_s, fc2_s, fc1_s, v_s, k_s, q_s, out_s, ig_s, gqkv_s, gproj_s, gfc1_s, gfc2_s, long_s, sem = rest
    ins = [pltpu.make_async_copy(a, b, sem.at[i]) for i, (a, b) in enumerate(
        ((orecv, o_s), (irecv, i_s), (r_fc2, fc2_s), (r_fc1, fc1_s), (r_v, v_s), (r_k, k_s), (r_q, q_s)))]
    outs = [pltpu.make_async_copy(a, b, sem.at[7 + i]) for i, (a, b) in enumerate(
        ((out_s, out_hbm), (ig_s, ig_hbm), (gfc2_s, gfc2_hbm), (gfc1_s, gfc1_hbm), (gproj_s, gproj_hbm),
         (gqkv_s, gqkv_hbm)))]
    for c in ins:
        c.start()
    lane_out = lax.broadcasted_iota(jnp.int32, (CS, TILE), 1)

    def join(recv, dst):
        for j in range(pn.cols // TILE):
            parts = [(m, j - pn.bases[m] // TILE) for m in range(pn.n_mp)
                     if pn.bases[m] <= j * TILE and j * TILE < pn.bases[m] + pn.shifts[m] + pn.tok]
            v = None
            for m, l in parts:
                w = recv[m, :, l * TILE:(l + 1) * TILE]
                v = w if v is None else jnp.where(lane_out < pn.shifts[m], v.astype(F32), w.astype(F32)).astype(BF16)
            dst[:, j * TILE:(j + 1) * TILE] = v

    def unpack(src, dst, at, lanes, rows):
        for y in range(2):
            lo = y * (src.shape[0] // 2) + at * (rows // 2)
            dst[y * (rows // 2):(y + 1) * (rows // 2), lanes] = src[lo:lo + rows // 2, :].astype(F32)

    pre_ref[...] = small[16:16 + HEADS, 0:HEADS] * (C // HEADS) ** (-0.5)
    pad = jnp.zeros((TILE - HEADS, TILE), F32)
    post_ref[...] = jnp.transpose(jnp.concatenate([small[16 + HEADS:16 + 2 * HEADS, :], pad], axis=0))[0:HEADS, 0:HEADS]
    for i, r in enumerate(vec_refs):
        r[...] = small[i:i + 1, 0:CS]
    for i in range(pn.FFS // CS):
        long_s[0:1, i * CS:(i + 1) * CS] = small[len(VECS) + i:len(VECS) + i + 1, 0:CS]
    rows, lanes = fb1_ref.shape
    for i in range(rows):
        fb1_ref[i:i + 1, :] = long_s[0:1, i * lanes:(i + 1) * lanes]
    ins[0].wait()
    join(o_s, out_s)
    outs[0].start()
    ins[1].wait()
    join(i_s, ig_s)
    outs[1].start()
    ins[2].wait()
    unpack(fc2_s, gfc2_s, 0, slice(0, C), pn.FFS)
    outs[2].start()
    ins[3].wait()
    for i in range(FF // C):
        unpack(fc1_s, gfc1_s, i, slice(i * C, (i + 1) * C), CS)
    outs[3].start()
    unpack(fc1_s, gproj_s, FF // C, slice(0, C), CS)
    outs[4].start()
    for c, src, i in zip(ins[4:], (v_s, k_s, q_s), (2, 1, 0)):
        c.wait()
        gqkv_s[:, i * C:(i + 1) * C] = src[0:CS, :].astype(F32)
    outs[5].start()
    for c in outs:
        c.wait()


def finish_call(pn, parts):
    S = jax.ShapeDtypeStruct
    V = pltpu.VMEM
    C, CS = pn.C, pn.CS
    big = ((CS, pn.cols), (CS, pn.cols), (CS, 3 * C), (CS, C), (CS, pn.FF), (pn.FFS, C))
    outs = tuple(S(b, BF16 if i < 2 else F32) for i, b in enumerate(big))
    outs += (S((HEADS, HEADS), F32), S((HEADS, HEADS), F32), S(pn.long, F32))
    outs += (S((1, CS), F32),) * len(VECS)
    vm = pl.BlockSpec(memory_space=pltpu.VMEM)
    hbm = pl.BlockSpec(memory_space=pl.ANY)
    scratch = [V(p.shape, BF16) for i, p in enumerate(parts) if i != 2]
    scratch += [V(b, BF16 if i < 2 else F32) for i, b in enumerate(big)]
    return pl.pallas_call(
        functools.partial(finish_kernel, pn),
        out_shape=outs,
        in_specs=[hbm, hbm, vm] + [hbm] * (len(parts) - 3),
        out_specs=[hbm] * len(big) + [vm] * (len(outs) - len(big)),
        scratch_shapes=scratch + [V((8, pn.FFS), F32), pltpu.SemaphoreType.DMA((13,))],
        compiler_params=pltpu.CompilerParams(vmem_limit_bytes=VMEM_BYTES),
        name="finish",
    )(*parts)


def local(patches, keep_mask, ln1_gain, ln1_bias, w_qkv, q_bias, v_bias, mix_pre, mix_post, w_proj, proj_bias,
          gamma1, ln2_gain, ln2_bias, w_fc1, fc1_bias, w_fc2, fc2_bias, gamma2, cotangent):
    n_mp, n_dp = lax.axis_size("mp"), lax.axis_size("dp")
    pn = Plan(n_dp, n_mp, patches.shape, keep_mask.shape, w_fc2.shape)
    vecs = (ln1_gain, ln1_bias, q_bias, v_bias, proj_bias, gamma1, ln2_gain, ln2_bias, fc2_bias, gamma2, fc1_bias)
    parts = layer_call(pn, patches, cotangent, (w_qkv, w_proj, w_fc1, w_fc2), keep_mask, mix_pre, mix_post,
                       [v.reshape(1, -1) for v in vecs[:-1]] + [vecs[-1].reshape(pn.long)])
    out, ig, gqkv, gproj, gfc1, gfc2, pre_total, post_total, gfb1, *gs = finish_call(pn, parts)
    gfb1 = gfb1.reshape(-1)
    gs = [g.reshape(-1) for g in gs]
    return (out, ig, gs[0], gs[1], gqkv, gs[2], gs[3], pre_total, post_total, gproj, gs[4], gs[5],
            gs[6], gs[7], gfc1, gfb1, gfc2, gs[8], gs[9])


def solution(mesh):
    m, mn = P("mp"), P("mp", None)
    big = P("mp", "dp")
    in_specs = (big, P("dp", None), m, m, mn, m, m, P(), P(), mn, m, m, m, m, mn, m, mn, m, m, big)
    out_specs = (big, big, m, m, mn, m, m, P(), P(), mn, m, m, m, m, mn, m, mn, m, m)
    return jax.shard_map(local, mesh=mesh, in_specs=in_specs, out_specs=out_specs, check_vma=False)
```

```python
import functools
import jax
import jax.numpy as jnp
from jax import lax
from jax.experimental import pallas as pl
from jax.experimental.pallas import tpu as pltpu
from jax.sharding import PartitionSpec as P

PATCHES = 196
HEADS = 8
EPSILON = 1e-06
MASKED = -1000000000.0
F32 = jnp.float32
BF16 = jnp.bfloat16
VMEM_BYTES = 63 * 2 ** 20
LANES = 256
KEYS = 208


def dot(a, b):
    return lax.dot_general(a, b, (((1,), (0,)), ((), ())), preferred_element_type=F32)


def dot_nt(a, b):
    return lax.dot_general(a, b, (((1,), (1,)), ((), ())), preferred_element_type=F32)


def dot_tn(a, b):
    return lax.dot_general(a, b, (((0,), (0,)), ((), ())), preferred_element_type=F32)


def twice(col):
    return jnp.concatenate([col, col], axis=1)


def fold(v):
    r = v[:, :128]
    for i in range(128, v.shape[1], 128):
        r = r + v[:, i:i + 128]
    return r


def lane_column(row):
    return jnp.transpose(jnp.broadcast_to(row, (128, row.shape[1])))


def gelu_parts(h):
    e = jnp.exp(-0.5 * h * h)
    cum = 0.5 * (1.0 + lax.erf(h * 0.7071067811865476))
    return cum, cum + h * (e * 0.3989422804014327)


MESH = pl.DeviceIdType.MESH
TILE = 128
VECS = ("g1", "b1", "qb", "vb", "pb", "s1", "g2", "b2", "fb2", "s2")


class Plan:
    def __init__(self, n_dp, n_mp, patches, keep_mask, w_fc2):
        self.n_dp = n_dp
        self.n_mp = n_mp
        self.nx = n_mp // 2
        self.CS, self.cols = patches
        self.C = self.CS * n_mp
        self.FFS = w_fc2[0]
        self.FF = self.FFS * n_mp
        self.n_img = keep_mask[0] // n_mp
        self.tok = self.n_img * PATCHES
        starts = [self.tok * m for m in range(n_mp)]
        self.bases = [s // TILE * TILE for s in starts]
        self.shifts = [s % TILE for s in starts]
        top = max(self.shifts)
        self.width = -(-(self.tok + top) // TILE) * TILE
        self.wide = self.width + TILE
        self.pairs = self.n_img // 2
        self.in_cuts = [0] + [-(-(2 * PATCHES * (k + 1) + top) // TILE) * TILE for k in range(self.pairs)]
        self.out_cuts = [0] + [2 * PATCHES * (k + 1) // TILE * TILE for k in range(self.pairs - 1)] + [self.width]
        self.vrows = len(VECS) + self.FFS // self.CS
        self.off = {}
        at = 0
        for name in VECS + ("fb1",):
            w = self.FF if name == "fb1" else self.C
            self.off[name] = (at, w)
            at += w
        self.total = at
        self.long = (self.FFS // TILE, TILE) if self.FFS % TILE == 0 else (1, self.FFS)
        half = self.CS // 2
        self.groups = ((2, self.pieces(self.FFS // 2, n_dp // 2), True),
                       (2, self.pieces(half * (self.FF // self.C + 1), n_dp // 2), True))
        self.groups += ((1, self.pieces(self.CS, n_dp), False),) * 3
    def pieces(self, rows, cuts):
        return -(-rows // (16 * cuts)) * 16 * cuts

    def group_scratch(self, ny, half, lent):
        V = pltpu.VMEM
        nx, more, lanes, nz = self.nx, max(self.nx - 1, 1), self.C, self.n_dp // ny
        second = half if ny > 1 else 16
        return [V((16 if lent else nx * ny * half, lanes), BF16), V((nx, ny * half, lanes), BF16),
                V((nx, second, lanes), BF16), V((nx, second, lanes), BF16), V((more, half, lanes), BF16),
                V((more, half, lanes), BF16), V((half, lanes), BF16), V((nz, half // nz, lanes), BF16),
                V((half, lanes), BF16)]


class Group:
    def __init__(self, pn, ny, first, refs, blocks):
        self.pn, self.ny, self.first_owner, self.blocks = pn, ny, first, blocks
        self.nz = pn.n_dp // ny
        self.s1, self.r1, self.s2, self.r2, self.s3, self.r3, self.s4, self.r4, self.s5, self.out = refs
        self.half = self.s4.shape[0]
        self.piece = self.half // self.nz

    def build(self, remote, local_copy, xi, core, sibling, dp):
        pn, half, ny = self.pn, self.half, self.ny
        self.xi, self.core = xi, core
        self.y, self.z = (dp % 2, dp // 2) if ny > 1 else (0, dp)
        other = dp + 1 - 2 * self.y
        used = pn.CS if ny == 1 else ny * half
        self.c1 = [remote(self.s1.at[pl.ds(ny * half * x, used), :], self.r1.at[x, pl.ds(0, used), :], {"mp": sibling})
                   for x in range(pn.nx)]
        self.c2 = []
        if ny > 1:
            self.c2 = [remote(self.s2.at[x], self.r2.at[x], {"dp": other}) for x in range(pn.nx)]
        used = pn.CS if ny == 1 else half
        self.c3 = [remote(self.s3.at[d - 1, pl.ds(0, used), :], self.r3.at[d - 1, pl.ds(0, used), :], {"mp": ((xi + d) % pn.nx) * 2 + core})
                   for d in range(1, pn.nx)]
        self.real = -(-used // self.piece)
        self.p = self.piece_of(self.z)
        self.c4, self.c5 = [], []
        own = self.s5.at[self.rows(self.p)]
        for e in range(1, self.nz):
            to = (self.z + e) % self.nz
            self.c4.append(remote(self.s4.at[self.rows(self.piece_of(to))], self.r4.at[e], {"dp": ny * to + self.y}))
            self.c5.append(remote(own, own, {"dp": ny * to + self.y}))
        there = self.out.at[pl.ds(pl.multiple_of(self.y * half, 16), half), :]
        self.c6 = [local_copy(self.s5, there)]
        if ny > 1:
            self.c6.append(remote(self.s5, there, {"dp": other}))

    def piece_of(self, z):
        return (z + self.nz - self.first_owner) % self.nz

    def only(self, piece, do):
        if self.real == self.nz:
            do()
        else:
            pl.when(piece < self.real)(do)

    def scattered(self, wait):
        for e in range(1, self.nz):
            self.only(self.piece_of((self.z + e) % self.nz), lambda: wait(self.c4[e - 1]))

    def gathered(self, wait):
        def each():
            for c in self.c5:
                wait(c)

        self.only(self.p, each)

    def rows(self, q):
        return pl.ds(pl.multiple_of(q * self.piece, 16), self.piece)

    def fill(self, dst, j, y, add):
        lo = 0
        for v in self.blocks(j, y):
            at = slice(lo, lo + v.shape[0])
            dst[at, :] = add(at, v).astype(BF16)
            lo = at.stop

    def over_cores(self):
        half = self.half
        for x in range(self.pn.nx):
            for y in range(self.ny):
                self.fill(self.s1.at[pl.ds((self.ny * x + y) * half, half), :], 2 * x + 1 - self.core, y, lambda at, v: v)
            self.c1[x].start()

    def from_core(self, x, y, at):
        if self.ny == 1:
            return self.r1[x, at, :].astype(F32)
        upper = slice(at.start + self.half, at.stop + self.half)
        return jnp.where(y == 0, self.r1[x, at, :].astype(F32), self.r1[x, upper, :].astype(F32))

    def over_y(self):
        y = 1 - self.y
        for x in range(self.pn.nx):
            self.c1[x].wait_recv()
            self.fill(self.s2.at[x], 2 * x + self.core, y, lambda at, v: v + self.from_core(x, y, at))
            self.c2[x].start()

    def so_far(self, x, at, v):
        v = v + self.from_core(x, self.y, at)
        return v + self.r2[x, at, :].astype(F32) if self.ny > 1 else v

    def over_x(self):
        for c in self.c2 if self.ny > 1 else self.c1:
            c.wait_recv()
        for d in range(1, self.pn.nx):
            x = (self.xi + d) % self.pn.nx
            self.fill(self.s3.at[d - 1], 2 * x + self.core, self.y, lambda at, v: self.so_far(x, at, v))
            self.c3[d - 1].start()

    def over_z(self):
        for c in self.c3:
            c.wait_recv()

        def add(at, v):
            v = self.so_far(self.xi, at, v)
            for d in range(1, self.pn.nx):
                v = v + self.r3[d - 1, at, :].astype(F32)
            return v

        self.fill(self.s4, 2 * self.xi + self.core, self.y, add)
        self.scattered(lambda c: c.start())

    def back_z(self):
        def own():
            v = self.s4[self.rows(self.p), :].astype(F32)
            for e in range(1, self.nz):
                self.c4[e - 1].wait_recv()
                v = v + self.r4[e].astype(F32)
            self.s5[self.rows(self.p), :] = v.astype(BF16)
            for c in self.c5:
                c.start()

        self.only(self.p, own)

    def back_y(self):
        for e in range(1, self.nz):
            self.only(self.piece_of((self.z + self.nz - e) % self.nz), lambda: self.c5[e - 1].wait_recv())
        for c in self.c6:
            c.start()

    def finish(self):
        self.c6[0].wait()
        for c in self.c6[1:]:
            c.wait_recv()


def layer_kernel(pn, x_hbm, c_hbm, wqkv_hbm, wproj_hbm, wfc1_hbm, wfc2_hbm, keep_ref, pre_ref, post_ref, *rest):
    vec_refs, rest = rest[:len(VECS) + 1], rest[len(VECS) + 1:]
    layer_body(pn, x_hbm, c_hbm, wqkv_hbm, wproj_hbm, wfc1_hbm, wfc2_hbm, keep_ref, pre_ref, post_ref, vec_refs,
               *rest)


def layer_body(pn, x_hbm, c_hbm, wqkv_hbm, wproj_hbm, wfc1_hbm, wfc2_hbm, keep_ref, pre_ref, post_ref, vec_refs,
                 orecv_s, irecv_s, small_ref, r4_fc2, r4_fc1, r4_v, r4_k, r4_q,
                 xw_s, cw_s, pv_s, wqkv_s, wproj_s, wfc1_s, wfc2_s, wqkvT_s, wprojT_s, wfc1T_s, wfc2T_s,
                 x_s, first_s, qkv_s, p_s, a_s, gm_s, col_s, act_s, slope_s, gh_s, two_s, mrow_s, mask_s,
                 dqkv_ref, dproj_ref, dfc1_ref, dfc2_ref, dvec_ref, dmix_ref,
                 pack_s, hop1_s, pack2_s, hop2_s, pvec_ref, *rest):
    group_refs = [list(rest[9 * i:9 * i + 9]) + [r] for i, r in enumerate((r4_fc2, r4_fc1, r4_v, r4_k, r4_q))]
    group_refs[0][0], group_refs[1][0] = wfc1T_s, wfc2_s
    ssem, rsem, lsem = rest[45:]
    ow_s, iw_s = xw_s, cw_s
    C, CS, FF, n_img, n_mp, nx = pn.C, pn.CS, pn.FF, pn.n_img, pn.n_mp, pn.nx
    inv_c = 1.0 / C
    n_dp = pn.n_dp
    dp = lax.axis_index("dp")
    me = lax.axis_index("mp")
    core = me % 2
    xi = me // 2
    sibling = me + 1 - 2 * core
    my_shift = (pn.tok * me) % TILE

    count = [0, 0]
    sent = []

    def remote(src, dst, dev):
        i = count[0]
        count[0] += 1
        copy = pltpu.make_async_remote_copy(src_ref=src, dst_ref=dst, send_sem=ssem.at[i], recv_sem=rsem.at[i],
                                            device_id=dev, device_id_type=MESH)
        sent.append(copy)
        return copy

    def local_copy(src, dst):
        i = count[1]
        count[1] += 1
        return pltpu.make_async_copy(src, dst, lsem.at[i])

    def peer(d):
        return (me + d) % n_mp

    def aligned(v, n):
        return pl.multiple_of(v, n)

    def window(src, dst, k):
        lo, hi = pn.in_cuts[k], pn.in_cuts[k + 1]
        mine = dst.at[pl.ds(aligned(me * CS, CS), CS), pl.ds(lo, hi - lo)]

        def part(m):
            base = (pn.tok * m) // TILE * TILE
            return src.at[:, pl.ds(aligned(base + lo, TILE), hi - lo)]

        return [local_copy(part(me), mine)] + [remote(part(peer(d)), mine, {"mp": peer(d)}) for d in range(1, n_mp)]

    x_parts = [window(x_hbm, xw_s, k) for k in range(pn.pairs)]
    c_parts = [window(c_hbm, cw_s, k) for k in range(pn.pairs)]
    vec_parts = [local_copy(pvec_ref, pv_s.at[me])]
    vec_parts += [remote(pvec_ref, pv_s.at[me], {"mp": peer(d)}) for d in range(1, n_mp)]

    def weight(src, dst):
        rows = src.shape[0]

        def shard(m):
            return dst.at[pl.ds(aligned(m * rows, rows), rows), :]

        own = local_copy(src, shard(me))
        across = [remote(src, shard(me), {"mp": ((xi + d) % nx) * 2 + core}) for d in range(1, nx)]
        beside = remote(src, shard(me), {"mp": sibling})
        relay = []
        for d in range(1, nx):
            s = shard(((xi + nx - d) % nx) * 2 + core)
            relay.append(remote(s, s, {"mp": sibling}))
        return own, across, beside, relay

    def spread_weight(src, dst, block):
        rows = src.shape[0]

        def shard(m):
            return dst.at[pl.ds(aligned(m * rows, rows), rows), :]

        own = local_copy(src, shard(me))
        beside = remote(src, shard(me), {"mp": sibling})
        across = [remote(block(src, 0, quarter), block(dst, me * rows, quarter), {"mp": ((xi + d) % nx) * 2 + core})
                  for d in range(1, nx)]
        along, relay = [], []
        for d in range(1, nx):
            m = ((xi + nx - d) % nx) * 2 + core
            mine = block(dst, m * rows, quarter)
            along += [remote(mine, mine, {"dp": dp - quarter + (quarter + e) % 4}) for e in range(1, 4)]
            relay.append(remote(shard(m), shard(m), {"mp": sibling}))
        return own, across, beside, relay, along

    quarter = dp % 4

    def fc1_block(ref, row, q):
        return ref.at[pl.ds(aligned(row, 16), CS), pl.ds(aligned(q * (FF // 4), TILE), FF // 4)]

    def fc2_block(ref, row, q):
        rows = pn.FFS // 4
        return ref.at[pl.ds(aligned(row + q * rows, 16), rows), :]

    w_parts = [weight(s, d) for s, d in ((wqkv_hbm, wqkv_s), (wproj_hbm, wproj_s))]
    for s, d, block in ((wfc1_hbm, wfc1_s, fc1_block), (wfc2_hbm, wfc2_s, fc2_block)):
        w_parts.append(spread_weight(s, d, block))

    def result(src, dst, k):
        lo, hi = pn.out_cuts[k], pn.out_cuts[k + 1]
        there = dst.at[me, :, pl.ds(lo, hi - lo)]

        def part(m):
            return src.at[pl.ds(aligned(m * CS, CS), CS), pl.ds(lo, hi - lo)]

        return [local_copy(part(me), there)] + [remote(part(peer(d)), there, {"mp": peer(d)}) for d in range(1, n_mp)]

    o_parts = [result(ow_s, orecv_s, k) for k in range(pn.pairs)]
    i_parts = [result(iw_s, irecv_s, k) for k in range(pn.pairs)]

    def rows_of(j, y, rows):
        return pl.ds(aligned(j * rows + y * (rows // 2), 8), rows // 2)

    def fc2_blocks(j, y):
        return [dfc2_ref[rows_of(j, y, pn.FFS), :]]

    def fc1_blocks(j, y):
        at = rows_of(j, y, CS)
        return [dfc1_ref[at, i * C:(i + 1) * C] for i in range(FF // C)] + [dproj_ref[at, :]]

    def third(i):
        return lambda j, y: [dqkv_ref[pl.ds(aligned(j * CS, 8), CS), i * C:(i + 1) * C]]

    blocks = (fc2_blocks, fc1_blocks, third(2), third(1), third(0))
    firsts = (0, 0, 0, n_dp // 4, n_dp // 2)
    groups = [Group(pn, g[0], o, r, f) for g, o, r, f in zip(pn.groups, firsts, group_refs, blocks)]
    for g in groups:
        g.build(remote, local_copy, xi, core, sibling, dp)
    g_fc2, g_fc1, g_v, g_k, g_q = groups
    hop1 = [remote(pack_s.at[peer(d)], hop1_s.at[me], {"mp": peer(d)}) for d in range(1, n_mp)]
    hop2 = [remote(pack2_s, hop2_s.at[dp], {"dp": (dp + e) % n_dp}) for e in range(1, n_dp)]

    def start(copies):
        for c in copies:
            c.start()

    def arrive(copies):
        copies[0].wait()
        for c in copies[1:]:
            c.wait_recv()

    def start_weight(w):
        start(w[1])
        w[0].start()
        w[2].start()

    def spread_along(w):
        if len(w) > 4:
            for a in w[1]:
                a.wait_recv()
            start(w[4])

    def relay_weight(w):
        for a in w[4] if len(w) > 4 else w[1]:
            a.wait_recv()
        start(w[3])

    def have_weight(w):
        own, _, beside, relay = w[:4]
        own.wait()
        beside.wait_recv()
        for r in relay:
            r.wait_recv()

    pvec_ref[...] = jnp.zeros_like(pvec_ref)
    for i, r in enumerate(vec_refs[:-1]):
        pvec_ref[i:i + 1, 0:CS] = r[...].astype(F32)
    long = [vec_refs[-1][i:i + 1, :].astype(F32) for i in range(vec_refs[-1].shape[0])]
    long = jnp.concatenate(long, axis=1)
    for i in range(pn.FFS // CS):
        pvec_ref[len(VECS) + i:len(VECS) + i + 1, 0:CS] = long[:, i * CS:(i + 1) * CS]

    barrier = pltpu.get_barrier_semaphore()
    for d in range(1, n_mp):
        pl.semaphore_signal(barrier, inc=1, device_id={"mp": peer(d)}, device_id_type=MESH)
    for e in range(1, n_dp):
        pl.semaphore_signal(barrier, inc=1, device_id={"dp": (dp + e) % n_dp}, device_id_type=MESH)
    pl.semaphore_wait(barrier, n_mp - 1 + n_dp - 1)

    start(vec_parts)
    start_weight(w_parts[0])
    start(x_parts[0])

    hd = C // HEADS
    factor = hd ** (-0.5)
    head_of = lax.broadcasted_iota(jnp.int32, (1, C), 1) // hd
    for h in range(HEADS):
        pre = post = jnp.zeros((1, C), F32)
        for g in range(HEADS):
            pre = jnp.where(head_of == g, pre_ref[h, g] * factor, pre)
            post = jnp.where(head_of == g, post_ref[g, h], post)
        mrow_s[h:h + 1, :] = pre
        mrow_s[HEADS + h:HEADS + h + 1, :] = post
    mask_s[...] = jnp.full_like(mask_s, MASKED)
    for i in range(n_img):
        keep = keep_ref[pl.ds(me * n_img + i, 1), :]
        mask_s[i:i + 1, 0:PATCHES] = jnp.where(keep > 0, 0.0, MASKED)
    for r in (dqkv_ref, dproj_ref, dfc1_ref, dfc2_ref, dvec_ref, dmix_ref):
        r[...] = jnp.zeros_like(r)

    arrive(vec_parts)
    for m in range(n_mp):
        t = jnp.transpose(jnp.concatenate([pv_s[m], jnp.zeros((TILE - 16, TILE), F32)], axis=0))
        for i in range(pn.vrows):
            if i < len(VECS):
                at = pn.off[VECS[i]][0] + m * CS
            else:
                at = pn.off["fb1"][0] + m * pn.FFS + (i - len(VECS)) * CS
            col_s[at:at + CS, :] = jnp.broadcast_to(t[:CS, i:i + 1], (CS, TILE)).astype(BF16)

    def turn(src, dst):
        rows, cols = src.shape
        for r in range(0, rows, 384):
            for c in range(0, cols, 384):
                dst[c:c + 384, r:r + 384] = jnp.transpose(src[r:r + 384, c:c + 384])

    relay_weight(w_parts[0])
    start(x_parts[1])
    have_weight(w_parts[0])
    turn(wqkv_s, wqkvT_s)

    def col(name, lo=0, hi=None, width=2 * LANES):
        o, w = pn.off[name]
        hi = w if hi is None else hi
        v = twice(col_s[o + lo:o + hi, :].astype(F32))
        return v if width == LANES else twice(v)

    def lanes_of(b):
        return pl.ds(pl.multiple_of(b * LANES, LANES), LANES)

    def lanes_of_pair(k):
        return pl.ds(pl.multiple_of(k * 2 * LANES, 2 * LANES), 2 * LANES)

    def both(f, k):
        return jnp.concatenate([f(2 * k), f(2 * k + 1)], axis=1)

    lane = lax.broadcasted_iota(jnp.int32, (C, TILE), 1)

    def take(src, b):
        s = b * PATCHES + my_shift
        r = s % TILE
        t = s // TILE
        left = (TILE - r) % TILE
        last = (s + PATCHES - 1) // TILE
        parts = [pltpu.roll(src[:, pl.ds(aligned(i * TILE, TILE), TILE)].astype(F32), left, 1)
                 for i in (t, t + 1, last)]
        lo = jnp.where(lane < TILE - r, parts[0], parts[1])
        hi = jnp.where(lane < TILE - r, parts[1], parts[2])
        hi = jnp.where(lane < PATCHES - TILE, hi, 0.0)
        return jnp.concatenate([lo, hi], axis=1)

    def put(dst, b, v):
        s = b * PATCHES + my_shift
        r = s % TILE
        t = s // TILE
        at = [pl.ds(aligned((t + i) * TILE, TILE), TILE) for i in range(3)]
        lo = pltpu.roll(v[:, :TILE], r, 1)
        hi = pltpu.roll(v[:, TILE:], r, 1)
        old = dst[:, at[0]].astype(F32)
        dst[:, at[0]] = jnp.where(lane < r, old, lo).astype(BF16)
        dst[:, at[1]] = jnp.where(lane < r, lo, hi).astype(BF16)
        dst[:, at[2]] = hi.astype(BF16)

    def norm(x):
        mean = jnp.sum(x, axis=0, keepdims=True) * inv_c
        d = x - mean
        inv = lax.rsqrt(jnp.sum(d * d, axis=0, keepdims=True) * inv_c + EPSILON)
        return d * inv, inv

    def norm_back(u, n, inv, g):
        s = u * g
        m1 = jnp.sum(s, axis=0, keepdims=True) * inv_c
        m2 = jnp.sum(s * n, axis=0, keepdims=True) * inv_c
        return inv * (s - m1 - n * m2)

    def add_vec(name, v, lo=0):
        o = pn.off[name][0] + lo
        dvec_ref[o:o + v.shape[0], :] += fold(v)

    def when_each(k, do):
        for j in range(pn.pairs):
            pl.when(k == j)(functools.partial(do, j))

    def steps(k, plan):
        for at, do in plan:
            pl.when(k == at * pn.pairs // 4)(do)

    def start_weights():
        for w in w_parts[1:]:
            start_weight(w)

    def along_weights():
        for w in w_parts[2:]:
            spread_along(w)

    def relay_weights():
        for w in w_parts[1:]:
            relay_weight(w)

    mixed = gh_s.at[0:HEADS * KEYS, 0:C]

    def phase_a(k, _):
        when_each(k, lambda j: arrive(x_parts[j]))
        pl.when(k == 0)(start_weights)
        pl.when(k == min(2, pn.pairs - 1))(along_weights)
        for j in range(2, pn.pairs):
            pl.when(k == j - 1)(functools.partial(start, x_parts[j]))
        for j in range(pn.pairs // 2):
            pl.when(k == j + pn.pairs // 2)(functools.partial(start, c_parts[j]))
        for b in (2 * k, 2 * k + 1):
            at = lanes_of(b)
            x = take(xw_s, b)
            x_s[:, at] = x.astype(BF16)
            n1, _inv = norm(x)
            first = (n1 * col("g1", width=LANES) + col("b1", width=LANES)).astype(BF16)
            first_s[:, at] = first
            q = (dot(wqkvT_s[0:C, :], first) + col("qb", width=LANES)).astype(BF16)
            qkv_s[0:C, at] = q
            kT = dot(wqkvT_s[C:2 * C, :], first).astype(BF16)
            qkv_s[C:2 * C, at] = kT
            vT = (dot(wqkvT_s[2 * C:3 * C, :], first) + col("vb", width=LANES)).astype(BF16)
            qkv_s[2 * C:3 * C, at] = vT
            maskc = twice(lane_column(mask_s[pl.ds(b, 1), :])[:KEYS])
            kr = jnp.transpose(kT.astype(F32))[:KEYS]
            vr = jnp.transpose(vT.astype(F32))[:KEYS]
            for h in range(HEADS):
                rows = slice(h * KEYS, (h + 1) * KEYS)
                kmix = (kr * mrow_s[h:h + 1, :]).astype(BF16)
                logit = dot(kmix, q) + maskc
                top = jnp.max(logit, axis=0, keepdims=True)
                e = jnp.exp(logit - top)
                inv = 1.0 / jnp.sum(e, axis=0, keepdims=True)
                p_s[b, rows, :] = (e * inv).astype(BF16)
                mixed[rows, :] = (vr * mrow_s[HEADS + h:HEADS + h + 1, :]).astype(BF16)
            a_s[:, at] = dot_tn(mixed[...], p_s[b]).astype(BF16)
        return 0

    lax.fori_loop(0, pn.pairs, phase_a, 0)

    relay_weights()
    for w, s, d in zip(w_parts[1:], (wproj_s, wfc1_s, wfc2_s), (wprojT_s, wfc1T_s, wfc2T_s)):
        have_weight(w)
        turn(s, d)

    def phase_b(k, _):
        when_each(k, lambda j: arrive(c_parts[j]))
        for j in range(pn.pairs // 2, pn.pairs):
            pl.when(k == j - pn.pairs // 2)(functools.partial(start, c_parts[j]))
        at = lanes_of_pair(k)
        x = x_s[:, at].astype(F32)
        att = a_s[:, at]
        branch = dot(wprojT_s[...], att) + col("pb")
        middle = x + col("s1") * branch
        n2, inv2 = norm(middle)
        second = (n2 * col("g2") + col("b2")).astype(BF16)
        step = 256
        for r in range(0, FF, step):
            hid = dot(wfc1T_s[r:r + step, :], second) + col("fb1", r, r + step)
            cum, slope = gelu_parts(hid)
            act_s[r:r + step, :] = (hid * cum).astype(BF16)
            slope_s[r:r + step, :] = slope
        mlp = dot(wfc2T_s[...], act_s[0:FF, :]) + col("fb2")
        cot = both(lambda b: take(cw_s, b), k)
        result = middle + col("s2") * mlp
        put(ow_s, 2 * k, result[:, :LANES])
        put(ow_s, 2 * k + 1, result[:, LANES:])
        when_each(k, lambda j: start(o_parts[j]))
        add_vec("s2", cot * mlp)
        g_mlp = (col("s2") * cot).astype(BF16)
        add_vec("fb2", g_mlp.astype(F32))
        for r in range(0, FF, step):
            g_act = dot(wfc2_s[r:r + step, :], g_mlp)
            gh = (g_act * slope_s[r:r + step, :]).astype(BF16)
            gh_s[r:r + step, :] = gh
            add_vec("fb1", gh.astype(F32), r)
            dfc2_ref[r:r + step, :] += dot_nt(act_s[r:r + step, :], g_mlp)
        gh = gh_s[0:FF, :]
        dfc1_ref[...] += dot_nt(second, gh)
        g_second = dot(wfc1_s[...], gh)
        add_vec("g2", g_second * n2)
        add_vec("b2", g_second)
        g_mid = cot + norm_back(g_second, n2, inv2, col("g2"))
        gm_s[:, at] = g_mid
        add_vec("s1", g_mid * branch)
        g_br = (col("s1") * g_mid).astype(BF16)
        add_vec("pb", g_br.astype(F32))
        dproj_ref[...] += dot_nt(att, g_br)
        a_s[:, at] = dot(wproj_s[...], g_br).astype(BF16)
        return 0

    lax.fori_loop(0, pn.pairs, phase_b, 0)

    gt_s = act_s.at[0:HEADS * KEYS, 0:LANES]
    one_s = slope_s.at[0:HEADS * KEYS, 0:C]
    block = 16

    def unmix(wide, rows, side, out):
        parts = []
        for j in range(0, KEYS, block):
            total = jnp.zeros((block, C), F32)
            vj = side[j:j + block]
            for h in range(HEADS):
                wj = wide[h * KEYS + j:h * KEYS + j + block, :]
                total = total + mrow_s[rows + h:rows + h + 1, :] * wj
                t = wj * vj
                dmix_ref[rows + h] += t[:8] + t[8:]
            parts.append(total)
        parts.append(jnp.zeros((LANES - KEYS, C), F32))
        return jnp.transpose(jnp.concatenate(parts, axis=0)).astype(BF16)

    def phase_d(k, _):
        at = lanes_of_pair(k)
        g_first = dot(wqkv_s[...], qkv_s[:, at])
        n1, inv1 = norm(x_s[:, at].astype(F32))
        add_vec("g1", g_first * n1)
        add_vec("b1", g_first)
        grad = gm_s[:, at] + norm_back(g_first, n1, inv1, col("g1"))
        put(iw_s, 2 * k, grad[:, :LANES])
        put(iw_s, 2 * k + 1, grad[:, LANES:])
        when_each(k, lambda j: start(i_parts[j]))
        return 0

    def behind(k):
        phase_d(k, 0)

    def phase_c(k, _):
        for b in (2 * k, 2 * k + 1):
            at = lanes_of(b)
            da = a_s[:, at]
            q = qkv_s[0:C, at]
            kr = jnp.transpose(qkv_s[C:2 * C, at].astype(F32))[:KEYS]
            vr = jnp.transpose(qkv_s[2 * C:3 * C, at].astype(F32))[:KEYS]
            for h in range(HEADS):
                rows = slice(h * KEYS, (h + 1) * KEYS)
                vmix = (vr * mrow_s[HEADS + h:HEADS + h + 1, :]).astype(BF16)
                gs = dot(vmix, da)
                p = p_s[b, rows, :].astype(F32)
                d = jnp.sum(gs * p, axis=0, keepdims=True)
                gt_s[rows, :] = (p * (gs - d)).astype(BF16)
                mixed[rows, :] = (kr * mrow_s[h:h + 1, :]).astype(BF16)
            gq = dot_tn(mixed[...], gt_s[...]).astype(BF16)
            one_s[...] = dot_nt(p_s[b], da)
            two_s[...] = dot_nt(gt_s[...], q)
            gv = unmix(one_s, HEADS, vr, None)
            gk = unmix(two_s, 0, kr, None)
            add_vec("qb", gq.astype(F32))
            add_vec("vb", gv.astype(F32))
            qkv_s[0:C, at] = gq
            qkv_s[C:2 * C, at] = gk
            qkv_s[2 * C:3 * C, at] = gv
        at = lanes_of_pair(k)
        dqkv_ref[...] += dot_nt(first_s[:, at], qkv_s[:, at])
        steps(k, ((0, g_fc2.over_x), (1, g_fc2.over_z), (2, g_fc2.back_z), (2, g_fc1.over_x), (3, g_fc2.back_y),
                  (3, g_fc1.over_z)))
        pl.when(k > 0)(lambda: behind(k - 1))
        return 0

    lent = [c for w in w_parts[1:] for c in w[3] + (w[4] if len(w) > 4 else [])]
    for c in lent:
        c.wait_send()
    g_fc2.over_cores()
    g_fc1.over_cores()
    g_fc2.over_y()
    g_fc1.over_y()
    lax.fori_loop(0, pn.pairs, phase_c, 0)
    for g in (g_v, g_k, g_q):
        g.over_cores()
    for g in (g_v, g_k, g_q):
        g.over_x()
    lax.fori_loop(pn.pairs - 1, pn.pairs, phase_d, 0)

    for m in range(n_mp):
        for i in range(pn.vrows):
            if i < len(VECS):
                o = pn.off[VECS[i]][0] + m * CS
            else:
                o = pn.off["fb1"][0] + m * pn.FFS + (i - len(VECS)) * CS
            block = jnp.concatenate([dvec_ref[o:o + CS, :], jnp.zeros((TILE - CS, TILE), F32)], axis=0)
            pack_s[m, i:i + 1, :] = jnp.sum(jnp.transpose(block), axis=0, keepdims=True)
        pack_s[m, pn.vrows:16, :] = jnp.zeros((16 - pn.vrows, TILE), F32)
    lane_of = lax.broadcasted_iota(jnp.int32, (2 * HEADS, TILE), 1)
    heads = lax.broadcasted_iota(jnp.int32, (2 * HEADS, C), 1) // hd
    dmix = jnp.sum(dmix_ref[...], axis=1)
    mix = jnp.zeros((2 * HEADS, TILE), F32)
    for g in range(HEADS):
        mix = jnp.where(lane_of == g, jnp.sum(jnp.where(heads == g, dmix, 0.0), axis=1, keepdims=True), mix)
    for m in range(n_mp):
        pack_s[m, 16:32, :] = mix
    start(hop1)
    g_fc1.back_z()
    for g in (g_v, g_k, g_q):
        g.over_z()
    hop1_s[me] = pack_s[me]
    for c in hop1:
        c.wait_recv()
    both_hops = hop1_s[0]
    for m in range(1, n_mp):
        both_hops = both_hops + hop1_s[m]
    pack2_s[...] = both_hops
    start(hop2)
    g_fc1.back_y()
    for g in (g_v, g_k, g_q):
        g.back_z()
    hop2_s[dp] = both_hops
    for c in hop2:
        c.wait_recv()
    both_hops = hop2_s[0]
    for e in range(1, n_dp):
        both_hops = both_hops + hop2_s[e]
    small_ref[...] = both_hops
    for g in (g_v, g_k, g_q):
        g.back_y()

    for k in range(pn.pairs):
        arrive(o_parts[k])
        arrive(i_parts[k])
    for g in groups:
        g.finish()
    lent = [id(c) for c in lent]
    lent += [id(c) for g in groups for c in g.c4 + g.c5]
    for g in groups:
        g.scattered(lambda c: c.wait_send())
        g.gathered(lambda c: c.wait_send())
    for c in sent:
        if id(c) not in lent:
            c.wait_send()


def layer_call(pn, x, cot, ws, keep, pre, post, vecs):
    C, CS, FF, n_img, n_mp, n_dp = pn.C, pn.CS, pn.FF, pn.n_img, pn.n_mp, pn.n_dp
    S = jax.ShapeDtypeStruct
    T = n_img * LANES
    outs = (S((n_mp, CS, pn.width), BF16), S((n_mp, CS, pn.width), BF16), S((32, TILE), F32))
    outs += tuple(S((ny * half, C), BF16) for ny, half, _ in pn.groups)
    V = pltpu.VMEM
    remotes = (4 * pn.pairs + 2) * (n_mp - 1) + 4 * (2 * (pn.nx - 1) + 1)
    remotes += 2 * (3 * pn.nx - 1 + 2 * (n_dp // 2 - 1) + 1) + 3 * (2 * pn.nx - 1 + 2 * (n_dp - 1)) + n_dp - 1
    remotes += 2 * (pn.nx - 1) * 3
    locals_ = 4 * pn.pairs + 1 + 4 + 5
    tall = max(FF, HEADS * KEYS)
    scratch = [V((C, pn.wide), BF16), V((C, pn.wide), BF16), V((n_mp, 16, TILE), F32),
               V((C, 3 * C), BF16), V((C, C), BF16), V((C, FF), BF16), V((FF, C), BF16),
               V((3 * C, C), BF16), V((C, C), BF16), V((FF, C), BF16), V((C, FF), BF16),
               V((C, T), BF16), V((C, T), BF16), V((3 * C, T), BF16), V((n_img, HEADS * KEYS, LANES), BF16),
               V((C, T), BF16), V((C, T), F32), V((pn.total, TILE), BF16), V((tall, 2 * LANES), BF16),
               V((tall, 2 * LANES), F32), V((tall, 2 * LANES), BF16), V((HEADS * KEYS, C), F32),
               V((2 * HEADS, C), F32), V((max(n_img, 8), LANES), F32),
               V((C, 3 * C), F32), V((C, C), F32), V((C, FF), F32), V((FF, C), F32), V((pn.total, TILE), F32),
               V((2 * HEADS, 8, C), F32),
               V((n_mp, 32, TILE), F32), V((n_mp, 32, TILE), F32), V((32, TILE), F32), V((n_dp, 32, TILE), F32),
               V((16, TILE), F32)]
    for g in pn.groups:
        scratch += pn.group_scratch(*g)
    scratch += [pltpu.SemaphoreType.DMA((remotes,)), pltpu.SemaphoreType.DMA((remotes,)),
                pltpu.SemaphoreType.DMA((locals_,))]
    vm = pl.BlockSpec(memory_space=pltpu.VMEM)
    sm = pl.BlockSpec(memory_space=pltpu.SMEM)
    hbm = pl.BlockSpec(memory_space=pl.ANY)
    return pl.pallas_call(
        functools.partial(layer_kernel, pn),
        out_shape=outs,
        in_specs=[hbm] * 6 + [vm] + [sm] * 2 + [vm] * len(vecs),
        out_specs=[hbm, hbm, vm] + [hbm] * len(pn.groups),
        scratch_shapes=scratch,
        compiler_params=pltpu.CompilerParams(vmem_limit_bytes=VMEM_BYTES, collective_id=0, has_side_effects=True),
        name="layer",
    )(x, cot, *ws, keep, pre, post, *vecs)


def finish_kernel(pn, orecv, irecv, small, r_fc2, r_fc1, r_v, r_k, r_q, out_hbm, ig_hbm, gqkv_hbm, gproj_hbm, gfc1_hbm,
                  gfc2_hbm, pre_ref, post_ref, fb1_ref, *rest):
    C, CS, FF = pn.C, pn.CS, pn.FF
    vec_refs, rest = rest[:len(VECS)], rest[len(VECS):]
    o_s, i_s, fc2_s, fc1_s, v_s, k_s, q_s, out_s, ig_s, gqkv_s, gproj_s, gfc1_s, gfc2_s, long_s, sem = rest
    ins = [pltpu.make_async_copy(a, b, sem.at[i]) for i, (a, b) in enumerate(
        ((orecv, o_s), (irecv, i_s), (r_fc2, fc2_s), (r_fc1, fc1_s), (r_v, v_s), (r_k, k_s), (r_q, q_s)))]
    outs = [pltpu.make_async_copy(a, b, sem.at[7 + i]) for i, (a, b) in enumerate(
        ((out_s, out_hbm), (ig_s, ig_hbm), (gfc2_s, gfc2_hbm), (gfc1_s, gfc1_hbm), (gproj_s, gproj_hbm),
         (gqkv_s, gqkv_hbm)))]
    for c in ins:
        c.start()
    lane_out = lax.broadcasted_iota(jnp.int32, (CS, TILE), 1)

    def join(recv, dst):
        for j in range(pn.cols // TILE):
            parts = [(m, j - pn.bases[m] // TILE) for m in range(pn.n_mp)
                     if pn.bases[m] <= j * TILE and j * TILE < pn.bases[m] + pn.shifts[m] + pn.tok]
            v = None
            for m, l in parts:
                w = recv[m, :, l * TILE:(l + 1) * TILE]
                v = w if v is None else jnp.where(lane_out < pn.shifts[m], v.astype(F32), w.astype(F32)).astype(BF16)
            dst[:, j * TILE:(j + 1) * TILE] = v

    def unpack(src, dst, at, lanes, rows):
        for y in range(2):
            lo = y * (src.shape[0] // 2) + at * (rows // 2)
            dst[y * (rows // 2):(y + 1) * (rows // 2), lanes] = src[lo:lo + rows // 2, :].astype(F32)

    pre_ref[...] = small[16:16 + HEADS, 0:HEADS] * (C // HEADS) ** (-0.5)
    pad = jnp.zeros((TILE - HEADS, TILE), F32)
    post_ref[...] = jnp.transpose(jnp.concatenate([small[16 + HEADS:16 + 2 * HEADS, :], pad], axis=0))[0:HEADS, 0:HEADS]
    for i, r in enumerate(vec_refs):
        r[...] = small[i:i + 1, 0:CS]
    for i in range(pn.FFS // CS):
        long_s[0:1, i * CS:(i + 1) * CS] = small[len(VECS) + i:len(VECS) + i + 1, 0:CS]
    rows, lanes = fb1_ref.shape
    for i in range(rows):
        fb1_ref[i:i + 1, :] = long_s[0:1, i * lanes:(i + 1) * lanes]
    ins[0].wait()
    join(o_s, out_s)
    outs[0].start()
    ins[1].wait()
    join(i_s, ig_s)
    outs[1].start()
    ins[2].wait()
    unpack(fc2_s, gfc2_s, 0, slice(0, C), pn.FFS)
    outs[2].start()
    ins[3].wait()
    for i in range(FF // C):
        unpack(fc1_s, gfc1_s, i, slice(i * C, (i + 1) * C), CS)
    outs[3].start()
    unpack(fc1_s, gproj_s, FF // C, slice(0, C), CS)
    outs[4].start()
    for c, src, i in zip(ins[4:], (v_s, k_s, q_s), (2, 1, 0)):
        c.wait()
        gqkv_s[:, i * C:(i + 1) * C] = src[0:CS, :].astype(F32)
    outs[5].start()
    for c in outs:
        c.wait()


def finish_call(pn, parts):
    S = jax.ShapeDtypeStruct
    V = pltpu.VMEM
    C, CS = pn.C, pn.CS
    big = ((CS, pn.cols), (CS, pn.cols), (CS, 3 * C), (CS, C), (CS, pn.FF), (pn.FFS, C))
    outs = tuple(S(b, BF16 if i < 2 else F32) for i, b in enumerate(big))
    outs += (S((HEADS, HEADS), F32), S((HEADS, HEADS), F32), S(pn.long, F32))
    outs += (S((1, CS), F32),) * len(VECS)
    vm = pl.BlockSpec(memory_space=pltpu.VMEM)
    hbm = pl.BlockSpec(memory_space=pl.ANY)
    scratch = [V(p.shape, BF16) for i, p in enumerate(parts) if i != 2]
    scratch += [V(b, BF16 if i < 2 else F32) for i, b in enumerate(big)]
    return pl.pallas_call(
        functools.partial(finish_kernel, pn),
        out_shape=outs,
        in_specs=[hbm, hbm, vm] + [hbm] * (len(parts) - 3),
        out_specs=[hbm] * len(big) + [vm] * (len(outs) - len(big)),
        scratch_shapes=scratch + [V((8, pn.FFS), F32), pltpu.SemaphoreType.DMA((13,))],
        compiler_params=pltpu.CompilerParams(vmem_limit_bytes=VMEM_BYTES),
        name="finish",
    )(*parts)


def local(patches, keep_mask, ln1_gain, ln1_bias, w_qkv, q_bias, v_bias, mix_pre, mix_post, w_proj, proj_bias,
          gamma1, ln2_gain, ln2_bias, w_fc1, fc1_bias, w_fc2, fc2_bias, gamma2, cotangent):
    n_mp, n_dp = lax.axis_size("mp"), lax.axis_size("dp")
    pn = Plan(n_dp, n_mp, patches.shape, keep_mask.shape, w_fc2.shape)
    vecs = (ln1_gain, ln1_bias, q_bias, v_bias, proj_bias, gamma1, ln2_gain, ln2_bias, fc2_bias, gamma2, fc1_bias)
    parts = layer_call(pn, patches, cotangent, (w_qkv, w_proj, w_fc1, w_fc2), keep_mask, mix_pre, mix_post,
                       [v.reshape(1, -1) for v in vecs[:-1]] + [vecs[-1].reshape(pn.long)])
    out, ig, gqkv, gproj, gfc1, gfc2, pre_total, post_total, gfb1, *gs = finish_call(pn, parts)
    gfb1 = gfb1.reshape(-1)
    gs = [g.reshape(-1) for g in gs]
    return (out, ig, gs[0], gs[1], gqkv, gs[2], gs[3], pre_total, post_total, gproj, gs[4], gs[5],
            gs[6], gs[7], gfc1, gfb1, gfc2, gs[8], gs[9])


def solution(mesh):
    m, mn = P("mp"), P("mp", None)
    big = P("mp", "dp")
    in_specs = (big, P("dp", None), m, m, mn, m, m, P(), P(), mn, m, m, m, m, mn, m, mn, m, m, big)
    out_specs = (big, big, m, m, mn, m, m, P(), P(), mn, m, m, m, m, mn, m, mn, m, m)
    return jax.shard_map(local, mesh=mesh, in_specs=in_specs, out_specs=out_specs, check_vma=False)
```
